32 devices in a mesh: dp: 8 (over y, x, core), ctx: 4 (over z).
Axes of the slice: x: 2, y: 2, z: 4, core: 2. Of those that a mesh axis runs over, the one named last changes fastest.
Arguments:
- inputs: bfloat16 [8, 2048, 1280], P('dp', 'ctx'), may hold values from -6 to 6
- teacher: bfloat16 [8, 2048, 1280], P('dp', 'ctx'), may hold values from -6 to 6
- lengths: int32 [8], P('dp'), may hold values from 512 to 2048, as said below
- query_weight: bfloat16 [1280, 1280], P(('dp', 'ctx')), may hold values from -0.15625 to 0.15625
- key_weight: bfloat16 [1280, 1280], P(('dp', 'ctx')), may hold values from -0.15625 to 0.15625
- value_projection: bfloat16 [1280, 1280], P(('dp', 'ctx')), may hold values from -0.15625 to 0.15625
- output_weight: bfloat16 [1280, 1280], P(('dp', 'ctx')), may hold values from -0.15625 to 0.15625
- score_gain: bfloat16 [1280], P(('dp', 'ctx')), may hold values from 1 to 1.59375
- attention_step: bfloat16 [1280], P(('dp', 'ctx')), may hold values from 0.19921875 to 0.59765625
- up_weight: bfloat16 [1280, 5120], P(('dp', 'ctx')), may hold values from -0.15625 to 0.15625
- gate_weight: bfloat16 [1280, 5120], P(('dp', 'ctx')), may hold values from -0.15625 to 0.15625
- down_weight: bfloat16 [5120, 1280], P(('dp', 'ctx')), may hold values from -0.078125 to 0.078125
- up_scale: bfloat16 [5120], P(('dp', 'ctx')), may hold values from 0.5 to 2
- gate_scale: bfloat16 [5120], P(('dp', 'ctx')), may hold values from 0.5 to 2
- swiglu_step: bfloat16 [1280], P(('dp', 'ctx')), may hold values from 0.19921875 to 0.59765625
Outputs:
- layer_out: bfloat16 [8, 2048, 1280], P('dp', 'ctx')
- distill_loss_mean: float32 [], replicated
- input_grad: float32 [8, 2048, 1280], P('dp', 'ctx')
- query_grad: float32 [1280, 1280], P(('dp', 'ctx'))
- key_grad: float32 [1280, 1280], P(('dp', 'ctx'))
- value_grad: float32 [1280, 1280], P(('dp', 'ctx'))
- output_grad: float32 [1280, 1280], P(('dp', 'ctx'))
- score_gain_grad: float32 [1280], P(('dp', 'ctx'))
- attention_step_grad: float32 [1280], P(('dp', 'ctx'))
- up_grad: float32 [1280, 5120], P(('dp', 'ctx'))
- gate_grad: float32 [1280, 5120], P(('dp', 'ctx'))
- down_grad: float32 [5120, 1280], P(('dp', 'ctx'))
- up_scale_grad: float32 [5120], P(('dp', 'ctx'))
- gate_scale_gradient: float32 [5120], P(('dp', 'ctx'))
- swiglu_step_grad: float32 [1280], P(('dp', 'ctx'))
The draws below stay inside these ranges and needn't reach their ends.
Inputs may be any that keep to these rules, and one draw needn't show every extreme that they name: `lengths`: each slot's valid tokens are its first positions; at least one slot is full in every draw.
All inputs are finite; a program needn't handle non-finite values.
Results may differ from the reference program's by a relative error of at most 0.019.
Values may be sent and summed in bfloat16 or wider, within the bound.
No kernel may reach another device: no remote copies, remote signals or barrier semaphores. Data moves between devices by JAX's collectives and lax.ppermute only.
A program may use at most 320 MiB of HBM per device.

```python
import math
import jax
import jax.numpy as jnp
from jax import lax

D = 1280
HD = 64
FF = 5120
SLOT = 2048
SLOTS = 8


def draw_lengths(key, part):
    drop_key = jax.random.fold_in(key, 17)
    index = jnp.arange(SLOTS, dtype=jnp.int32)
    quarter = SLOT // 4
    ceiling = quarter + (SLOT - quarter) * index // max(SLOTS - 1, 1)
    drop = jax.random.randint(drop_key, (SLOTS,), 0, SLOT // 8 + 1)
    drawn = jnp.maximum(ceiling - drop, quarter)
    return jnp.where(index == SLOTS - 1, SLOT, drawn).astype(jnp.int32)


def block_scale(own_key, extent, cuts, least, top_value):
    gain = 1.0
    for position, parts in cuts:
        heights = jax.random.uniform(jax.random.fold_in(jax.random.fold_in(own_key, 6), position), (parts,), jnp.float32, least / len(cuts), top_value / len(cuts))
        gain = gain * jnp.repeat(jnp.exp(heights), extent[position] // parts).reshape((-1,) + (1,) * (len(extent) - 1 - position))
    return gain


def bell_draw(key, shape, spread, reach, shards=(), kind=jnp.bfloat16):
    values = spread * jax.random.normal(key, shape, jnp.float32)
    if shards:
        values = values * block_scale(key, shape, shards, -0.22, 0.18)
    return jnp.clip(values, -reach, reach).astype(kind)


def setup_inputs(seed: int = 0) -> dict:
    key_of = jax.random.split(jax.random.key(seed), 16)
    return {
        "inputs": bell_draw(key_of[0], (SLOTS, SLOT, D), 1.0, 6.0, ((0, 8), (1, 4))),
        "teacher": bell_draw(key_of[1], (SLOTS, SLOT, D), 1.0, 6.0, ((0, 8), (1, 4))),
        "lengths": draw_lengths(jax.random.fold_in(key_of[15], 71), 0),
        "query_weight": bell_draw(key_of[3], (D, D), D ** -0.5, 0.15625, ((0, 32),)),
        "key_weight": bell_draw(key_of[4], (D, D), D ** -0.5, 0.15625, ((0, 32),)),
        "value_projection": bell_draw(key_of[5], (D, D), D ** -0.5, 0.15625, ((0, 32),)),
        "output_weight": bell_draw(key_of[6], (D, D), D ** -0.5, 0.15625, ((0, 32),)),
        "score_gain": jnp.clip(jnp.exp(math.log(1.59375) - 0.46608973 * jax.random.uniform(key_of[7], (D,), jnp.float32) ** block_scale(key_of[7], (D,), ((0, 32),), -0.2, 0.2)), 1.0, 1.59375).astype(jnp.bfloat16),
        "attention_step": jnp.clip(0.19921875 + 0.3984375 * jax.random.uniform(key_of[8], (D,), jnp.float32) ** block_scale(key_of[8], (D,), ((0, 32),), -0.2, 0.2), 0.19921875, 0.59765625).astype(jnp.bfloat16),
        "up_weight": bell_draw(key_of[9], (D, FF), D ** -0.5, 0.15625, ((0, 32),)),
        "gate_weight": bell_draw(key_of[10], (D, FF), D ** -0.5, 0.15625, ((0, 32),)),
        "down_weight": bell_draw(key_of[11], (FF, D), FF ** -0.5, 0.078125, ((0, 32),)),
        "up_scale": jnp.clip(jnp.exp(math.log(2.0) - 1.3862944 * jax.random.uniform(key_of[12], (FF,), jnp.float32) ** block_scale(key_of[12], (FF,), ((0, 32),), -0.2, 0.2)), 0.5, 2.0).astype(jnp.bfloat16),
        "gate_scale": jnp.clip(jnp.exp(math.log(2.0) - 1.3862944 * jax.random.uniform(key_of[13], (FF,), jnp.float32) ** block_scale(key_of[13], (FF,), ((0, 32),), -0.2, 0.2)), 0.5, 2.0).astype(jnp.bfloat16),
        "swiglu_step": jnp.clip(0.19921875 + 0.3984375 * jax.random.uniform(key_of[14], (D,), jnp.float32) ** block_scale(key_of[14], (D,), ((0, 32),), -0.2, 0.2), 0.19921875, 0.59765625).astype(jnp.bfloat16),
    }


eps = 1e-06
loss_scale = 32768.0
highest_precision = lax.Precision.HIGHEST

@jax.custom_vjp
def low(v):
    return lax.optimization_barrier(v.astype(jnp.bfloat16)).astype(jnp.float32)

@jax.custom_vjp
def low_back(v):
    return v

def low_keep(v):
    return (low(v), None)

def low_pass(kept, grad):
    return (grad,)

def back_keep(v):
    return (v, None)

def back_low(kept, grad):
    return (low(grad),)
low.defvjp(low_keep, low_pass)
low_back.defvjp(back_keep, back_low)

def normalize(value_rows):
    return value_rows * lax.rsqrt(lax.optimization_barrier(jnp.mean(value_rows * value_rows, axis=-1, keepdims=True)) + eps)

def project(value_rows, weight_matrix):
    return jnp.einsum('kiy,yg->kig', value_rows, weight_matrix, precision=highest_precision)

def attend_one(queries, keys, value_rows, length):
    full_len = queries.shape[0]
    block = min(512, full_len)
    positions = jnp.arange(full_len, dtype=jnp.int32)

    def one_block(index):
        start = (index * block).astype(jnp.int32)
        query_block = lax.dynamic_slice_in_dim(queries, start, block, 0)
        query_pos = start + jnp.arange(block, dtype=jnp.int32)
        scores = jnp.einsum('qhd,khd->hqk', query_block, keys, precision=highest_precision) * HD ** (-0.5)
        scores = low_back(scores)
        allowed = (positions[None, :] <= query_pos[:, None]) & (positions[None, :] < length)
        scores = jnp.where(allowed[None], scores, -1e+30)
        top = lax.optimization_barrier(jnp.max(scores, axis=-1, keepdims=True))
        weights = jnp.where(allowed[None], jnp.exp(scores - top), 0.0)
        total = lax.optimization_barrier(jnp.sum(weights, axis=-1))
        mixed = jnp.einsum('hqk,khd->qhd', low(weights), value_rows, precision=highest_precision)
        return mixed / jnp.transpose(total)[:, :, None]
    blocks = lax.map(jax.checkpoint(one_block), jnp.arange(full_len // block, dtype=jnp.int32))
    return blocks.reshape(queries.shape)

def layer(params, inputs, lens):
    w_query, w_key, w_value, w_output, gain_qk, step_attn, w_upper, w_gating, lower_weight, scale_upper, scale_gating, step_swiglu = params
    seqs_here, full_len, width = inputs.shape
    heads = width // HD
    gains = gain_qk.reshape(heads, HD)
    queries = low_back(project(inputs, w_query))
    keys_raw = low_back(project(inputs, w_key))
    values_raw = low_back(project(inputs, w_value))
    q_heads = low(gains * normalize(queries.reshape(seqs_here, full_len, heads, HD)))
    k_heads = low(gains * normalize(keys_raw.reshape(seqs_here, full_len, heads, HD)))
    v_heads = low(values_raw.reshape(seqs_here, full_len, heads, HD))
    mixed = jax.vmap(attend_one)(q_heads, k_heads, v_heads, lens)
    mixed = low(low_back(mixed.reshape(seqs_here, full_len, width)))
    branch = low_back(project(mixed, w_output))
    first = inputs + step_attn * (normalize(branch) - inputs)
    middle = normalize(first)
    middle_low = low(middle)
    upper = low_back(project(middle_low, w_upper))
    gating = low_back(project(middle_low, w_gating))
    hidden = low(upper * scale_upper * jax.nn.silu(gating * scale_gating))
    lower = low_back(project(hidden, lower_weight))
    second = middle + step_swiglu * (normalize(lower) - middle)
    return normalize(second)

def reference(inputs, teacher, lengths, query_weight, key_weight, value_projection, output_weight, score_gain, attention_step, up_weight, gate_weight, down_weight, up_scale, gate_scale, swiglu_step):
    params = tuple((p.astype(jnp.float32) for p in (query_weight, key_weight, value_projection, output_weight, score_gain, attention_step, up_weight, gate_weight, down_weight, up_scale, gate_scale, swiglu_step)))
    count = jnp.sum(lengths).astype(jnp.float32)
    per_step = math.gcd(SLOTS, max(1, 4096 // SLOT))
    groups = SLOTS // per_step
    states = inputs.astype(jnp.float32).reshape(groups, per_step, SLOT, D)
    targets = teacher.astype(jnp.float32).reshape(groups, per_step, SLOT, D)
    group_lens = lengths.reshape(groups, per_step)
    positions = jnp.arange(SLOT, dtype=jnp.int32)

    def step(carry, item):
        grads, err = carry
        state, target, lens = item

        def forward(weights, value_rows):
            return layer(weights, value_rows, lens)
        final, pull = jax.vjp(forward, params, state)
        valid = (positions[None, :] < lens[:, None]).astype(jnp.float32)[:, :, None]
        diff = final - target
        err = err + jnp.sum(valid * diff * diff)
        cot = loss_scale * 2.0 / count * valid * diff
        grad_params, grad_state = pull(cot)
        grads = jax.tree.map(lambda total, part: total + part, grads, grad_params)
        return ((grads, err), (final.astype(jnp.bfloat16), grad_state))
    zero_grads = tuple((jnp.zeros(p.shape, jnp.float32) for p in params))
    (grads, err), (finals, grad_states) = lax.scan(step, (zero_grads, jnp.zeros((), jnp.float32)), (states, targets, group_lens))
    layer_out = finals.reshape(SLOTS, SLOT, D)
    input_grad = grad_states.reshape(SLOTS, SLOT, D)
    distill_loss_mean = err / count
    return (layer_out, distill_loss_mean, input_grad, grads[0], grads[1], grads[2], grads[3], grads[4], grads[5], grads[6], grads[7], grads[8], grads[9], grads[10], grads[11])
```

```python
import functools

import jax
import jax.numpy as jnp
from jax import lax
from jax.experimental import pallas as pl
from jax.experimental.pallas import tpu as pltpu
from jax.sharding import PartitionSpec as P

HD = 64


eps = 1e-06
loss_scale = 32768.0


def normalize(value_rows):
    return value_rows * lax.rsqrt(jnp.mean(value_rows * value_rows, axis=-1, keepdims=True) + eps)


def norm_back(value_rows, normed, grad):
    factor = lax.rsqrt(jnp.mean(value_rows * value_rows, axis=-1, keepdims=True) + eps)
    return factor * (grad - normed * jnp.mean(grad * normed, axis=-1, keepdims=True))


def matmul(left, right):
    return jnp.dot(left, right, preferred_element_type=jnp.float32)


def left_tdot(left, right):
    return lax.dot_general(
        left, right, (((0,), (0,)), ((), ())), preferred_element_type=jnp.float32
    )


def right_tdot(left, right):
    return lax.dot_general(
        left, right, (((1,), (1,)), ((), ())), preferred_element_type=jnp.float32
    )


def block_scores(queries, keys, query_pos, key_pos, lens):
    scores = jnp.einsum(
        "sqhd,skhd->shqk", queries, keys, preferred_element_type=jnp.float32
    ) * HD ** (-0.5)
    allowed = (key_pos[None, None, :] <= query_pos[None, :, None]) & (
        key_pos[None, None, :] < lens[:, None, None]
    )
    return (scores, allowed[:, None])


BLK = 512
LANES = 128


def head_cols(ref, rows, offset):
    base = offset // LANES * LANES
    pair = ref[rows, base : base + LANES]
    return pair[:, offset - base : offset - base + HD]


def split3(v):
    hi = v.astype(jnp.bfloat16)
    rest = v - hi.astype(jnp.float32)
    mid = rest.astype(jnp.bfloat16)
    low = (rest - mid.astype(jnp.float32)).astype(jnp.bfloat16)
    return hi, mid, low


def attend_kernel(heads, length_ref, qkv_ref, gain_ref, mixed_ref, low_ref, qa_ref, ka_ref, va_ref, out_ref):
    tokens = qkv_ref.shape[0]
    width = heads * HD
    length = length_ref[0]
    lane = lax.broadcasted_iota(jnp.int32, (BLK, HD), 1)

    def prepare(block, carry):
        start = pl.multiple_of(block * BLK, BLK)
        rows = pl.ds(start, BLK)
        inside = (lax.broadcasted_iota(jnp.int32, (BLK, 1), 0) + start < length).astype(jnp.float32)
        ones = jnp.where(lane < 3, inside, 0.0).astype(jnp.bfloat16)
        nothing = jnp.zeros((BLK, HD), jnp.bfloat16)
        for head in range(heads):
            gain = gain_ref[:, head * HD : (head + 1) * HD]
            q = head_cols(qkv_ref, rows, head * HD)
            k = head_cols(qkv_ref, rows, width + head * HD)
            v = head_cols(qkv_ref, rows, 2 * width + head * HD)
            qn = q * lax.rsqrt(jnp.mean(q * q, axis=-1, keepdims=True) + eps)
            kn = k * lax.rsqrt(jnp.mean(k * k, axis=-1, keepdims=True) + eps)
            qs = (gain * qn).astype(jnp.bfloat16) * jnp.bfloat16(HD**-0.5)
            ks = (gain * kn * inside).astype(jnp.bfloat16)
            vs = (v * inside).astype(jnp.bfloat16)
            qa_ref[head, rows, :] = jnp.concatenate([qs, nothing], axis=1)
            ka_ref[head, rows, :] = jnp.concatenate([ks, ones], axis=1)
            va_ref[head, rows, :] = jnp.concatenate([vs, ones], axis=1)
        return carry

    lax.fori_loop(0, tokens // BLK, prepare, 0)
    causal = lax.broadcasted_iota(jnp.int32, (BLK, BLK), 1) <= lax.broadcasted_iota(jnp.int32, (BLK, BLK), 0)

    def per_head(head, carry):
        for qi in range(tokens // BLK):
            rows = pl.ds(qi * BLK, BLK)
            q = qa_ref[head, rows, :]
            acc = jnp.zeros((BLK, LANES), jnp.float32)
            for ki in range(qi + 1):
                keys = pl.ds(ki * BLK, BLK)
                scores = lax.dot_general(
                    q, ka_ref[head, keys, :], (((1,), (1,)), ((), ())), preferred_element_type=jnp.float32
                )
                weights = jnp.exp(scores)
                if ki == qi:
                    weights = jnp.where(causal, weights, 0.0)
                acc = acc + jnp.dot(
                    weights.astype(jnp.bfloat16), va_ref[head, keys, :], preferred_element_type=jnp.float32
                )
            total = acc[:, HD : HD + 1]
            out_ref[head, rows, :] = acc / total
            hi, mid, low = split3(-jnp.log(total))
            extra = jnp.where(lane == 0, hi, jnp.where(lane == 1, mid, jnp.where(lane == 2, low, jnp.zeros_like(low))))
            qa_ref[head, rows, :] = jnp.concatenate([q[:, :HD], extra], axis=1)
        return carry

    lax.fori_loop(0, heads, per_head, 0)

    def finish(block, carry):
        rows = pl.ds(pl.multiple_of(block * BLK, BLK), BLK)
        whole = jnp.concatenate([out_ref[head, rows, :][:, :HD] for head in range(heads)], axis=1)
        mixed_ref[rows, :] = whole
        low_ref[rows, :] = whole.astype(jnp.bfloat16)
        return carry

    lax.fori_loop(0, tokens // BLK, finish, 0)


def attend(qkv, gain, length):
    tokens, three = qkv.shape
    width = three // 3
    heads = width // HD
    vmem = pl.BlockSpec(memory_space=pltpu.VMEM)
    aug = jax.ShapeDtypeStruct((heads, tokens, LANES), jnp.bfloat16)
    return pl.pallas_call(
        functools.partial(attend_kernel, heads),
        out_shape=(
            jax.ShapeDtypeStruct((tokens, width), jnp.float32),
            jax.ShapeDtypeStruct((tokens, width), jnp.bfloat16),
            aug,
            aug,
            aug,
        ),
        in_specs=[pl.BlockSpec(memory_space=pltpu.SMEM), vmem, vmem],
        out_specs=(vmem,) * 5,
        scratch_shapes=[pltpu.VMEM((heads, tokens, LANES), jnp.float32)],
        compiler_params=pltpu.CompilerParams(vmem_limit_bytes=56 << 20),
        cost_estimate=pl.CostEstimate(
            flops=16 * heads * tokens * tokens * HD // 2, bytes_accessed=24 << 20, transcendentals=heads * tokens * tokens // 2
        ),
        name="attend",
    )(length, qkv, gain)


def attend_back_kernel(
    heads, length_ref, qkv_ref, gain_ref, mixed_ref, cot_ref, qa_ref, ka_ref, va_ref,
    grads_ref, gain_grad_ref, doa_ref, dq_ref, dk_ref, dv_ref,
):
    tokens = qkv_ref.shape[0]
    width = heads * HD
    length = length_ref[0]
    lane = lax.broadcasted_iota(jnp.int32, (BLK, HD), 1)

    def prepare(block, carry):
        rows = pl.ds(pl.multiple_of(block * BLK, BLK), BLK)
        for head in range(heads):
            d_mixed = head_cols(cot_ref, rows, head * HD)
            mixed = head_cols(mixed_ref, rows, head * HD)
            delta = jnp.sum(d_mixed.astype(jnp.float32) * mixed, axis=-1, keepdims=True)
            hi, mid, low = split3(-delta)
            extra = jnp.where(lane == 0, hi, jnp.where(lane == 1, mid, jnp.where(lane == 2, low, jnp.zeros_like(low))))
            doa_ref[head, rows, :] = jnp.concatenate([d_mixed, extra], axis=1)
        return carry

    lax.fori_loop(0, tokens // BLK, prepare, 0)
    causal = lax.broadcasted_iota(jnp.int32, (BLK, BLK), 0) <= lax.broadcasted_iota(jnp.int32, (BLK, BLK), 1)

    def per_head(head, carry):
        for ki in range(tokens // BLK):
            keys = pl.ds(ki * BLK, BLK)
            k = ka_ref[head, keys, :]
            v = va_ref[head, keys, :]
            dk = jnp.zeros((BLK, LANES), jnp.float32)
            dv = jnp.zeros((BLK, LANES), jnp.float32)
            for qi in range(ki, tokens // BLK):
                rows = pl.ds(qi * BLK, BLK)
                q = qa_ref[head, rows, :]
                d_out = doa_ref[head, rows, :]
                scores = lax.dot_general(k, q, (((1,), (1,)), ((), ())), preferred_element_type=jnp.float32)
                probs = jnp.exp(scores)
                if ki == qi:
                    probs = jnp.where(causal, probs, 0.0)
                d_probs = lax.dot_general(v, d_out, (((1,), (1,)), ((), ())), preferred_element_type=jnp.float32)
                d_scores = (probs * d_probs).astype(jnp.bfloat16)
                dv = dv + jnp.dot(probs.astype(jnp.bfloat16), d_out, preferred_element_type=jnp.float32)
                dk = dk + jnp.dot(d_scores, q, preferred_element_type=jnp.float32)
                dq = lax.dot_general(d_scores, k, (((0,), (0,)), ((), ())), preferred_element_type=jnp.float32)
                if ki == 0:
                    dq_ref[head, rows, :] = dq
                else:
                    dq_ref[head, rows, :] += dq
            dk_ref[head, keys, :] = dk
            dv_ref[head, keys, :] = dv
        return carry

    lax.fori_loop(0, heads, per_head, 0)

    def finish(block, sums):
        start = pl.multiple_of(block * BLK, BLK)
        rows = pl.ds(start, BLK)
        inside = lax.broadcasted_iota(jnp.int32, (BLK, 1), 0) + start < length
        dqs, dks, dvs, sums_new = [], [], [], []
        for head in range(heads):
            gain = gain_ref[:, head * HD : (head + 1) * HD]
            part = sums[head]
            for offset, ref, outs, scale in ((0, dq_ref, dqs, HD**-0.5), (width, dk_ref, dks, 1.0)):
                raw = head_cols(qkv_ref, rows, offset + head * HD)
                factor = lax.rsqrt(jnp.mean(raw * raw, axis=-1, keepdims=True) + eps)
                normed = raw * factor
                grad = ref[head, rows, :][:, :HD] * scale
                part = part + jnp.sum(grad * normed, axis=0, keepdims=True)
                scaled = grad * gain
                outs.append(
                    (factor * (scaled - normed * jnp.mean(scaled * normed, axis=-1, keepdims=True))).astype(jnp.bfloat16)
                )
            dvs.append(jnp.where(inside, dv_ref[head, rows, :][:, :HD], 0.0).astype(jnp.bfloat16))
            sums_new.append(part)
        grads_ref[rows, :] = jnp.concatenate(dqs + dks + dvs, axis=1)
        return tuple(sums_new)

    sums = lax.fori_loop(
        0, tokens // BLK, finish, tuple(jnp.zeros((1, HD), jnp.float32) for _ in range(heads))
    )
    gain_grad_ref[...] = jnp.concatenate(sums, axis=1)


def attend_back(qkv, gain, length, mixed, d_mixed, qa, ka, va):
    tokens, three = qkv.shape
    width = three // 3
    heads = width // HD
    vmem = pl.BlockSpec(memory_space=pltpu.VMEM)
    aug = pltpu.VMEM((heads, tokens, LANES), jnp.float32)
    return pl.pallas_call(
        functools.partial(attend_back_kernel, heads),
        out_shape=(
            jax.ShapeDtypeStruct((tokens, three), jnp.bfloat16),
            jax.ShapeDtypeStruct((1, width), jnp.float32),
        ),
        in_specs=[pl.BlockSpec(memory_space=pltpu.SMEM)] + [vmem] * 7,
        out_specs=(vmem,) * 2,
        scratch_shapes=[pltpu.VMEM((heads, tokens, LANES), jnp.bfloat16), aug, aug, aug],
        compiler_params=pltpu.CompilerParams(vmem_limit_bytes=60 << 20),
        cost_estimate=pl.CostEstimate(
            flops=40 * heads * tokens * tokens * HD // 2, bytes_accessed=24 << 20, transcendentals=heads * tokens * tokens // 2
        ),
        name="attend_back",
    )(length, qkv, gain, mixed, d_mixed, qa, ka, va)


CORE, XAX, YAX = 1, 2, 4


def swap_dp(v, bit):
    return lax.ppermute(v, "dp", [(i, i ^ bit) for i in range(8)])


def swap_z(v, mask):
    return lax.ppermute(v, "ctx", [(i, i ^ mask) for i in range(4)])


def pick(v, index, axis=0):
    return lax.dynamic_index_in_dim(v, index, axis, keepdims=False)


def gather_z(shard):
    far = swap_z(shard, 2)
    return {0: shard, 1: swap_z(shard, 1), 2: far, 3: swap_z(far, 1)}


def gather_chips(shard, flip):
    pieces = {}
    for mz, piece in gather_z(shard).items():
        y_first = (mz % 2 == 0) != flip
        first, second = (YAX, XAX) if y_first else (XAX, YAX)
        across = swap_dp(piece, first)
        for key, value in (
            (0, piece),
            (first, across),
            (second, swap_dp(piece, second)),
            (first | second, swap_dp(across, second)),
        ):
            pieces[(key // YAX, key // XAX % 2, mz)] = value
    return pieces


def assemble(pieces, coords, shape, place):
    keys = sorted(pieces)

    def kernel(coord_ref, *refs):
        out_ref, sems = refs[len(keys)], refs[len(keys) + 1]
        copies = []
        for at, key in enumerate(keys):
            where = place(*[jnp.bitwise_xor(coord_ref[d], key[d]) for d in range(len(key))])
            copies.append(pltpu.make_async_copy(refs[at], out_ref.at[where], sems.at[at]))
        for copy in copies:
            copy.start()
        for copy in copies:
            copy.wait()

    some = pieces[keys[0]]
    return pl.pallas_call(
        kernel,
        out_shape=jax.ShapeDtypeStruct(shape, some.dtype),
        in_specs=[pl.BlockSpec(memory_space=pltpu.SMEM)] + [pl.BlockSpec(memory_space=pl.ANY)] * len(keys),
        out_specs=pl.BlockSpec(memory_space=pltpu.VMEM),
        scratch_shapes=[pltpu.SemaphoreType.DMA((len(keys),))],
        compiler_params=pltpu.CompilerParams(vmem_limit_bytes=40 << 20),
        cost_estimate=pl.CostEstimate(flops=0, bytes_accessed=2 * len(keys) * some.size * some.dtype.itemsize, transcendentals=0),
        name="assemble",
    )(coords, *[pieces[key] for key in keys])


def add_low(a, b):
    return (a.astype(jnp.float32) + b.astype(jnp.float32)).astype(jnp.bfloat16)


def reduce_z(parts, z):
    relay = swap_z(pick(parts, z ^ 3), 1)
    far = add_low(pick(parts, z ^ 2), relay)
    near = swap_z(pick(parts, z ^ 1), 1)
    far = swap_z(far, 2)
    return pick(parts, z).astype(jnp.float32) + near.astype(jnp.float32) + far.astype(jnp.float32)


def reduce_xy(parts, x, y, x_first):
    if x_first:
        half = add_low(pick(parts, x, 1), swap_dp(pick(parts, 1 - x, 1), XAX))
        return add_low(pick(half, y), swap_dp(pick(half, 1 - y), YAX))
    half = add_low(pick(parts, y), swap_dp(pick(parts, 1 - y), YAX))
    return add_low(pick(half, x), swap_dp(pick(half, 1 - x), XAX))


def by_core(c, own, other, axis=0):
    return jnp.where(c == 0, jnp.stack([own, other], axis), jnp.stack([other, own], axis))


def on_cores(
    inputs,
    teacher,
    lengths,
    query_weight,
    key_weight,
    value_projection,
    output_weight,
    score_gain,
    attention_step,
    up_weight,
    gate_weight,
    down_weight,
    up_scale,
    gate_scale,
    swiglu_step,
):
    local, width = inputs.shape[1:]
    share = query_weight.shape[0]
    hidden_share = down_weight.shape[0]
    heads_width = width // 4
    tokens = local * 4
    low = jnp.bfloat16
    f32 = jnp.float32
    dp, z = lax.axis_index("dp"), lax.axis_index("ctx")
    c, x, y = dp % 2, dp // 2 % 2, dp // 4
    chip = jnp.stack([y, x, z]).astype(jnp.int32)
    line = z.astype(jnp.int32).reshape(1)
    states = inputs.reshape(local, width)

    shards = jnp.stack([query_weight, key_weight, value_projection], 1).reshape(share, 3, 4, heads_width)
    shards = shards.transpose(2, 0, 1, 3).reshape(4, share, 3 * heads_width)
    pieces = {(m,): swap_z(pick(shards, z ^ m), m) if m else pick(shards, z) for m in range(4)}
    rows_qkv = assemble(pieces, line, (4, share, 3 * heads_width), lambda zz: (zz,)).reshape(2, 2 * share, 3 * heads_width)
    pieces = {}
    for half, (first, second) in enumerate(((XAX, YAX), (YAX, XAX))):
        piece = rows_qkv[half]
        across = swap_dp(piece, first)
        for key, value in ((0, piece), (first, across), (second, swap_dp(piece, second)), (first | second, swap_dp(across, second))):
            for core in (0, 1):
                pieces[(key // YAX, key // XAX % 2, core, half)] = swap_dp(value, CORE) if core else value
    full_qkv = assemble(
        pieces,
        jnp.stack([y, x, c, jnp.zeros_like(c)]).astype(jnp.int32),
        (2, 2, 2, 2, 2 * share, 3 * heads_width),
        lambda yy, xx, cc, half: (yy, xx, cc, half),
    ).reshape(width, 3 * heads_width)

    whole_states = assemble(
        {(m,): piece for m, piece in gather_z(states).items()}, line, (4, local, width), lambda zz: (zz,)
    ).reshape(tokens, width)

    length_parts = jnp.stack([lengths[0] // 64, lengths[0] % 64]).astype(low)
    small = jnp.concatenate([score_gain, attention_step, up_scale, gate_scale, swiglu_step, length_parts])
    small = jnp.pad(small, (0, width - small.shape[0])).reshape(1, width)
    misc_rows = share + 8
    misc = jnp.concatenate([output_weight, small, jnp.zeros((7, width), low)], 0)
    misc = assemble(gather_chips(misc, False), chip, (2, 2, 4, misc_rows, width), lambda yy, xx, zz: (yy, xx, zz))
    misc = by_core(c, misc, swap_dp(misc, CORE), 2)
    full_output = misc[:, :, :, :, :share].reshape(width, width)
    vectors = misc[:, :, :, :, share]
    cuts = [0]
    for size in (share, share, hidden_share, hidden_share, share, 2):
        cuts.append(cuts[-1] + size)
    full_gain, full_astep, full_uscale, full_gscale, full_mstep, full_lengths = (
        vectors[..., a:b].astype(f32) for a, b in zip(cuts[:-1], cuts[1:])
    )
    count = jnp.sum(full_lengths[:, :, :, 0] * jnp.array([64.0, 1.0], f32))
    astep = full_astep.reshape(width)
    mstep = full_mstep.reshape(width)
    scale_up = pick(full_uscale, c, 2).reshape(-1)
    scale_gate = pick(full_gscale, c, 2).reshape(-1)
    gain = pick(full_gain.reshape(4, 1, heads_width), z)

    def halves(weight):
        cut = weight.reshape(share, 4, 2, hidden_share * 4)
        return cut[:, :, 0].reshape(share, -1), cut[:, :, 1].reshape(share, -1)

    up_halves, gate_halves = halves(up_weight), halves(gate_weight)
    half0 = jnp.concatenate([up_halves[0], gate_halves[0]], 1)
    half1 = jnp.concatenate([up_halves[1], gate_halves[1]], 1)
    own, other = jnp.where(c == 0, half0, half1), jnp.where(c == 0, half1, half0)
    shard = by_core(c, own, swap_dp(other, CORE))
    wide = half0.shape[1]
    hidden_half = wide // 2
    full_wide = assemble(
        gather_chips(shard, False), chip, (2, 2, 2, 4, share, wide), lambda yy, xx, zz: (yy, xx, slice(None), zz)
    ).reshape(width, wide)
    full_down = assemble(
        gather_chips(down_weight, True), chip, (2, 2, 4, hidden_share, width), lambda yy, xx, zz: (yy, xx, zz)
    ).reshape(hidden_half, width)

    qkv = matmul(whole_states, full_qkv)
    mixed, mixed_heads, qa, ka, va = attend(qkv, gain, lengths)
    blocks = mixed_heads.reshape(4, local, heads_width)
    pieces = {(m,): swap_z(pick(blocks, z ^ m), m) if m else pick(blocks, z) for m in range(4)}
    mixed_low = assemble(pieces, line, (4, local, heads_width), lambda zz: (zz,)).transpose(1, 0, 2).reshape(local, width)
    branch = matmul(mixed_low, full_output)
    resid = states.astype(f32)
    branch_norm = normalize(branch)
    first = resid + astep * (branch_norm - resid)
    middle = normalize(first)

    middle_low = middle.astype(low)
    middle_both = jnp.concatenate([middle_low, swap_dp(middle_low, CORE)], 0)
    both = matmul(middle_both, full_wide)
    upper, gating = both[:, :hidden_half], both[:, hidden_half:]
    upper_scaled = upper * scale_up
    gate_arg = gating * scale_gate
    gate_act = jax.nn.silu(gate_arg)
    hidden = (upper_scaled * gate_act).astype(low)
    lower = matmul(hidden, full_down)
    lower = lower[:local] + swap_dp(lower[local:], CORE)
    lower_norm = normalize(lower)
    second = middle + mstep * (lower_norm - middle)
    final = normalize(second)

    query_pos = z * local + jnp.arange(local, dtype=jnp.int32)
    valid = (query_pos < lengths[0]).astype(f32).reshape(local, 1)
    diff = final - teacher.reshape(local, width).astype(f32)
    err_local = jnp.sum(valid * diff * diff)
    cot = loss_scale * 2.0 / count * valid * diff

    d_second = norm_back(second, final, cot)
    d_middle = d_second * (1.0 - mstep)
    grad_mstep = jnp.sum(d_second * (lower_norm - middle), axis=0)
    d_lower = norm_back(lower, lower_norm, d_second * mstep).astype(low)
    d_lower_both = jnp.concatenate([d_lower, swap_dp(d_lower, CORE)], 0)
    grad_down = left_tdot(hidden, d_lower_both).astype(low).reshape(2, 2, 4, 2, hidden_share // 2, width)
    down_grad = jnp.concatenate(
        [reduce_z(reduce_xy(grad_down[:, :, :, part], x, y, part == 0), z) for part in range(2)], 0
    )
    d_hidden = right_tdot(d_lower_both, full_down)
    d_upper = d_hidden * gate_act
    sigmoid_gate = jax.nn.sigmoid(gate_arg)
    d_gate_arg = d_hidden * upper_scaled * (sigmoid_gate * (1.0 + gate_arg * (1.0 - sigmoid_gate)))
    grad_uscale = jnp.sum(d_upper * upper, axis=0)
    grad_gscale = jnp.sum(d_gate_arg * gating, axis=0)
    d_wide = jnp.concatenate([(d_upper * scale_up).astype(low), (d_gate_arg * scale_gate).astype(low)], 1)
    grad_wide = left_tdot(middle_both, d_wide).astype(low).reshape(2, 2, 2, 4, share, wide)
    wide_rows = [reduce_z(reduce_xy(grad_wide[:, :, core], x, y, core == 0), z) for core in range(2)]
    own = jnp.where(c == 0, wide_rows[0], wide_rows[1])
    other = swap_dp(jnp.where(c == 0, wide_rows[1], wide_rows[0]), CORE)
    wide_grad = by_core(c, own.reshape(share, 2, 4, -1), other.reshape(share, 2, 4, -1), 3)
    up_grad = wide_grad[:, 0].reshape(up_weight.shape)
    gate_grad = wide_grad[:, 1].reshape(up_weight.shape)
    d_both = right_tdot(d_wide, full_wide)
    d_middle = d_middle + d_both[:local] + swap_dp(d_both[local:], CORE)

    d_first = norm_back(first, middle, d_middle)
    input_grad = d_first * (1.0 - astep)
    grad_astep = jnp.sum(d_first * (branch_norm - resid), axis=0)
    d_branch = norm_back(branch, branch_norm, d_first * astep).astype(low)
    d_mixed = right_tdot(d_branch, full_output).astype(low)
    blocks = d_mixed.reshape(local, 4, heads_width).transpose(1, 0, 2)
    pieces = {(m,): swap_z(pick(blocks, z ^ m), m) if m else pick(blocks, z) for m in range(4)}
    d_mixed = assemble(pieces, line, (4, local, heads_width), lambda zz: (zz,)).reshape(tokens, heads_width)
    grad_output = left_tdot(mixed_low, d_branch).astype(low).reshape(2, 2, 2, 4, share, width)
    grad_output = add_low(pick(grad_output, c, 2), swap_dp(pick(grad_output, 1 - c, 2), CORE))
    output_grad = reduce_z(reduce_xy(grad_output, x, y, True), z)
    d_qkv, grad_gain = attend_back(qkv, gain, lengths, mixed, d_mixed, qa, ka, va)
    d_states = right_tdot(d_qkv, full_qkv).astype(low).reshape(4, local, width)
    input_grad = input_grad + reduce_z(d_states, z)
    grad_qkv = left_tdot(whole_states, d_qkv).astype(low).reshape(2, 2, 2, 2, 2 * share, 3 * heads_width)
    grad_qkv = add_low(pick(grad_qkv, c, 2), swap_dp(pick(grad_qkv, 1 - c, 2), CORE))
    rows_qkv = jnp.stack([reduce_xy(grad_qkv[:, :, half], x, y, half == 0) for half in range(2)])
    rows_qkv = rows_qkv.reshape(4, share, 3 * heads_width)
    pieces = {(m,): swap_z(pick(rows_qkv, z ^ m), m) if m else pick(rows_qkv, z) for m in range(4)}
    columns = assemble(pieces, line, (4, share, 3 * heads_width), lambda zz: (zz,))
    columns = columns.reshape(4, share, 3, heads_width).transpose(2, 1, 0, 3).reshape(3, share, width).astype(f32)

    gain_all = lax.dynamic_update_slice(jnp.zeros((4, heads_width), f32), grad_gain, (z, 0)).reshape(32, share)
    scales = jnp.concatenate([grad_uscale.reshape(2, 2, 4, hidden_share), grad_gscale.reshape(2, 2, 4, hidden_share)], -1)
    scales = jnp.where((jnp.arange(2) == c)[None, None, :, None, None], scales[:, :, None], 0.0).reshape(32, -1)
    packed = jnp.concatenate(
        [gain_all, grad_astep.reshape(32, share), scales, grad_mstep.reshape(32, share), jnp.full((32, 1), err_local)], 1
    )
    packed = jnp.pad(packed, ((0, 0), (0, 512 - packed.shape[1]))).reshape(2, 2, 2, 4, 4, 128)
    packed = pick(packed, c, 2) + swap_dp(pick(packed, 1 - c, 2), CORE)
    packed = pick(packed, x, 1) + swap_dp(pick(packed, 1 - x, 1), XAX)
    packed = pick(packed, y) + swap_dp(pick(packed, 1 - y), YAX)
    packed = (
        pick(packed, z)
        + swap_z(pick(packed, z ^ 1), 1)
        + swap_z(pick(packed, z ^ 2), 2)
        + swap_z(pick(packed, z ^ 3), 3)
    ).reshape(512)
    return (
        final.astype(low)[None],
        packed[cuts[5]] / count,
        input_grad[None],
        columns[0],
        columns[1],
        columns[2],
        output_grad,
        packed[: cuts[1]],
        packed[cuts[1] : cuts[2]],
        up_grad,
        gate_grad,
        down_grad,
        packed[cuts[2] : cuts[3]],
        packed[cuts[3] : cuts[4]],
        packed[cuts[4] : cuts[5]],
    )


def per_device(
    inputs,
    teacher,
    lengths,
    query_weight,
    key_weight,
    value_projection,
    output_weight,
    score_gain,
    attention_step,
    up_weight,
    gate_weight,
    down_weight,
    up_scale,
    gate_scale,
    swiglu_step,
):
    seqs, local, width = inputs.shape
    full_len = local * lax.axis_size("ctx")
    rows = seqs * local
    heads = width // HD
    key_block = min(512, full_len)
    query_pos = lax.axis_index("ctx") * local + jnp.arange(local, dtype=jnp.int32)
    valid = (query_pos[None, :] < lengths[:, None]).astype(jnp.float32).reshape(rows, 1)
    count_local = jnp.sum(valid)
    full_query, full_key, full_value, full_output, full_gain, full_astep = (
        lax.all_gather(query_weight, ("dp", "ctx"), axis=0, tiled=True),
        lax.all_gather(key_weight, ("dp", "ctx"), axis=0, tiled=True),
        lax.all_gather(value_projection, ("dp", "ctx"), axis=0, tiled=True),
        lax.all_gather(output_weight, ("dp", "ctx"), axis=0, tiled=True),
        lax.all_gather(score_gain, ("dp", "ctx"), axis=0, tiled=True),
        lax.all_gather(attention_step, ("dp", "ctx"), axis=0, tiled=True),
    )
    states = inputs.reshape(rows, width)
    resid = states.astype(jnp.float32)
    queries = matmul(states, full_query)
    keys_raw = matmul(states, full_key)
    values_raw = matmul(states, full_value)
    gains = full_gain.astype(jnp.float32).reshape(heads, HD)
    query_norm = normalize(queries.reshape(rows, heads, HD))
    key_norm = normalize(keys_raw.reshape(rows, heads, HD))
    q_heads = (gains * query_norm).astype(jnp.bfloat16).reshape(seqs, local, heads, HD)
    k_flat = (gains * key_norm).astype(jnp.bfloat16).reshape(seqs, local, width)
    v_flat = values_raw.astype(jnp.bfloat16).reshape(seqs, local, width)

    def key_step(carry, key_piece, value_piece, key_pos):
        top, total, accum = carry
        count_keys = key_piece.shape[1]
        scores, allowed = block_scores(
            q_heads, key_piece.reshape(seqs, count_keys, heads, HD), query_pos, key_pos, lengths
        )
        scores = jnp.where(allowed, scores, -1e30)
        top_new = jnp.maximum(top, jnp.max(scores, axis=-1))
        weights = jnp.where(allowed, jnp.exp(scores - top_new[..., None]), 0.0)
        factor = jnp.exp(top - top_new)
        total = total * factor + jnp.sum(weights, axis=-1)
        accum = accum * jnp.transpose(factor, (0, 2, 1))[..., None] + jnp.einsum(
            "shqk,skhd->sqhd",
            weights.astype(jnp.bfloat16),
            value_piece.reshape(seqs, count_keys, heads, HD),
            preferred_element_type=jnp.float32,
        )
        return (top_new, total, accum)

    init = (
        jnp.full((seqs, heads, local), -1e30, jnp.float32),
        jnp.zeros((seqs, heads, local), jnp.float32),
        jnp.zeros((seqs, local, heads, HD), jnp.float32),
    )
    carry = init
    key_piece = lax.all_gather(k_flat, "ctx", axis=1, tiled=True)
    value_piece = lax.all_gather(v_flat, "ctx", axis=1, tiled=True)
    count_keys = key_piece.shape[1]

    def inner(state, index):
        offset = index * key_block
        key_part = lax.dynamic_slice_in_dim(key_piece, offset, key_block, 1)
        value_part = lax.dynamic_slice_in_dim(value_piece, offset, key_block, 1)
        positions = offset + jnp.arange(key_block, dtype=jnp.int32)
        return (key_step(state, key_part, value_part, positions), None)

    carry, unused = lax.scan(inner, carry, jnp.arange(count_keys // key_block, dtype=jnp.int32))
    top, total, accum = carry
    mixed = accum / jnp.transpose(total, (0, 2, 1))[..., None]
    log_total = top + jnp.log(total)
    mixed_low = mixed.reshape(rows, width).astype(jnp.bfloat16)
    branch = matmul(mixed_low, full_output)
    branch_norm = normalize(branch)
    astep = full_astep.astype(jnp.float32)
    first = resid + astep * (branch_norm - resid)
    middle = normalize(first)
    middle_low = middle.astype(jnp.bfloat16)
    full_up, full_gate, full_down, full_uscale, complete_gate_scale, full_mstep = (
        lax.all_gather(up_weight, ("dp", "ctx"), axis=0, tiled=True),
        lax.all_gather(gate_weight, ("dp", "ctx"), axis=0, tiled=True),
        lax.all_gather(down_weight, ("dp", "ctx"), axis=0, tiled=True),
        lax.all_gather(up_scale, ("dp", "ctx"), axis=0, tiled=True),
        lax.all_gather(gate_scale, ("dp", "ctx"), axis=0, tiled=True),
        lax.all_gather(swiglu_step, ("dp", "ctx"), axis=0, tiled=True),
    )
    upper = matmul(middle_low, full_up)
    gating = matmul(middle_low, full_gate)
    scale_up = full_uscale.astype(jnp.float32)
    scale_gate = complete_gate_scale.astype(jnp.float32)
    upper_scaled = upper * scale_up
    gate_arg = gating * scale_gate
    gate_act = jax.nn.silu(gate_arg)
    hidden = (upper_scaled * gate_act).astype(jnp.bfloat16)
    lower = matmul(hidden, full_down)
    lower_norm = normalize(lower)
    mstep = full_mstep.astype(jnp.float32)
    second = middle + mstep * (lower_norm - middle)
    final = normalize(second)
    target = teacher.reshape(rows, width).astype(jnp.float32)
    diff = final - target
    err_local = jnp.sum(valid * diff * diff)
    err_total, count = lax.psum((err_local, count_local), ("dp", "ctx"))
    cot = loss_scale * 2.0 / count * valid * diff
    full_up, full_gate, full_down, full_uscale, complete_gate_scale, full_mstep = (
        lax.all_gather(up_weight, ("dp", "ctx"), axis=0, tiled=True),
        lax.all_gather(gate_weight, ("dp", "ctx"), axis=0, tiled=True),
        lax.all_gather(down_weight, ("dp", "ctx"), axis=0, tiled=True),
        lax.all_gather(up_scale, ("dp", "ctx"), axis=0, tiled=True),
        lax.all_gather(gate_scale, ("dp", "ctx"), axis=0, tiled=True),
        lax.all_gather(swiglu_step, ("dp", "ctx"), axis=0, tiled=True),
    )
    d_second = norm_back(second, final, cot)
    d_middle = d_second * (1.0 - mstep)
    grad_mstep = jnp.sum(d_second * (lower_norm - middle), axis=0)
    d_lower = norm_back(lower, lower_norm, d_second * mstep).astype(jnp.bfloat16)
    grad_down = left_tdot(hidden, d_lower)
    d_hidden = right_tdot(d_lower, full_down)
    d_upper = d_hidden * gate_act
    sigmoid_gate = jax.nn.sigmoid(gate_arg)
    d_gate_arg = d_hidden * upper_scaled * (sigmoid_gate * (1.0 + gate_arg * (1.0 - sigmoid_gate)))
    grad_uscale = jnp.sum(d_upper * upper, axis=0)
    grad_gscale = jnp.sum(d_gate_arg * gating, axis=0)
    d_up_low = (d_upper * scale_up).astype(jnp.bfloat16)
    d_gate_low = (d_gate_arg * scale_gate).astype(jnp.bfloat16)
    d_middle = d_middle + right_tdot(d_up_low, full_up) + right_tdot(d_gate_low, full_gate)
    grad_up = left_tdot(middle_low, d_up_low)
    grad_gate = left_tdot(middle_low, d_gate_low)
    up_grad, gate_grad, down_grad, up_scale_grad, gate_scale_gradient, swiglu_step_grad = (
        lax.psum_scatter(grad_up, ("dp", "ctx"), scatter_dimension=0, tiled=True),
        lax.psum_scatter(grad_gate, ("dp", "ctx"), scatter_dimension=0, tiled=True),
        lax.psum_scatter(grad_down, ("dp", "ctx"), scatter_dimension=0, tiled=True),
        lax.psum_scatter(grad_uscale, ("dp", "ctx"), scatter_dimension=0, tiled=True),
        lax.psum_scatter(grad_gscale, ("dp", "ctx"), scatter_dimension=0, tiled=True),
        lax.psum_scatter(grad_mstep, ("dp", "ctx"), scatter_dimension=0, tiled=True),
    )
    d_first = norm_back(first, middle, d_middle)
    input_grad = d_first * (1.0 - astep)
    grad_astep = jnp.sum(d_first * (branch_norm - resid), axis=0)
    d_branch = norm_back(branch, branch_norm, d_first * astep).astype(jnp.bfloat16)
    full_query, full_key, full_value, full_output, full_gain, full_astep = (
        lax.all_gather(query_weight, ("dp", "ctx"), axis=0, tiled=True),
        lax.all_gather(key_weight, ("dp", "ctx"), axis=0, tiled=True),
        lax.all_gather(value_projection, ("dp", "ctx"), axis=0, tiled=True),
        lax.all_gather(output_weight, ("dp", "ctx"), axis=0, tiled=True),
        lax.all_gather(score_gain, ("dp", "ctx"), axis=0, tiled=True),
        lax.all_gather(attention_step, ("dp", "ctx"), axis=0, tiled=True),
    )
    gains = full_gain.astype(jnp.float32).reshape(heads, HD)
    grad_output = left_tdot(mixed_low, d_branch)
    d_mixed = right_tdot(d_branch, full_output).astype(jnp.bfloat16)
    d_mixed_heads = d_mixed.reshape(seqs, local, heads, HD)
    delta = jnp.transpose(jnp.sum(d_mixed_heads.astype(jnp.float32) * mixed, axis=-1), (0, 2, 1))
    whole_keys, whole_values = (
        lax.all_gather(k_flat, "ctx", axis=1, tiled=True),
        lax.all_gather(v_flat, "ctx", axis=1, tiled=True),
    )

    def query_terms(index):
        offset = index * key_block
        key_part = lax.dynamic_slice_in_dim(whole_keys, offset, key_block, 1).reshape(
            seqs, key_block, heads, HD
        )
        value_part = lax.dynamic_slice_in_dim(whole_values, offset, key_block, 1).reshape(
            seqs, key_block, heads, HD
        )
        key_pos = offset + jnp.arange(key_block, dtype=jnp.int32)
        scores, allowed = block_scores(q_heads, key_part, query_pos, key_pos, lengths)
        probs = jnp.where(allowed, jnp.exp(scores - log_total[..., None]), 0.0)
        d_probs = jnp.einsum(
            "sqhd,skhd->shqk", d_mixed_heads, value_part, preferred_element_type=jnp.float32
        )
        d_scores = (probs * (d_probs - delta[..., None])).astype(jnp.bfloat16)
        d_query_part = jnp.einsum(
            "shqk,skhd->sqhd", d_scores, key_part, preferred_element_type=jnp.float32
        )
        return (offset, probs, d_scores, d_query_part)

    def key_back(carry, index):
        d_query_acc, d_key_all, d_value_all = carry
        offset, probs, d_scores, d_query_part = query_terms(index)
        d_query_acc = d_query_acc + d_query_part
        d_key_part = jnp.einsum(
            "shqk,sqhd->skhd", d_scores, q_heads, preferred_element_type=jnp.float32
        ) * HD ** (-0.5)
        d_value_part = jnp.einsum(
            "shqk,sqhd->skhd",
            probs.astype(jnp.bfloat16),
            d_mixed_heads,
            preferred_element_type=jnp.float32,
        )
        d_key_all = lax.dynamic_update_slice_in_dim(
            d_key_all, d_key_part.reshape(seqs, key_block, width), offset, 1
        )
        d_value_all = lax.dynamic_update_slice_in_dim(
            d_value_all, d_value_part.reshape(seqs, key_block, width), offset, 1
        )
        return ((d_query_acc, d_key_all, d_value_all), None)

    start_carry = (
        jnp.zeros((seqs, local, heads, HD), jnp.float32),
        jnp.zeros((seqs, full_len, width), jnp.float32),
        jnp.zeros((seqs, full_len, width), jnp.float32),
    )
    (d_query_heads, d_key_all, d_value_all), unused = lax.scan(
        key_back, start_carry, jnp.arange(full_len // key_block, dtype=jnp.int32)
    )
    d_key_local, d_value_local = (
        lax.psum_scatter(
            d_key_all.astype(jnp.bfloat16), "ctx", scatter_dimension=1, tiled=True
        ).astype(jnp.float32),
        lax.psum_scatter(
            d_value_all.astype(jnp.bfloat16), "ctx", scatter_dimension=1, tiled=True
        ).astype(jnp.float32),
    )
    d_key_heads = d_key_local.reshape(rows, heads, HD)
    d_value_local = d_value_local.reshape(rows, width)
    d_query_heads = (d_query_heads * HD ** (-0.5)).reshape(rows, heads, HD)
    grad_gain = jnp.sum(d_query_heads * query_norm, axis=0) + jnp.sum(
        d_key_heads * key_norm, axis=0
    )
    d_query_low = (
        norm_back(queries.reshape(rows, heads, HD), query_norm, d_query_heads * gains)
        .reshape(rows, width)
        .astype(jnp.bfloat16)
    )
    d_key_low = (
        norm_back(keys_raw.reshape(rows, heads, HD), key_norm, d_key_heads * gains)
        .reshape(rows, width)
        .astype(jnp.bfloat16)
    )
    d_value_low = d_value_local.astype(jnp.bfloat16)
    input_grad = (
        input_grad
        + right_tdot(d_query_low, full_query)
        + right_tdot(d_key_low, full_key)
        + right_tdot(d_value_low, full_value)
    )
    grad_query = left_tdot(states, d_query_low)
    grad_key = left_tdot(states, d_key_low)
    grad_value = left_tdot(states, d_value_low)
    query_grad, key_grad, value_grad, output_grad, score_gain_grad, attention_step_grad = (
        lax.psum_scatter(grad_query, ("dp", "ctx"), scatter_dimension=0, tiled=True),
        lax.psum_scatter(grad_key, ("dp", "ctx"), scatter_dimension=0, tiled=True),
        lax.psum_scatter(grad_value, ("dp", "ctx"), scatter_dimension=0, tiled=True),
        lax.psum_scatter(grad_output, ("dp", "ctx"), scatter_dimension=0, tiled=True),
        lax.psum_scatter(grad_gain.reshape(width), ("dp", "ctx"), scatter_dimension=0, tiled=True),
        lax.psum_scatter(grad_astep, ("dp", "ctx"), scatter_dimension=0, tiled=True),
    )
    distill_loss_mean = err_total / count
    layer_out = final.astype(jnp.bfloat16).reshape(seqs, local, width)
    return (
        layer_out,
        distill_loss_mean,
        input_grad.reshape(seqs, local, width),
        query_grad,
        key_grad,
        value_grad,
        output_grad,
        score_gain_grad,
        attention_step_grad,
        up_grad,
        gate_grad,
        down_grad,
        up_scale_grad,
        gate_scale_gradient,
        swiglu_step_grad,
    )


def solution(mesh):
    placed = (
        P("dp", "ctx", None),
        P("dp", "ctx", None),
        P("dp"),
        P(("dp", "ctx"), None),
        P(("dp", "ctx"), None),
        P(("dp", "ctx"), None),
        P(("dp", "ctx"), None),
        P(("dp", "ctx")),
        P(("dp", "ctx")),
        P(("dp", "ctx"), None),
        P(("dp", "ctx"), None),
        P(("dp", "ctx"), None),
        P(("dp", "ctx")),
        P(("dp", "ctx")),
        P(("dp", "ctx")),
    )
    on_one = on_cores if dict(mesh.shape) == {"dp": 8, "ctx": 4} else per_device
    return jax.shard_map(
        on_one,
        mesh=mesh,
        in_specs=placed,
        out_specs=(
            P("dp", "ctx", None),
            P(),
            P("dp", "ctx", None),
            P(("dp", "ctx"), None),
            P(("dp", "ctx"), None),
            P(("dp", "ctx"), None),
            P(("dp", "ctx"), None),
            P(("dp", "ctx")),
            P(("dp", "ctx")),
            P(("dp", "ctx"), None),
            P(("dp", "ctx"), None),
            P(("dp", "ctx"), None),
            P(("dp", "ctx")),
            P(("dp", "ctx")),
            P(("dp", "ctx")),
        ),
        check_vma=False,
    )
```

```python
import functools

import jax
import jax.numpy as jnp
from jax import lax
from jax.experimental import pallas as pl
from jax.experimental.pallas import tpu as pltpu
from jax.sharding import PartitionSpec as P

HD = 64


eps = 1e-06
loss_scale = 32768.0


def normalize(value_rows):
    return value_rows * lax.rsqrt(jnp.mean(value_rows * value_rows, axis=-1, keepdims=True) + eps)


def norm_back(value_rows, normed, grad):
    factor = lax.rsqrt(jnp.mean(value_rows * value_rows, axis=-1, keepdims=True) + eps)
    return factor * (grad - normed * jnp.mean(grad * normed, axis=-1, keepdims=True))


def matmul(left, right):
    return jnp.dot(left, right, preferred_element_type=jnp.float32)


def left_tdot(left, right):
    return lax.dot_general(
        left, right, (((0,), (0,)), ((), ())), preferred_element_type=jnp.float32
    )


def right_tdot(left, right):
    return lax.dot_general(
        left, right, (((1,), (1,)), ((), ())), preferred_element_type=jnp.float32
    )


def block_scores(queries, keys, query_pos, key_pos, lens):
    scores = jnp.einsum(
        "sqhd,skhd->shqk", queries, keys, preferred_element_type=jnp.float32
    ) * HD ** (-0.5)
    allowed = (key_pos[None, None, :] <= query_pos[None, :, None]) & (
        key_pos[None, None, :] < lens[:, None, None]
    )
    return (scores, allowed[:, None])


BLK = 512
LANES = 128


def head_cols(ref, rows, offset):
    base = offset // LANES * LANES
    pair = ref[rows, base : min(base + LANES, ref.shape[1])]
    return pair[:, offset - base : offset - base + HD]


def split3(v):
    hi = v.astype(jnp.bfloat16)
    rest = v - hi.astype(jnp.float32)
    mid = rest.astype(jnp.bfloat16)
    low = (rest - mid.astype(jnp.float32)).astype(jnp.bfloat16)
    return hi, mid, low


def attend_kernel(heads, length_ref, qkv_ref, gain_ref, mixed_ref, low_ref, qa_ref, ka_ref, va_ref, out_ref):
    tokens = qkv_ref.shape[0]
    width = heads * HD
    length = length_ref[0]
    lane = lax.broadcasted_iota(jnp.int32, (BLK, HD), 1)

    def prepare(block, carry):
        start = pl.multiple_of(block * BLK, BLK)
        rows = pl.ds(start, BLK)
        inside = (lax.broadcasted_iota(jnp.int32, (BLK, 1), 0) + start < length).astype(jnp.float32)
        ones = jnp.where(lane < 3, inside, 0.0).astype(jnp.bfloat16)
        nothing = jnp.zeros((BLK, HD), jnp.bfloat16)
        for head in range(heads):
            gain = gain_ref[:, head * HD : (head + 1) * HD]
            q = head_cols(qkv_ref, rows, head * HD)
            k = head_cols(qkv_ref, rows, width + head * HD)
            v = head_cols(qkv_ref, rows, 2 * width + head * HD)
            qn = q * lax.rsqrt(jnp.mean(q * q, axis=-1, keepdims=True) + eps)
            kn = k * lax.rsqrt(jnp.mean(k * k, axis=-1, keepdims=True) + eps)
            qs = (gain * qn).astype(jnp.bfloat16) * jnp.bfloat16(HD**-0.5)
            ks = (gain * kn * inside).astype(jnp.bfloat16)
            vs = (v * inside).astype(jnp.bfloat16)
            qa_ref[head, rows, :] = jnp.concatenate([qs, nothing], axis=1)
            ka_ref[head, rows, :] = jnp.concatenate([ks, ones], axis=1)
            va_ref[head, rows, :] = jnp.concatenate([vs, ones], axis=1)
        return carry

    lax.fori_loop(0, tokens // BLK, prepare, 0)
    causal = lax.broadcasted_iota(jnp.int32, (BLK, BLK), 1) <= lax.broadcasted_iota(jnp.int32, (BLK, BLK), 0)

    def per_head(head, carry):
        for qi in range(tokens // BLK):
            rows = pl.ds(qi * BLK, BLK)
            q = qa_ref[head, rows, :]
            acc = jnp.zeros((BLK, LANES), jnp.float32)
            for ki in range(qi + 1):
                keys = pl.ds(ki * BLK, BLK)
                scores = lax.dot_general(
                    q, ka_ref[head, keys, :], (((1,), (1,)), ((), ())), preferred_element_type=jnp.float32
                )
                weights = jnp.exp(scores)
                if ki == qi:
                    weights = jnp.where(causal, weights, 0.0)
                acc = acc + jnp.dot(
                    weights.astype(jnp.bfloat16), va_ref[head, keys, :], preferred_element_type=jnp.float32
                )
            total = acc[:, HD : HD + 1]
            out_ref[head, rows, :] = acc / total
            hi, mid, low = split3(-jnp.log(total))
            extra = jnp.where(lane == 0, hi, jnp.where(lane == 1, mid, jnp.where(lane == 2, low, jnp.zeros_like(low))))
            qa_ref[head, rows, :] = jnp.concatenate([q[:, :HD], extra], axis=1)
        return carry

    lax.fori_loop(0, heads, per_head, 0)

    def finish(block, carry):
        rows = pl.ds(pl.multiple_of(block * BLK, BLK), BLK)
        whole = jnp.concatenate([out_ref[head, rows, :][:, :HD] for head in range(heads)], axis=1)
        mixed_ref[rows, :] = whole
        low_ref[rows, :] = whole.astype(jnp.bfloat16)
        return carry

    lax.fori_loop(0, tokens // BLK, finish, 0)


def attend(qkv, gain, length):
    tokens, width = qkv.shape[0], gain.shape[1]
    heads = width // HD
    vmem = pl.BlockSpec(memory_space=pltpu.VMEM)
    aug = jax.ShapeDtypeStruct((heads, tokens, LANES), jnp.bfloat16)
    return pl.pallas_call(
        functools.partial(attend_kernel, heads),
        out_shape=(
            jax.ShapeDtypeStruct((tokens, width), jnp.float32),
            jax.ShapeDtypeStruct((tokens, width), jnp.bfloat16),
            aug,
            aug,
            aug,
        ),
        in_specs=[pl.BlockSpec(memory_space=pltpu.SMEM), vmem, vmem],
        out_specs=(vmem,) * 5,
        scratch_shapes=[pltpu.VMEM((heads, tokens, LANES), jnp.float32)],
        compiler_params=pltpu.CompilerParams(vmem_limit_bytes=56 << 20),
        cost_estimate=pl.CostEstimate(
            flops=heads * tokens * tokens, bytes_accessed=8 << 20, transcendentals=0
        ),
        name="attend",
    )(length, qkv, gain)


def attend_back_kernel(
    heads, length_ref, qkv_ref, gain_ref, mixed_ref, cot_ref, qa_ref, ka_ref, va_ref,
    grads_ref, gain_grad_ref, doa_ref, dq_ref, dk_ref, dv_ref,
):
    tokens = qkv_ref.shape[0]
    width = heads * HD
    length = length_ref[0]
    lane = lax.broadcasted_iota(jnp.int32, (BLK, HD), 1)

    def prepare(block, carry):
        rows = pl.ds(pl.multiple_of(block * BLK, BLK), BLK)
        for head in range(heads):
            d_mixed = head_cols(cot_ref, rows, head * HD)
            mixed = head_cols(mixed_ref, rows, head * HD)
            delta = jnp.sum(d_mixed.astype(jnp.float32) * mixed, axis=-1, keepdims=True)
            hi, mid, low = split3(-delta)
            extra = jnp.where(lane == 0, hi, jnp.where(lane == 1, mid, jnp.where(lane == 2, low, jnp.zeros_like(low))))
            doa_ref[head, rows, :] = jnp.concatenate([d_mixed, extra], axis=1)
        return carry

    lax.fori_loop(0, tokens // BLK, prepare, 0)
    causal = lax.broadcasted_iota(jnp.int32, (BLK, BLK), 0) <= lax.broadcasted_iota(jnp.int32, (BLK, BLK), 1)

    def per_head(head, carry):
        for ki in range(tokens // BLK):
            keys = pl.ds(ki * BLK, BLK)
            k = ka_ref[head, keys, :]
            v = va_ref[head, keys, :]
            dk = jnp.zeros((BLK, LANES), jnp.float32)
            dv = jnp.zeros((BLK, LANES), jnp.float32)
            for qi in range(ki, tokens // BLK):
                rows = pl.ds(qi * BLK, BLK)
                q = qa_ref[head, rows, :]
                d_out = doa_ref[head, rows, :]
                scores = lax.dot_general(k, q, (((1,), (1,)), ((), ())), preferred_element_type=jnp.float32)
                probs = jnp.exp(scores)
                if ki == qi:
                    probs = jnp.where(causal, probs, 0.0)
                d_probs = lax.dot_general(v, d_out, (((1,), (1,)), ((), ())), preferred_element_type=jnp.float32)
                d_scores = (probs * d_probs).astype(jnp.bfloat16)
                dv = dv + jnp.dot(probs.astype(jnp.bfloat16), d_out, preferred_element_type=jnp.float32)
                dk = dk + jnp.dot(d_scores, q, preferred_element_type=jnp.float32)
                dq = lax.dot_general(d_scores, k, (((0,), (0,)), ((), ())), preferred_element_type=jnp.float32)
                if ki == 0:
                    dq_ref[head, rows, :] = dq
                else:
                    dq_ref[head, rows, :] += dq
            dk_ref[head, keys, :] = dk
            dv_ref[head, keys, :] = dv
        return carry

    lax.fori_loop(0, heads, per_head, 0)

    def finish(block, sums):
        start = pl.multiple_of(block * BLK, BLK)
        rows = pl.ds(start, BLK)
        inside = lax.broadcasted_iota(jnp.int32, (BLK, 1), 0) + start < length
        dqs, dks, dvs, sums_new = [], [], [], []
        for head in range(heads):
            gain = gain_ref[:, head * HD : (head + 1) * HD]
            part = sums[head]
            for offset, ref, outs, scale in ((0, dq_ref, dqs, HD**-0.5), (width, dk_ref, dks, 1.0)):
                raw = head_cols(qkv_ref, rows, offset + head * HD)
                factor = lax.rsqrt(jnp.mean(raw * raw, axis=-1, keepdims=True) + eps)
                normed = raw * factor
                grad = ref[head, rows, :][:, :HD] * scale
                part = part + jnp.sum(grad * normed, axis=0, keepdims=True)
                scaled = grad * gain
                outs.append(
                    (factor * (scaled - normed * jnp.mean(scaled * normed, axis=-1, keepdims=True))).astype(jnp.bfloat16)
                )
            dvs.append(jnp.where(inside, dv_ref[head, rows, :][:, :HD], 0.0).astype(jnp.bfloat16))
            sums_new.append(part)
        rest = grads_ref.shape[1] - 3 * width
        nothing = [jnp.zeros((BLK, rest), jnp.bfloat16)] if rest else []
        grads_ref[rows, :] = jnp.concatenate(dqs + dks + dvs + nothing, axis=1)
        return tuple(sums_new)

    sums = lax.fori_loop(
        0, tokens // BLK, finish, tuple(jnp.zeros((1, HD), jnp.float32) for _ in range(heads))
    )
    gain_grad_ref[...] = jnp.concatenate(sums, axis=1)


def attend_back(qkv, gain, length, mixed, d_mixed, qa, ka, va):
    tokens, three = qkv.shape
    width = gain.shape[1]
    heads = width // HD
    vmem = pl.BlockSpec(memory_space=pltpu.VMEM)
    aug = pltpu.VMEM((heads, tokens, LANES), jnp.float32)
    return pl.pallas_call(
        functools.partial(attend_back_kernel, heads),
        out_shape=(
            jax.ShapeDtypeStruct((tokens, three), jnp.bfloat16),
            jax.ShapeDtypeStruct((1, width), jnp.float32),
        ),
        in_specs=[pl.BlockSpec(memory_space=pltpu.SMEM)] + [vmem] * 7,
        out_specs=(vmem,) * 2,
        scratch_shapes=[pltpu.VMEM((heads, tokens, LANES), jnp.bfloat16), aug, aug, aug],
        compiler_params=pltpu.CompilerParams(vmem_limit_bytes=60 << 20),
        cost_estimate=pl.CostEstimate(
            flops=heads * tokens * tokens, bytes_accessed=8 << 20, transcendentals=0
        ),
        name="attend_back",
    )(length, qkv, gain, mixed, d_mixed, qa, ka, va)


CORE, XAX, YAX = 1, 2, 4
GROUPS = ((0, 3), (3, 5))


def swap_dp(v, bit):
    return lax.ppermute(v, "dp", [(i, i ^ bit) for i in range(8)])


def swap_z(v, mask):
    return lax.ppermute(v, "ctx", [(i, i ^ mask) for i in range(4)])


def fence(*arrays):
    return lax.optimization_barrier(arrays)


def pick(v, index, axis=0):
    return lax.dynamic_index_in_dim(v, index, axis, keepdims=False)


def assemble(pieces, coords, shapes, place):
    keys = sorted(pieces)
    count = len(keys)

    def kernel(coord_ref, *refs):
        outs, sems = refs[count : count + len(shapes)], refs[-1]
        copies = []
        for at, key in enumerate(keys):
            where = place(*[jnp.bitwise_xor(coord_ref[d], key[d]) for d in range(len(key))])
            for out, (out_ref, (index, rows)) in enumerate(zip(outs, where)):
                source = refs[at] if rows is None else refs[at].at[pl.ds(*rows)]
                copies.append(pltpu.make_async_copy(source, out_ref.at[index], sems.at[at, out]))
        for copy in copies:
            copy.start()
        for copy in copies:
            copy.wait()

    some = pieces[keys[0]]
    outs = pl.pallas_call(
        kernel,
        out_shape=[jax.ShapeDtypeStruct(shape, some.dtype) for shape in shapes],
        in_specs=[pl.BlockSpec(memory_space=pltpu.SMEM)] + [pl.BlockSpec(memory_space=pltpu.HBM)] * count,
        out_specs=[pl.BlockSpec(memory_space=pltpu.VMEM)] * len(shapes),
        scratch_shapes=[pltpu.SemaphoreType.DMA((count, len(shapes)))],
        compiler_params=pltpu.CompilerParams(vmem_limit_bytes=60 << 20),
        cost_estimate=pl.CostEstimate(flops=0, bytes_accessed=2 * count * some.size * some.dtype.itemsize, transcendentals=0),
        name="assemble",
    )(coords, *[pieces[key] for key in keys])
    return outs


def add_low(a, b):
    return (a.astype(jnp.float32) + b.astype(jnp.float32)).astype(jnp.bfloat16)


def by_core(c, own, other, axis=0):
    return jnp.where(c == 0, jnp.stack([own, other], axis), jnp.stack([other, own], axis))


def add3(a, b, d):
    return (a.astype(jnp.float32) + b.astype(jnp.float32) + d.astype(jnp.float32)).astype(jnp.bfloat16)


class Plane:
    def __init__(self, whole, y, x, x_first):
        self.whole, self.y, self.x, self.x_first = whole, y, x, x_first
        self.links = (XAX, YAX) if x_first else (YAX, XAX)

    def cell(self, y_other, x_other):
        v = self.whole
        yy = 1 - self.y if y_other else self.y
        xx = 1 - self.x if x_other else self.x
        at = (yy, xx) + (0,) * (v.ndim - 2)
        return lax.dynamic_slice(v, at, (1, 1) + v.shape[2:]).reshape(v.shape[2:])

    def corner(self):
        return self.cell(True, True)

    def side(self):
        return self.cell(not self.x_first, self.x_first)

    def far(self):
        return lax.dynamic_index_in_dim(
            self.whole, 1 - (self.x if self.x_first else self.y), 1 if self.x_first else 0, keepdims=False
        )

    def swap_first(self, v):
        return swap_dp(v, self.links[0])

    def relay(self, got, alone=False):
        other = 1 - (self.y if self.x_first else self.x)
        return add_low(self.cell(self.x_first, not self.x_first), got if alone else pick(got, other))

    def swap_second(self, v):
        return swap_dp(v, self.links[1])

    def total(self, got, relay, alone=False):
        here = self.y if self.x_first else self.x
        return add3(self.cell(False, False), got if alone else pick(got, here), relay)


def total3(a, b, d):
    return a.astype(jnp.float32) + b.astype(jnp.float32) + d.astype(jnp.float32)


COLS = (0, 640, 1024)


def heads_kernel(q_ref, k_ref, v_ref, o_ref, small_ref, out_ref):
    share, width = o_ref.shape
    heads_width = width // 4
    out_ref[...] = jnp.zeros_like(out_ref)
    for z in range(4):
        out_ref[z, :, :width] = o_ref[...]
        for (a, b), at in zip(GROUPS, COLS):
            size = (b - a) * HD
            cols = [ref[:, z * heads_width + a * HD : z * heads_width + b * HD] for ref in (q_ref, k_ref, v_ref)]
            out_ref[z, :, width + at : width + at + 3 * size] = jnp.concatenate(cols, 1)
        out_ref[z, : small_ref.shape[0], out_ref.shape[2] - small_ref.shape[1] :] = small_ref[...]


def prepare_heads(query, key, value, output, small, half):
    share = output.shape[0]
    vmem = pl.BlockSpec(memory_space=pltpu.VMEM)
    return pl.pallas_call(
        heads_kernel,
        out_shape=jax.ShapeDtypeStruct((4, share, half), jnp.bfloat16),
        in_specs=[vmem] * 5,
        out_specs=vmem,
        compiler_params=pltpu.CompilerParams(vmem_limit_bytes=60 << 20),
        cost_estimate=pl.CostEstimate(flops=0, bytes_accessed=2 << 20, transcendentals=0),
        name="prepare_heads",
    )(query, key, value, output, small)


def prepare_kernel(core_ref, up_ref, gate_ref, down_ref, own_ref, other_ref, dw_ref):
    width = down_ref.shape[2]
    step = up_ref.shape[1] // 8
    for kind, ref in enumerate((up_ref, gate_ref)):
        for core in range(2):

            @pl.when(core_ref[0] == core)
            def _():
                for at in range(4):
                    here = pl.ds(at * step, step)
                    own_ref[kind, :, here] = ref[:, (2 * at + core) * step : (2 * at + core + 1) * step]
                    other_ref[kind, :, here] = ref[:, (2 * at + 1 - core) * step : (2 * at + 2 - core) * step]
    for part in range(2):
        for side in range(2):
            dw_ref[part, :, side * width : (side + 1) * width] = down_ref[2 * part + side]


def prepare(c, up, gate, down):
    share, wide = up.shape
    vmem = pl.BlockSpec(memory_space=pltpu.VMEM)
    planes = jax.ShapeDtypeStruct((2, share, wide // 2), jnp.bfloat16)
    return pl.pallas_call(
        prepare_kernel,
        out_shape=(planes,) * 3,
        in_specs=[pl.BlockSpec(memory_space=pltpu.SMEM)] + [vmem] * 3,
        out_specs=(vmem,) * 3,
        compiler_params=pltpu.CompilerParams(vmem_limit_bytes=60 << 20),
        cost_estimate=pl.CostEstimate(flops=0, bytes_accessed=4 << 20, transcendentals=0),
        name="prepare",
    )(c.astype(jnp.int32).reshape(1), up, gate, down)


def run_copies(copies):
    copies = [pltpu.make_async_copy(*copy) for copy in copies]
    for copy in copies:
        copy.start()
    for copy in copies:
        copy.wait()


def join(upper, lower):
    rows, width = upper.shape

    def kernel(upper_ref, lower_ref, out_ref, sems):
        run_copies(
            [
                (upper_ref, out_ref.at[pl.ds(0, rows)], sems.at[0]),
                (lower_ref, out_ref.at[pl.ds(rows, rows)], sems.at[1]),
            ]
        )

    return pl.pallas_call(
        kernel,
        out_shape=jax.ShapeDtypeStruct((2 * rows, width), upper.dtype),
        in_specs=[pl.BlockSpec(memory_space=pltpu.HBM)] * 2,
        out_specs=pl.BlockSpec(memory_space=pltpu.VMEM),
        scratch_shapes=[pltpu.SemaphoreType.DMA((2,))],
        compiler_params=pltpu.CompilerParams(vmem_limit_bytes=60 << 20),
        cost_estimate=pl.CostEstimate(flops=0, bytes_accessed=6 << 20, transcendentals=0),
        name="join",
    )(upper, lower)


def place(sources, plan, coords, cuts):
    count, rows = len(sources), sources[0].shape[1]

    def kernel(coord_ref, *refs):
        outs, sems = refs[count:-1], refs[-1]
        copies = []
        for at, (key, array, plane, inner) in enumerate(plan):
            where = tuple(jnp.bitwise_xor(coord_ref[d], key[d]) for d in range(3)) + (inner,)
            for out, (out_ref, (size, start, length)) in enumerate(zip(outs, cuts)):
                copies.append((refs[array].at[plane, :, pl.ds(start, length)], out_ref.at[where], sems.at[at, out]))
        run_copies(copies)

    return pl.pallas_call(
        kernel,
        out_shape=[jax.ShapeDtypeStruct((2, 2, 2, 4, rows, size), jnp.bfloat16) for size, _, _ in cuts],
        in_specs=[pl.BlockSpec(memory_space=pltpu.SMEM)] + [pl.BlockSpec(memory_space=pltpu.HBM)] * count,
        out_specs=[pl.BlockSpec(memory_space=pltpu.VMEM)] * len(cuts),
        scratch_shapes=[pltpu.SemaphoreType.DMA((len(plan), len(cuts)))],
        compiler_params=pltpu.CompilerParams(vmem_limit_bytes=60 << 20),
        cost_estimate=pl.CostEstimate(flops=0, bytes_accessed=14 << 20, transcendentals=0),
        name="place",
    )(coords, *sources)


def spread(sources, plan, coords, width):
    count, share, half = len(sources), sources[0].shape[1], sources[0].shape[2]

    def kernel(coord_ref, *refs):
        up_ref, gate_ref, down_ref, sems = refs[count:]
        copies = []
        for at, (key, array, plane, core) in enumerate(plan):
            yy, xx, zz = (jnp.bitwise_xor(coord_ref[d], key[d]) for d in range(3))
            for kind, out_ref in enumerate((up_ref, gate_ref)):
                copies.append((refs[array].at[plane + kind], out_ref.at[yy, xx, core, zz], sems.at[at, kind]))
            for side in range(2):
                lanes = pl.ds(side * width, width)
                copies.append((refs[array].at[plane + 2, :, lanes], down_ref.at[yy, xx, zz, core, side], sems.at[at, 2 + side]))
        run_copies(copies)

    up, gate, down = pl.pallas_call(
        kernel,
        out_shape=[
            jax.ShapeDtypeStruct((2, 2, 2, 4, share, half), jnp.bfloat16),
            jax.ShapeDtypeStruct((2, 2, 2, 4, share, half), jnp.bfloat16),
            jax.ShapeDtypeStruct((2, 2, 4, 2, 2, share, width), jnp.bfloat16),
        ],
        in_specs=[pl.BlockSpec(memory_space=pltpu.SMEM)] + [pl.BlockSpec(memory_space=pltpu.HBM)] * count,
        out_specs=[pl.BlockSpec(memory_space=pltpu.VMEM)] * 3,
        scratch_shapes=[pltpu.SemaphoreType.DMA((len(plan), 4))],
        compiler_params=pltpu.CompilerParams(vmem_limit_bytes=60 << 20),
        cost_estimate=pl.CostEstimate(flops=0, bytes_accessed=40 << 20, transcendentals=0),
        name="spread",
    )(coords, *sources)
    return up.reshape(32 * share, half), gate.reshape(32 * share, half), down.reshape(64 * share, width)


def on_cores(
    inputs,
    teacher,
    lengths,
    query_weight,
    key_weight,
    value_projection,
    output_weight,
    score_gain,
    attention_step,
    up_weight,
    gate_weight,
    down_weight,
    up_scale,
    gate_scale,
    swiglu_step,
):
    local, width = inputs.shape[1:]
    share = query_weight.shape[0]
    hidden_share = down_weight.shape[0]
    heads_width = width // 4
    three = COLS[-1]
    hidden_half = up_weight.shape[1] // 2
    tokens = local * 4
    low = jnp.bfloat16
    f32 = jnp.float32
    dp, z = lax.axis_index("dp"), lax.axis_index("ctx")
    c, x, y = dp % 2, dp // 2 % 2, dp // 4
    chip = jnp.stack([y, x, z]).astype(jnp.int32)
    line = z.astype(jnp.int32).reshape(1)
    states = inputs.reshape(local, width)

    length_parts = jnp.stack([lengths[0] // 64, lengths[0] % 64]).astype(low)
    small = jnp.concatenate([score_gain, attention_step, up_scale, gate_scale, swiglu_step, length_parts])
    cuts = [0]
    for size in (share, share, hidden_share, hidden_share, share, 2):
        cuts.append(cuts[-1] + size)
    small = jnp.pad(small, (0, 512 - small.shape[0])).reshape(2, 256)
    half = up_weight.shape[1] // 2
    ug_own, ug_other, dw = prepare(c, up_weight, gate_weight, down_weight.reshape(4, share, width))
    q0 = prepare_heads(query_weight, key_weight, value_projection, output_weight, small, half)

    def on_x(*v):
        return swap_dp(jnp.concatenate(v) if len(v) > 1 else v[0], XAX)

    def on_y(*v):
        return swap_dp(jnp.concatenate(v) if len(v) > 1 else v[0], YAX)

    def exchange(blocks):
        return lax.all_to_all(blocks, "ctx", 0, 0, tiled=True)

    ug_sib = swap_dp(ug_other, CORE)
    ug_sib, ug_own = fence(ug_sib, ug_own)
    f0 = jnp.concatenate([by_core(c, ug_own, ug_sib), dw[:, None]], 1).reshape(6, share, half)
    q0 = exchange(q0)
    f0x, f0y, f1 = on_x(f0), on_y(f0), swap_z(f0, 1)
    f0, f0x, f0y, f1, q0, states = fence(f0, f0x, f0y, f1, q0, states)
    xb, yb = on_x(f1, f0y[:3], q0), on_y(f1, f0x[3:], q0)
    s1, s2 = swap_z(states, 1), swap_z(states, 2)
    xb, yb, s1, s2, f0 = fence(xb, yb, s1, s2, f0)
    f2, s3 = swap_z(f0, 2), swap_z(s2, 1)
    xc, yc = on_x(yb[:3], yb[9:11]), on_y(xb[3:6], xb[11:])
    qc = swap_dp(jnp.concatenate([q0, xb[9:], yb[9:]]), CORE)
    f2, s3, xc, yc, qc = fence(f2, s3, xc, yc, qc)
    f2x, f2y, f3 = on_x(f2), on_y(f2), swap_z(f2, 1)
    qd = swap_dp(jnp.concatenate([xc[3:], yc[3:]]), CORE)
    sources = [q0, xb, yb, xc, yc, qc, qd]
    plan = []
    for mc, (own, own_at, on_x_, x_at, on_y_, y_at, cross0, at0, cross1, at1) in enumerate(
        ((0, 0, 1, 9, 2, 9, 3, 3, 4, 3), (5, 0, 5, 4, 5, 8, 6, 0, 6, 2))
    ):
        for zz in range(4):
            plan.append(((0, 0, mc), own, own_at + zz, zz))
            plan.append(((0, 1, mc), on_x_, x_at + zz, zz))
            plan.append(((1, 0, mc), on_y_, y_at + zz, zz))
            if zz < 2:
                plan.append(((1, 1, mc), cross0, at0 + zz, zz))
            else:
                plan.append(((1, 1, mc), cross1, at1 + zz - 2, zz))
    full_output, full_qkv, vectors = place(
        sources, plan, jnp.stack([y, x, c]).astype(jnp.int32),
        [(width, 0, width), (half - width - 256, width, half - width - 256), (256, half - 256, 256)],
    )
    vectors = vectors[:, :, :, :, :2].reshape(2, 2, 2, 4, 512)
    full_output = full_output.reshape(width, width)
    full_qkv = full_qkv.reshape(width, -1)
    full_gain, full_astep, full_uscale, full_gscale, full_mstep, full_lengths = (
        vectors[..., a:b].astype(f32) for a, b in zip(cuts[:-1], cuts[1:])
    )
    count = jnp.sum(full_lengths[:, :, :, 0] * jnp.array([64.0, 1.0], f32))
    astep = full_astep.reshape(width)
    mstep = full_mstep.reshape(width)
    scale_up = pick(full_uscale, c, 2).reshape(-1)
    scale_gate = pick(full_gscale, c, 2).reshape(-1)
    gain = pick(full_gain.reshape(4, 1, heads_width), z)
    (whole_states,) = assemble(
        {(0,): states, (1,): s1, (2,): s2, (3,): s3}, line, [(4, local, width)], lambda zz: [(zz, None)]
    )
    whole_states = whole_states.reshape(tokens, width)
    gains = [gain[:, a * HD : b * HD] for a, b in GROUPS]
    qkv0 = matmul(whole_states, full_qkv[:, : COLS[1]])
    qkv1 = matmul(whole_states, full_qkv[:, COLS[1] :])
    qkv0, qkv1, f2x, f2y, f3 = fence(qkv0, qkv1, f2x, f2y, f3)
    xd, yd = on_x(f3, f2y[:3]), on_y(f3, f2x[3:])
    mixed0, heads0, qa0, ka0, va0 = attend(qkv0, gains[0], lengths)
    heads0, xd, yd, qkv1 = fence(heads0, xd, yd, qkv1)
    parts0 = exchange(heads0.reshape(4, local, -1))
    xe, ye = on_x(yd[:3]), on_y(xd[3:6])
    mixed1, heads1, qa1, ka1, va1 = attend(qkv1, gains[1], lengths)
    heads1, xe, ye, parts0 = fence(heads1, xe, ye, parts0)
    parts1 = exchange(heads1.reshape(4, local, -1))
    sources = [f0, f0x, f0y, f1, xb, yb, xc, yc, f2, f2x, f2y, f3, xd, yd, xe, ye]
    plan = []
    for mz, (own, at_x, at_y, at_yx, at_xy) in enumerate(
        (
            ((0, 0), (1, 0), (2, 0), (4, 6), (5, 6)),
            ((3, 0), (4, 0), (5, 0), (6, 0), (7, 0)),
            ((8, 0), (9, 0), (10, 0), (12, 6), (13, 6)),
            ((11, 0), (12, 0), (13, 0), (14, 0), (15, 0)),
        )
    ):
        for core in range(2):
            for key, (array, plane) in (((0, 0), own), ((0, 1), at_x), ((1, 0), at_y)):
                plan.append((key + (mz,), array, plane + 3 * core, core))
            array, plane = (at_yx, at_xy)[core]
            plan.append(((1, 1, mz), array, plane, core))
    full_up, full_gate, full_down = spread(sources, plan, chip, width)
    full_up, full_gate, full_down, parts1 = fence(full_up, full_gate, full_down, parts1)
    mixed_low = jnp.concatenate([parts0, parts1], -1).transpose(1, 0, 2).reshape(local, width)
    branch = matmul(mixed_low, full_output)
    resid = states.astype(f32)
    branch_norm = normalize(branch)
    first = resid + astep * (branch_norm - resid)
    middle = normalize(first)
    middle_low = middle.astype(low)
    middle_both = join(middle_low, swap_dp(middle_low, CORE))
    upper = matmul(middle_both, full_up)
    gating = matmul(middle_both, full_gate)
    upper_scaled = upper * scale_up
    gate_arg = gating * scale_gate
    gate_act = jax.nn.silu(gate_arg)
    hidden = (upper_scaled * gate_act).astype(low)
    lower = matmul(hidden, full_down)
    lower = lower[:local] + swap_dp(lower[local:].astype(low), CORE).astype(f32)
    lower_norm = normalize(lower)
    second = middle + mstep * (lower_norm - middle)
    final = normalize(second)

    query_pos = z * local + jnp.arange(local, dtype=jnp.int32)
    valid = (query_pos < lengths[0]).astype(f32).reshape(local, 1)
    diff = final - teacher.reshape(local, width).astype(f32)
    err_local = jnp.sum(valid * diff * diff)
    cot = loss_scale * 2.0 / count * valid * diff

    d_second = norm_back(second, final, cot)
    d_middle = d_second * (1.0 - mstep)
    grad_mstep = jnp.sum(d_second * (lower_norm - middle), axis=0)
    d_lower = norm_back(lower, lower_norm, d_second * mstep).astype(low)
    d_lower_both = join(d_lower, swap_dp(d_lower, CORE))
    g_down = left_tdot(hidden, d_lower_both).astype(low).reshape(2, 2, 4, 2, hidden_share // 2, width)
    downs = [Plane(g_down[:, :, :, part], y, x, part == 0) for part in range(2)]
    sends = [p.far() for p in downs]
    sends, d_lower_both = fence(sends, d_lower_both)
    down_far = [p.swap_first(v) for p, v in zip(downs, sends)]
    d_hidden = right_tdot(d_lower_both, full_down)
    d_upper = d_hidden * gate_act
    sigmoid_gate = jax.nn.sigmoid(gate_arg)
    d_gate_arg = d_hidden * upper_scaled * (sigmoid_gate * (1.0 + gate_arg * (1.0 - sigmoid_gate)))
    grad_uscale = jnp.sum(d_upper * upper, axis=0)
    grad_gscale = jnp.sum(d_gate_arg * gating, axis=0)
    d_up, d_gate = (d_upper * scale_up).astype(low), (d_gate_arg * scale_gate).astype(low)
    d_up, d_gate, down_far = fence(d_up, d_gate, down_far)
    down_relay = [p.swap_second(p.relay(v)) for p, v in zip(downs, down_far)]
    ups = left_tdot(middle_both, d_up).astype(low).reshape(2, 2, 2, 4, share, hidden_half)
    ups = [Plane(ups[:, :, core], y, x, core == 0) for core in range(2)]
    corners, up_sides = [p.corner() for p in ups], [p.side() for p in ups]
    corners, up_sides, down_relay, d_up, d_gate = fence(corners, up_sides, down_relay, d_up, d_gate)
    up_corner = [p.swap_first(v) for p, v in zip(ups, corners)]
    d_both = right_tdot(d_up, full_up) + right_tdot(d_gate, full_gate)
    up_corner, d_both, d_gate, up_sides = fence(up_corner, d_both, d_gate, up_sides)
    up_side = [p.swap_first(v) for p, v in zip(ups, up_sides)]
    d_middle = d_middle + d_both[:local] + swap_dp(d_both[local:].astype(low), CORE).astype(f32)
    d_first = norm_back(first, middle, d_middle)
    input_grad = d_first * (1.0 - astep)
    grad_astep = jnp.sum(d_first * (branch_norm - resid), axis=0)
    d_branch = norm_back(branch, branch_norm, d_first * astep).astype(low)
    d_mixed = right_tdot(d_branch, full_output).astype(low)
    blocks = d_mixed.reshape(local, 4, heads_width).transpose(1, 0, 2)
    blocks = [blocks[:, :, a * HD : b * HD] for a, b in GROUPS]
    scales = jnp.concatenate([grad_uscale.reshape(2, 2, 4, hidden_share), grad_gscale.reshape(2, 2, 4, hidden_share)], -1)
    scales = jnp.where((jnp.arange(2) == c)[None, None, :, None, None], scales[:, :, None], 0.0).reshape(32, -1)
    packed = jnp.concatenate(
        [grad_astep.reshape(32, share), scales, grad_mstep.reshape(32, share), jnp.full((32, 1), err_local)], 1
    )
    packed = jnp.pad(packed, ((0, 0), (0, 512 - packed.shape[1]))).reshape(2, 2, 2, 4, 4, 128)
    packed = pick(packed, c, 2) + swap_dp(pick(packed, 1 - c, 2), CORE)
    down = jnp.stack([p.total(v, r) for p, v, r in zip(downs, down_far, down_relay)], 1)
    down_far = swap_z(pick(down, z ^ 3), 1)
    blocks, d_branch, up_side, d_gate, up_corner, packed, down, down_far = fence(
        blocks, d_branch, up_side, d_gate, up_corner, packed, down, down_far
    )
    parts0 = exchange(blocks[0])
    up_relay = [p.swap_second(p.relay(v, True)) for p, v in zip(ups, up_corner)]
    gates = left_tdot(middle_both, d_gate).astype(low).reshape(2, 2, 2, 4, share, hidden_half)
    gates = [Plane(gates[:, :, core], y, x, core == 0) for core in range(2)]
    corners, gate_sides = [p.corner() for p in gates], [p.side() for p in gates]
    packed = pick(packed, x, 1) + swap_dp(pick(packed, 1 - x, 1), XAX)
    up_relay, corners, gate_sides, block1, d_branch, packed = fence(
        up_relay, corners, gate_sides, blocks[1], d_branch, packed
    )
    gate_corner = [p.swap_first(v) for p, v in zip(gates, corners)]
    up = jnp.stack([p.total(v, r, True) for p, v, r in zip(ups, up_side, up_relay)])
    down_far, down_near = swap_z(add_low(pick(down, z ^ 2), down_far), 2), swap_z(pick(down, z ^ 1), 1)
    g_out = left_tdot(mixed_low, d_branch).astype(low).reshape(2, 2, 2, 2, 2 * share, width)
    out_c = swap_dp(pick(g_out, 1 - c, 2), CORE)
    g_out = add_low(pick(g_out, c, 2), out_c)
    parts0, gate_corner, up, g_out, gate_sides, down_far, down_near = fence(
        parts0, gate_corner, up, g_out, gate_sides, down_far, down_near
    )
    parts1 = exchange(block1)
    gate_side = [p.swap_first(v) for p, v in zip(gates, gate_sides)]
    gate_relay = [p.swap_second(p.relay(v, True)) for p, v in zip(gates, gate_corner)]
    up_far = swap_z(pick(up, z ^ 3, 1), 1)
    d_heads0 = parts0.reshape(tokens, -1)
    d_qkv0, gain_grad0 = attend_back(qkv0, gains[0], lengths, mixed0, d_heads0, qa0, ka0, va0)
    d_qkv0, gain_grad0, parts1, gate_side, gate_relay, up_far, up, packed = fence(
        d_qkv0, gain_grad0, parts1, gate_side, gate_relay, up_far, up, packed
    )
    gate = jnp.stack([p.total(v, r, True) for p, v, r in zip(gates, gate_side, gate_relay)])
    up_far, up_near = swap_z(add_low(pick(up, z ^ 2, 1), up_far), 2), swap_z(pick(up, z ^ 1, 1), 1)
    gate_far, gate_near = swap_z(pick(gate, z ^ 3, 1), 1), swap_z(pick(gate, z ^ 1, 1), 1)
    packed = pick(packed, y) + swap_dp(pick(packed, 1 - y), YAX)
    d_heads1 = parts1.reshape(tokens, -1)
    d_qkv1, gain_grad1 = attend_back(qkv1, gains[1], lengths, mixed1, d_heads1, qa1, ka1, va1)
    d_qkv1, gain_grad1, gate, up_far, up_near, gate_far, gate_near, d_qkv0, packed = fence(
        d_qkv1, gain_grad1, gate, up_far, up_near, gate_far, gate_near, d_qkv0, packed
    )
    d_qkv = jnp.concatenate([d_qkv0, d_qkv1], 1)
    d_states = right_tdot(d_qkv, full_qkv).astype(low).reshape(4, local, width)
    states_send = pick(d_states, z ^ 3)
    gate_send = add_low(pick(gate, z ^ 2, 1), gate_far)
    states_send, d_states, d_qkv, whole_states, gain_grad1, gate_send, gate, packed = fence(
        states_send, d_states, d_qkv, whole_states, gain_grad1, gate_send, gate, packed
    )
    cut = local // 2
    relay0 = swap_z(states_send[:cut], 1)
    gate_far = swap_z(gate_send, 2)
    pair = swap_z(jnp.stack([pick(packed, z ^ 2), pick(packed, z ^ 3)]), 2)
    packed = jnp.stack([pick(packed, z), pick(packed, z ^ 1)]) + pair
    grad_gain = jnp.concatenate([gain_grad0, gain_grad1], 1).reshape(-1)
    gain_all = lax.dynamic_update_slice(jnp.zeros((4 * heads_width,), f32), grad_gain, (z * heads_width,))
    spare = COLS[0] + 3 * (GROUPS[0][1] - GROUPS[0][0]) * HD
    g_qkv = left_tdot(whole_states, d_qkv)
    g_qkv = jnp.where(jnp.arange(three)[None] == spare, gain_all[:, None], g_qkv)
    g_qkv = g_qkv.astype(low).reshape(2, 2, 2, 2, 2 * share, three)
    qkv_c = swap_dp(pick(g_qkv, 1 - c, 2), CORE)
    relay0, qkv_c, g_qkv, d_states, states_send, packed, gate_far = fence(
        relay0, qkv_c, g_qkv, d_states, states_send, packed, gate_far
    )
    relay1 = swap_z(states_send[cut:], 1)
    far0 = swap_z(add_low(pick(d_states, z ^ 2)[:cut], relay0), 2)
    g_rows = jnp.concatenate([add_low(pick(g_qkv, c, 2), qkv_c), g_out], -1)
    rows = [Plane(g_rows[:, :, part], y, x, part == 0) for part in range(2)]
    row_far = [p.swap_first(p.far()) for p in rows]
    packed = packed[0] + swap_z(packed[1], 1)
    own_rows = total3(pick(up, z, 1), up_near, up_far), total3(pick(gate, z, 1), gate_near, gate_far)
    own_rows = jnp.stack(own_rows, 1)
    other = swap_dp(pick(own_rows, 1 - c), CORE)
    down_grad = total3(pick(down, z), down_near, down_far).reshape(hidden_share, width)
    relay1, far0, row_far, d_states, own_rows, other, packed, down_grad = fence(
        relay1, far0, row_far, d_states, own_rows, other, packed, down_grad
    )
    states_near = pick(d_states, z ^ 1)
    near0 = swap_z(states_near[:cut], 1)
    row_relay = [p.swap_second(p.relay(v)) for p, v in zip(rows, row_far)]
    states_send = add_low(pick(d_states, z ^ 2)[cut:], relay1)
    wide_grad = by_core(c, pick(own_rows, c).reshape(2, share, 4, -1), other.reshape(2, share, 4, -1), 3)
    up_grad = wide_grad[0].reshape(up_weight.shape)
    gate_grad = wide_grad[1].reshape(up_weight.shape)
    near0, row_relay, states_send, states_near, up_grad, gate_grad = fence(
        near0, row_relay, states_send, states_near, up_grad, gate_grad
    )
    rows_sum = jnp.stack([p.total(v, r) for p, v, r in zip(rows, row_far, row_relay)]).reshape(4, share, three + width)
    columns = exchange(rows_sum)
    far1, near1 = swap_z(states_send, 2), swap_z(states_near[cut:], 1)
    packed = packed.reshape(512)
    output_grad = jnp.sum(columns[..., three:].astype(f32), 0)
    columns_cut = [
        columns[..., at : at + 3 * (b - a) * HD].reshape(4, share, 3, -1) for (a, b), at in zip(GROUPS, COLS)
    ]
    score_gain_grad = jnp.sum(columns[..., spare].astype(f32), 0)
    columns = jnp.concatenate(columns_cut, -1).transpose(2, 1, 0, 3).reshape(3, share, width).astype(f32)
    columns, output_grad, score_gain_grad, input_grad, far1, near1 = fence(
        columns, output_grad, score_gain_grad, input_grad, far1, near1
    )
    own = pick(d_states, z)
    states_sum = [total3(own[:cut], near0, far0), total3(own[cut:], near1, far1)]
    input_grad = input_grad + jnp.concatenate(states_sum)
    return (
        final.astype(low)[None],
        packed[cuts[5] - cuts[1]] / count,
        input_grad[None],
        columns[0],
        columns[1],
        columns[2],
        output_grad,
        score_gain_grad,
        packed[: cuts[1]],
        up_grad,
        gate_grad,
        down_grad,
        packed[cuts[2] - cuts[1] : cuts[3] - cuts[1]],
        packed[cuts[3] - cuts[1] : cuts[4] - cuts[1]],
        packed[cuts[4] - cuts[1] : cuts[5] - cuts[1]],
    )


def per_device(
    inputs,
    teacher,
    lengths,
    query_weight,
    key_weight,
    value_projection,
    output_weight,
    score_gain,
    attention_step,
    up_weight,
    gate_weight,
    down_weight,
    up_scale,
    gate_scale,
    swiglu_step,
):
    seqs, local, width = inputs.shape
    full_len = local * lax.axis_size("ctx")
    rows = seqs * local
    heads = width // HD
    key_block = min(512, full_len)
    query_pos = lax.axis_index("ctx") * local + jnp.arange(local, dtype=jnp.int32)
    valid = (query_pos[None, :] < lengths[:, None]).astype(jnp.float32).reshape(rows, 1)
    count_local = jnp.sum(valid)
    full_query, full_key, full_value, full_output, full_gain, full_astep = (
        lax.all_gather(query_weight, ("dp", "ctx"), axis=0, tiled=True),
        lax.all_gather(key_weight, ("dp", "ctx"), axis=0, tiled=True),
        lax.all_gather(value_projection, ("dp", "ctx"), axis=0, tiled=True),
        lax.all_gather(output_weight, ("dp", "ctx"), axis=0, tiled=True),
        lax.all_gather(score_gain, ("dp", "ctx"), axis=0, tiled=True),
        lax.all_gather(attention_step, ("dp", "ctx"), axis=0, tiled=True),
    )
    states = inputs.reshape(rows, width)
    resid = states.astype(jnp.float32)
    queries = matmul(states, full_query)
    keys_raw = matmul(states, full_key)
    values_raw = matmul(states, full_value)
    gains = full_gain.astype(jnp.float32).reshape(heads, HD)
    query_norm = normalize(queries.reshape(rows, heads, HD))
    key_norm = normalize(keys_raw.reshape(rows, heads, HD))
    q_heads = (gains * query_norm).astype(jnp.bfloat16).reshape(seqs, local, heads, HD)
    k_flat = (gains * key_norm).astype(jnp.bfloat16).reshape(seqs, local, width)
    v_flat = values_raw.astype(jnp.bfloat16).reshape(seqs, local, width)

    def key_step(carry, key_piece, value_piece, key_pos):
        top, total, accum = carry
        count_keys = key_piece.shape[1]
        scores, allowed = block_scores(
            q_heads, key_piece.reshape(seqs, count_keys, heads, HD), query_pos, key_pos, lengths
        )
        scores = jnp.where(allowed, scores, -1e30)
        top_new = jnp.maximum(top, jnp.max(scores, axis=-1))
        weights = jnp.where(allowed, jnp.exp(scores - top_new[..., None]), 0.0)
        factor = jnp.exp(top - top_new)
        total = total * factor + jnp.sum(weights, axis=-1)
        accum = accum * jnp.transpose(factor, (0, 2, 1))[..., None] + jnp.einsum(
            "shqk,skhd->sqhd",
            weights.astype(jnp.bfloat16),
            value_piece.reshape(seqs, count_keys, heads, HD),
            preferred_element_type=jnp.float32,
        )
        return (top_new, total, accum)

    init = (
        jnp.full((seqs, heads, local), -1e30, jnp.float32),
        jnp.zeros((seqs, heads, local), jnp.float32),
        jnp.zeros((seqs, local, heads, HD), jnp.float32),
    )
    carry = init
    key_piece = lax.all_gather(k_flat, "ctx", axis=1, tiled=True)
    value_piece = lax.all_gather(v_flat, "ctx", axis=1, tiled=True)
    count_keys = key_piece.shape[1]

    def inner(state, index):
        offset = index * key_block
        key_part = lax.dynamic_slice_in_dim(key_piece, offset, key_block, 1)
        value_part = lax.dynamic_slice_in_dim(value_piece, offset, key_block, 1)
        positions = offset + jnp.arange(key_block, dtype=jnp.int32)
        return (key_step(state, key_part, value_part, positions), None)

    carry, unused = lax.scan(inner, carry, jnp.arange(count_keys // key_block, dtype=jnp.int32))
    top, total, accum = carry
    mixed = accum / jnp.transpose(total, (0, 2, 1))[..., None]
    log_total = top + jnp.log(total)
    mixed_low = mixed.reshape(rows, width).astype(jnp.bfloat16)
    branch = matmul(mixed_low, full_output)
    branch_norm = normalize(branch)
    astep = full_astep.astype(jnp.float32)
    first = resid + astep * (branch_norm - resid)
    middle = normalize(first)
    middle_low = middle.astype(jnp.bfloat16)
    full_up, full_gate, full_down, full_uscale, complete_gate_scale, full_mstep = (
        lax.all_gather(up_weight, ("dp", "ctx"), axis=0, tiled=True),
        lax.all_gather(gate_weight, ("dp", "ctx"), axis=0, tiled=True),
        lax.all_gather(down_weight, ("dp", "ctx"), axis=0, tiled=True),
        lax.all_gather(up_scale, ("dp", "ctx"), axis=0, tiled=True),
        lax.all_gather(gate_scale, ("dp", "ctx"), axis=0, tiled=True),
        lax.all_gather(swiglu_step, ("dp", "ctx"), axis=0, tiled=True),
    )
    upper = matmul(middle_low, full_up)
    gating = matmul(middle_low, full_gate)
    scale_up = full_uscale.astype(jnp.float32)
    scale_gate = complete_gate_scale.astype(jnp.float32)
    upper_scaled = upper * scale_up
    gate_arg = gating * scale_gate
    gate_act = jax.nn.silu(gate_arg)
    hidden = (upper_scaled * gate_act).astype(jnp.bfloat16)
    lower = matmul(hidden, full_down)
    lower_norm = normalize(lower)
    mstep = full_mstep.astype(jnp.float32)
    second = middle + mstep * (lower_norm - middle)
    final = normalize(second)
    target = teacher.reshape(rows, width).astype(jnp.float32)
    diff = final - target
    err_local = jnp.sum(valid * diff * diff)
    err_total, count = lax.psum((err_local, count_local), ("dp", "ctx"))
    cot = loss_scale * 2.0 / count * valid * diff
    full_up, full_gate, full_down, full_uscale, complete_gate_scale, full_mstep = (
        lax.all_gather(up_weight, ("dp", "ctx"), axis=0, tiled=True),
        lax.all_gather(gate_weight, ("dp", "ctx"), axis=0, tiled=True),
        lax.all_gather(down_weight, ("dp", "ctx"), axis=0, tiled=True),
        lax.all_gather(up_scale, ("dp", "ctx"), axis=0, tiled=True),
        lax.all_gather(gate_scale, ("dp", "ctx"), axis=0, tiled=True),
        lax.all_gather(swiglu_step, ("dp", "ctx"), axis=0, tiled=True),
    )
    d_second = norm_back(second, final, cot)
    d_middle = d_second * (1.0 - mstep)
    grad_mstep = jnp.sum(d_second * (lower_norm - middle), axis=0)
    d_lower = norm_back(lower, lower_norm, d_second * mstep).astype(jnp.bfloat16)
    grad_down = left_tdot(hidden, d_lower)
    d_hidden = right_tdot(d_lower, full_down)
    d_upper = d_hidden * gate_act
    sigmoid_gate = jax.nn.sigmoid(gate_arg)
    d_gate_arg = d_hidden * upper_scaled * (sigmoid_gate * (1.0 + gate_arg * (1.0 - sigmoid_gate)))
    grad_uscale = jnp.sum(d_upper * upper, axis=0)
    grad_gscale = jnp.sum(d_gate_arg * gating, axis=0)
    d_up_low = (d_upper * scale_up).astype(jnp.bfloat16)
    d_gate_low = (d_gate_arg * scale_gate).astype(jnp.bfloat16)
    d_middle = d_middle + right_tdot(d_up_low, full_up) + right_tdot(d_gate_low, full_gate)
    grad_up = left_tdot(middle_low, d_up_low)
    grad_gate = left_tdot(middle_low, d_gate_low)
    up_grad, gate_grad, down_grad, up_scale_grad, gate_scale_gradient, swiglu_step_grad = (
        lax.psum_scatter(grad_up, ("dp", "ctx"), scatter_dimension=0, tiled=True),
        lax.psum_scatter(grad_gate, ("dp", "ctx"), scatter_dimension=0, tiled=True),
        lax.psum_scatter(grad_down, ("dp", "ctx"), scatter_dimension=0, tiled=True),
        lax.psum_scatter(grad_uscale, ("dp", "ctx"), scatter_dimension=0, tiled=True),
        lax.psum_scatter(grad_gscale, ("dp", "ctx"), scatter_dimension=0, tiled=True),
        lax.psum_scatter(grad_mstep, ("dp", "ctx"), scatter_dimension=0, tiled=True),
    )
    d_first = norm_back(first, middle, d_middle)
    input_grad = d_first * (1.0 - astep)
    grad_astep = jnp.sum(d_first * (branch_norm - resid), axis=0)
    d_branch = norm_back(branch, branch_norm, d_first * astep).astype(jnp.bfloat16)
    full_query, full_key, full_value, full_output, full_gain, full_astep = (
        lax.all_gather(query_weight, ("dp", "ctx"), axis=0, tiled=True),
        lax.all_gather(key_weight, ("dp", "ctx"), axis=0, tiled=True),
        lax.all_gather(value_projection, ("dp", "ctx"), axis=0, tiled=True),
        lax.all_gather(output_weight, ("dp", "ctx"), axis=0, tiled=True),
        lax.all_gather(score_gain, ("dp", "ctx"), axis=0, tiled=True),
        lax.all_gather(attention_step, ("dp", "ctx"), axis=0, tiled=True),
    )
    gains = full_gain.astype(jnp.float32).reshape(heads, HD)
    grad_output = left_tdot(mixed_low, d_branch)
    d_mixed = right_tdot(d_branch, full_output).astype(jnp.bfloat16)
    d_mixed_heads = d_mixed.reshape(seqs, local, heads, HD)
    delta = jnp.transpose(jnp.sum(d_mixed_heads.astype(jnp.float32) * mixed, axis=-1), (0, 2, 1))
    whole_keys, whole_values = (
        lax.all_gather(k_flat, "ctx", axis=1, tiled=True),
        lax.all_gather(v_flat, "ctx", axis=1, tiled=True),
    )

    def query_terms(index):
        offset = index * key_block
        key_part = lax.dynamic_slice_in_dim(whole_keys, offset, key_block, 1).reshape(
            seqs, key_block, heads, HD
        )
        value_part = lax.dynamic_slice_in_dim(whole_values, offset, key_block, 1).reshape(
            seqs, key_block, heads, HD
        )
        key_pos = offset + jnp.arange(key_block, dtype=jnp.int32)
        scores, allowed = block_scores(q_heads, key_part, query_pos, key_pos, lengths)
        probs = jnp.where(allowed, jnp.exp(scores - log_total[..., None]), 0.0)
        d_probs = jnp.einsum(
            "sqhd,skhd->shqk", d_mixed_heads, value_part, preferred_element_type=jnp.float32
        )
        d_scores = (probs * (d_probs - delta[..., None])).astype(jnp.bfloat16)
        d_query_part = jnp.einsum(
            "shqk,skhd->sqhd", d_scores, key_part, preferred_element_type=jnp.float32
        )
        return (offset, probs, d_scores, d_query_part)

    def key_back(carry, index):
        d_query_acc, d_key_all, d_value_all = carry
        offset, probs, d_scores, d_query_part = query_terms(index)
        d_query_acc = d_query_acc + d_query_part
        d_key_part = jnp.einsum(
            "shqk,sqhd->skhd", d_scores, q_heads, preferred_element_type=jnp.float32
        ) * HD ** (-0.5)
        d_value_part = jnp.einsum(
            "shqk,sqhd->skhd",
            probs.astype(jnp.bfloat16),
            d_mixed_heads,
            preferred_element_type=jnp.float32,
        )
        d_key_all = lax.dynamic_update_slice_in_dim(
            d_key_all, d_key_part.reshape(seqs, key_block, width), offset, 1
        )
        d_value_all = lax.dynamic_update_slice_in_dim(
            d_value_all, d_value_part.reshape(seqs, key_block, width), offset, 1
        )
        return ((d_query_acc, d_key_all, d_value_all), None)

    start_carry = (
        jnp.zeros((seqs, local, heads, HD), jnp.float32),
        jnp.zeros((seqs, full_len, width), jnp.float32),
        jnp.zeros((seqs, full_len, width), jnp.float32),
    )
    (d_query_heads, d_key_all, d_value_all), unused = lax.scan(
        key_back, start_carry, jnp.arange(full_len // key_block, dtype=jnp.int32)
    )
    d_key_local, d_value_local = (
        lax.psum_scatter(
            d_key_all.astype(jnp.bfloat16), "ctx", scatter_dimension=1, tiled=True
        ).astype(jnp.float32),
        lax.psum_scatter(
            d_value_all.astype(jnp.bfloat16), "ctx", scatter_dimension=1, tiled=True
        ).astype(jnp.float32),
    )
    d_key_heads = d_key_local.reshape(rows, heads, HD)
    d_value_local = d_value_local.reshape(rows, width)
    d_query_heads = (d_query_heads * HD ** (-0.5)).reshape(rows, heads, HD)
    grad_gain = jnp.sum(d_query_heads * query_norm, axis=0) + jnp.sum(
        d_key_heads * key_norm, axis=0
    )
    d_query_low = (
        norm_back(queries.reshape(rows, heads, HD), query_norm, d_query_heads * gains)
        .reshape(rows, width)
        .astype(jnp.bfloat16)
    )
    d_key_low = (
        norm_back(keys_raw.reshape(rows, heads, HD), key_norm, d_key_heads * gains)
        .reshape(rows, width)
        .astype(jnp.bfloat16)
    )
    d_value_low = d_value_local.astype(jnp.bfloat16)
    input_grad = (
        input_grad
        + right_tdot(d_query_low, full_query)
        + right_tdot(d_key_low, full_key)
        + right_tdot(d_value_low, full_value)
    )
    grad_query = left_tdot(states, d_query_low)
    grad_key = left_tdot(states, d_key_low)
    grad_value = left_tdot(states, d_value_low)
    query_grad, key_grad, value_grad, output_grad, score_gain_grad, attention_step_grad = (
        lax.psum_scatter(grad_query, ("dp", "ctx"), scatter_dimension=0, tiled=True),
        lax.psum_scatter(grad_key, ("dp", "ctx"), scatter_dimension=0, tiled=True),
        lax.psum_scatter(grad_value, ("dp", "ctx"), scatter_dimension=0, tiled=True),
        lax.psum_scatter(grad_output, ("dp", "ctx"), scatter_dimension=0, tiled=True),
        lax.psum_scatter(grad_gain.reshape(width), ("dp", "ctx"), scatter_dimension=0, tiled=True),
        lax.psum_scatter(grad_astep, ("dp", "ctx"), scatter_dimension=0, tiled=True),
    )
    distill_loss_mean = err_total / count
    layer_out = final.astype(jnp.bfloat16).reshape(seqs, local, width)
    return (
        layer_out,
        distill_loss_mean,
        input_grad.reshape(seqs, local, width),
        query_grad,
        key_grad,
        value_grad,
        output_grad,
        score_gain_grad,
        attention_step_grad,
        up_grad,
        gate_grad,
        down_grad,
        up_scale_grad,
        gate_scale_gradient,
        swiglu_step_grad,
    )


def solution(mesh):
    placed = (
        P("dp", "ctx", None),
        P("dp", "ctx", None),
        P("dp"),
        P(("dp", "ctx"), None),
        P(("dp", "ctx"), None),
        P(("dp", "ctx"), None),
        P(("dp", "ctx"), None),
        P(("dp", "ctx")),
        P(("dp", "ctx")),
        P(("dp", "ctx"), None),
        P(("dp", "ctx"), None),
        P(("dp", "ctx"), None),
        P(("dp", "ctx")),
        P(("dp", "ctx")),
        P(("dp", "ctx")),
    )
    on_one = on_cores if dict(mesh.shape) == {"dp": 8, "ctx": 4} else per_device
    return jax.shard_map(
        on_one,
        mesh=mesh,
        in_specs=placed,
        out_specs=(
            P("dp", "ctx", None),
            P(),
            P("dp", "ctx", None),
            P(("dp", "ctx"), None),
            P(("dp", "ctx"), None),
            P(("dp", "ctx"), None),
            P(("dp", "ctx"), None),
            P(("dp", "ctx")),
            P(("dp", "ctx")),
            P(("dp", "ctx"), None),
            P(("dp", "ctx"), None),
            P(("dp", "ctx"), None),
            P(("dp", "ctx")),
            P(("dp", "ctx")),
            P(("dp", "ctx")),
        ),
        check_vma=False,
    )
```

```python
import functools

import jax
import jax.numpy as jnp
from jax import lax
from jax.experimental import pallas as pl
from jax.experimental.pallas import tpu as pltpu
from jax.sharding import PartitionSpec as P

HD = 64


eps = 1e-06
loss_scale = 32768.0


def normalize(value_rows):
    return value_rows * lax.rsqrt(jnp.mean(value_rows * value_rows, axis=-1, keepdims=True) + eps)


def norm_back(value_rows, normed, grad):
    factor = lax.rsqrt(jnp.mean(value_rows * value_rows, axis=-1, keepdims=True) + eps)
    return factor * (grad - normed * jnp.mean(grad * normed, axis=-1, keepdims=True))


def matmul(left, right):
    return jnp.dot(left, right, preferred_element_type=jnp.float32)


def left_tdot(left, right):
    return lax.dot_general(
        left, right, (((0,), (0,)), ((), ())), preferred_element_type=jnp.float32
    )


def right_tdot(left, right):
    return lax.dot_general(
        left, right, (((1,), (1,)), ((), ())), preferred_element_type=jnp.float32
    )


def block_scores(queries, keys, query_pos, key_pos, lens):
    scores = jnp.einsum(
        "sqhd,skhd->shqk", queries, keys, preferred_element_type=jnp.float32
    ) * HD ** (-0.5)
    allowed = (key_pos[None, None, :] <= query_pos[None, :, None]) & (
        key_pos[None, None, :] < lens[:, None, None]
    )
    return (scores, allowed[:, None])


BLK = 512
LANES = 128


def same_head(size, value):
    rows = lax.broadcasted_iota(jnp.int32, (size, size), 0) // HD
    cols = lax.broadcasted_iota(jnp.int32, (size, size), 1) // HD
    return jnp.where(rows == cols, value, 0.0).astype(jnp.bfloat16)


def over_heads(v, matrix):
    hi = v.astype(jnp.bfloat16)
    low = (v - hi.astype(jnp.float32)).astype(jnp.bfloat16)
    return jnp.dot(hi, matrix, preferred_element_type=jnp.float32) + jnp.dot(low, matrix, preferred_element_type=jnp.float32)


def split3(v):
    hi = v.astype(jnp.bfloat16)
    rest = v - hi.astype(jnp.float32)
    mid = rest.astype(jnp.bfloat16)
    low = (rest - mid.astype(jnp.float32)).astype(jnp.bfloat16)
    return hi, mid, low


def attend_kernel(heads, length_ref, qkv_ref, gain_ref, mixed_ref, low_ref, qa_ref, ka_ref, va_ref, out_ref):
    tokens = qkv_ref.shape[0]
    width = heads * HD
    length = length_ref[0]
    lane = lax.broadcasted_iota(jnp.int32, (BLK, HD), 1)

    mean = same_head(2 * width, 1.0 / HD)
    gains = jnp.concatenate([gain_ref[...], gain_ref[...]], axis=1)

    def prepare(block, carry):
        start = pl.multiple_of(block * BLK, BLK)
        rows = pl.ds(start, BLK)
        inside = (lax.broadcasted_iota(jnp.int32, (BLK, 1), 0) + start < length).astype(jnp.float32)
        ones = jnp.where(lane < 3, inside, 0.0).astype(jnp.bfloat16)
        nothing = jnp.zeros((BLK, HD), jnp.bfloat16)
        raw = qkv_ref[rows, : 2 * width]
        scaled = gains * (raw * lax.rsqrt(over_heads(raw * raw, mean) + eps))
        qs = scaled[:, :width].astype(jnp.bfloat16) * jnp.bfloat16(HD**-0.5)
        ks = (scaled[:, width:] * inside).astype(jnp.bfloat16)
        vs = (qkv_ref[rows, 2 * width : 3 * width] * inside).astype(jnp.bfloat16)
        for head in range(heads):
            cols = slice(head * HD, (head + 1) * HD)
            qa_ref[head, rows, :] = jnp.concatenate([qs[:, cols], nothing], axis=1)
            ka_ref[head, rows, :] = jnp.concatenate([ks[:, cols], ones], axis=1)
            va_ref[head, rows, :] = jnp.concatenate([vs[:, cols], ones], axis=1)
        return carry

    lax.fori_loop(0, tokens // BLK, prepare, 0)
    part = BLK // 2
    place = lax.broadcasted_iota(jnp.int32, (BLK, part), 0) - lax.broadcasted_iota(jnp.int32, (BLK, part), 1)

    def per_head(head, carry):
        for qi in range(tokens // BLK):
            rows = pl.ds(qi * BLK, BLK)
            q = qa_ref[head, rows, :]
            acc = jnp.zeros((BLK, LANES), jnp.float32)
            for ki in range(2 * (qi + 1)):
                keys = pl.ds(ki * part, part)
                scores = lax.dot_general(
                    q, ka_ref[head, keys, :], (((1,), (1,)), ((), ())), preferred_element_type=jnp.float32
                )
                weights = jnp.exp(scores)
                if ki >= 2 * qi:
                    weights = jnp.where(place >= (ki - 2 * qi) * part, weights, 0.0)
                acc = acc + jnp.dot(
                    weights.astype(jnp.bfloat16), va_ref[head, keys, :], preferred_element_type=jnp.float32
                )
            total = acc[:, HD : HD + 1]
            out_ref[head, rows, :] = acc / total
            hi, mid, low = split3(-jnp.log(total))
            extra = jnp.where(lane == 0, hi, jnp.where(lane == 1, mid, jnp.where(lane == 2, low, jnp.zeros_like(low))))
            qa_ref[head, rows, :] = jnp.concatenate([q[:, :HD], extra], axis=1)
        return carry

    lax.fori_loop(0, heads, per_head, 0)

    def finish(block, carry):
        rows = pl.ds(pl.multiple_of(block * BLK, BLK), BLK)
        whole = jnp.concatenate([out_ref[head, rows, :][:, :HD] for head in range(heads)], axis=1)
        mixed_ref[rows, :] = whole
        low_ref[rows, :] = whole.astype(jnp.bfloat16)
        return carry

    lax.fori_loop(0, tokens // BLK, finish, 0)


def attend(qkv, gain, length):
    tokens, width = qkv.shape[0], gain.shape[1]
    heads = width // HD
    vmem = pl.BlockSpec(memory_space=pltpu.VMEM)
    aug = jax.ShapeDtypeStruct((heads, tokens, LANES), jnp.bfloat16)
    return pl.pallas_call(
        functools.partial(attend_kernel, heads),
        out_shape=(
            jax.ShapeDtypeStruct((tokens, width), jnp.float32),
            jax.ShapeDtypeStruct((tokens, width), jnp.bfloat16),
            aug,
            aug,
            aug,
        ),
        in_specs=[pl.BlockSpec(memory_space=pltpu.SMEM), vmem, vmem],
        out_specs=(vmem,) * 5,
        scratch_shapes=[pltpu.VMEM((heads, tokens, LANES), jnp.float32)],
        compiler_params=pltpu.CompilerParams(vmem_limit_bytes=56 << 20),
        cost_estimate=pl.CostEstimate(
            flops=heads * tokens * tokens, bytes_accessed=8 << 20, transcendentals=0
        ),
        name="attend",
    )(length, qkv, gain)


def attend_back_kernel(
    heads, length_ref, qkv_ref, gain_ref, mixed_ref, cot_ref, qa_ref, ka_ref, va_ref,
    grads_ref, gain_grad_ref, doa_ref, dq_ref, dk_ref, dv_ref, raw_ref, sem,
):
    tokens = qkv_ref.shape[0]
    width = heads * HD
    length = length_ref[0]
    lane = lax.broadcasted_iota(jnp.int32, (BLK, HD), 1)
    raw_copy = pltpu.make_async_copy(qkv_ref.at[:, pl.ds(0, 2 * width)], raw_ref, sem)
    raw_copy.start()
    minus = same_head(width, -1.0)

    def prepare(block, carry):
        rows = pl.ds(pl.multiple_of(block * BLK, BLK), BLK)
        d_mixed = cot_ref[rows, :]
        hi, mid, low = split3(over_heads(d_mixed.astype(jnp.float32) * mixed_ref[rows, :], minus))
        for head in range(heads):
            cols = slice(head * HD, (head + 1) * HD)
            extra = jnp.where(
                lane == 0, hi[:, cols], jnp.where(lane == 1, mid[:, cols], jnp.where(lane == 2, low[:, cols], jnp.zeros_like(low[:, cols])))
            )
            doa_ref[head, rows, :] = jnp.concatenate([d_mixed[:, cols], extra], axis=1)
        return carry

    lax.fori_loop(0, tokens // BLK, prepare, 0)
    causal = lax.broadcasted_iota(jnp.int32, (BLK, BLK), 0) <= lax.broadcasted_iota(jnp.int32, (BLK, BLK), 1)

    def per_head(head, carry):
        for ki in range(tokens // BLK):
            keys = pl.ds(ki * BLK, BLK)
            k = ka_ref[head, keys, :]
            v = va_ref[head, keys, :]
            dk = jnp.zeros((BLK, LANES), jnp.float32)
            dv = jnp.zeros((BLK, LANES), jnp.float32)
            for qi in range(ki, tokens // BLK):
                rows = pl.ds(qi * BLK, BLK)
                q = qa_ref[head, rows, :]
                d_out = doa_ref[head, rows, :]
                scores = lax.dot_general(k, q, (((1,), (1,)), ((), ())), preferred_element_type=jnp.float32)
                probs = jnp.exp(scores)
                if ki == qi:
                    probs = jnp.where(causal, probs, 0.0)
                d_probs = lax.dot_general(v, d_out, (((1,), (1,)), ((), ())), preferred_element_type=jnp.float32)
                d_scores = (probs * d_probs).astype(jnp.bfloat16)
                dv = dv + jnp.dot(probs.astype(jnp.bfloat16), d_out, preferred_element_type=jnp.float32)
                dk = dk + jnp.dot(d_scores, q, preferred_element_type=jnp.float32)
                dq = lax.dot_general(d_scores, k, (((0,), (0,)), ((), ())), preferred_element_type=jnp.float32)
                if ki == 0:
                    dq_ref[head, rows, :] = dq
                else:
                    dq_ref[head, rows, :] += dq
            dk_ref[head, keys, :] = dk
            dv_ref[head, keys, :] = dv
        return carry

    lax.fori_loop(0, heads, per_head, 0)

    raw_copy.wait()
    mean = same_head(2 * width, 1.0 / HD)
    gains = jnp.concatenate([gain_ref[...], gain_ref[...]], axis=1)
    scale = jnp.where(lax.broadcasted_iota(jnp.int32, (1, 2 * width), 1) < width, HD**-0.5, 1.0)

    def finish(block, sums):
        start = pl.multiple_of(block * BLK, BLK)
        rows = pl.ds(start, BLK)
        inside = lax.broadcasted_iota(jnp.int32, (BLK, 1), 0) + start < length
        grad = jnp.concatenate([ref[head, rows, :][:, :HD] for ref in (dq_ref, dk_ref) for head in range(heads)], axis=1)
        grad = grad * scale
        raw = raw_ref[rows, :]
        factor = lax.rsqrt(over_heads(raw * raw, mean) + eps)
        normed = raw * factor
        scaled = grad * gains
        back = factor * (scaled - normed * over_heads(scaled * normed, mean))
        grads_ref[rows, : 2 * width] = back.astype(jnp.bfloat16)
        dv = jnp.concatenate([dv_ref[head, rows, :][:, :HD] for head in range(heads)], axis=1)
        grads_ref[rows, 2 * width : 3 * width] = jnp.where(inside, dv, 0.0).astype(jnp.bfloat16)
        rest = grads_ref.shape[1] - 3 * width
        if rest:
            grads_ref[rows, 3 * width :] = jnp.zeros((BLK, rest), jnp.bfloat16)
        return sums + jnp.sum(grad * normed, axis=0, keepdims=True)

    sums = lax.fori_loop(0, tokens // BLK, finish, jnp.zeros((1, 2 * width), jnp.float32))
    gain_grad_ref[...] = sums[:, :width] + sums[:, width:]


def attend_back(qkv, gain, length, mixed, d_mixed, qa, ka, va):
    tokens, three = qkv.shape
    width = gain.shape[1]
    heads = width // HD
    vmem = pl.BlockSpec(memory_space=pltpu.VMEM)
    aug = pltpu.VMEM((heads, tokens, LANES), jnp.float32)
    return pl.pallas_call(
        functools.partial(attend_back_kernel, heads),
        out_shape=(
            jax.ShapeDtypeStruct((tokens, three), jnp.bfloat16),
            jax.ShapeDtypeStruct((1, width), jnp.float32),
        ),
        in_specs=[pl.BlockSpec(memory_space=pltpu.SMEM), pl.BlockSpec(memory_space=pltpu.HBM)] + [vmem] * 6,
        out_specs=(vmem,) * 2,
        scratch_shapes=[
            pltpu.VMEM((heads, tokens, LANES), jnp.bfloat16),
            aug,
            aug,
            aug,
            pltpu.VMEM((tokens, 2 * width), jnp.float32),
            pltpu.SemaphoreType.DMA,
        ],
        compiler_params=pltpu.CompilerParams(vmem_limit_bytes=60 << 20),
        cost_estimate=pl.CostEstimate(
            flops=heads * tokens * tokens, bytes_accessed=8 << 20, transcendentals=0
        ),
        name="attend_back",
    )(length, qkv, gain, mixed, d_mixed, qa, ka, va)


CORE, XAX, YAX = 1, 2, 4
GROUPS = ((0, 3), (3, 5))


def swap_dp(v, bit):
    return lax.ppermute(v, "dp", [(i, i ^ bit) for i in range(8)])


def swap_z(v, mask):
    return lax.ppermute(v, "ctx", [(i, i ^ mask) for i in range(4)])


def fence(*arrays):
    return lax.optimization_barrier(arrays)


def pick(v, index, axis=0):
    return lax.dynamic_index_in_dim(v, index, axis, keepdims=False)


def add_low(a, b):
    return (a.astype(jnp.float32) + b.astype(jnp.float32)).astype(jnp.bfloat16)


def by_core(c, own, other, axis=0):
    return jnp.where(c == 0, jnp.stack([own, other], axis), jnp.stack([other, own], axis))


def add3(a, b, d):
    return (a.astype(jnp.float32) + b.astype(jnp.float32) + d.astype(jnp.float32)).astype(jnp.bfloat16)


class Cells:
    def __init__(self, parts, x_first):
        self.corner, self.side, self.relay, self.keep = parts
        self.links = (XAX, YAX) if x_first else (YAX, XAX)

    def first(self, v):
        return swap_dp(v, self.links[0])

    def second(self, corner):
        return swap_dp(add_low(self.relay, corner), self.links[1])

    def total(self, side, relay):
        return add3(self.keep, side, relay)


def cells(parts):
    return [Cells(parts[:4], True), Cells(parts[4:], False)]


def total3(a, b, d):
    return a.astype(jnp.float32) + b.astype(jnp.float32) + d.astype(jnp.float32)


COLS = (0, 640, 1024)


def heads_kernel(q_ref, k_ref, v_ref, o_ref, small_ref, out_ref):
    share, width = o_ref.shape
    heads_width = width // 4
    out_ref[...] = jnp.zeros_like(out_ref)
    for z in range(4):
        out_ref[z, :, :width] = o_ref[...]
        for (a, b), at in zip(GROUPS, COLS):
            size = (b - a) * HD
            cols = [ref[:, z * heads_width + a * HD : z * heads_width + b * HD] for ref in (q_ref, k_ref, v_ref)]
            out_ref[z, :, width + at : width + at + 3 * size] = jnp.concatenate(cols, 1)
        out_ref[z, : small_ref.shape[0], out_ref.shape[2] - small_ref.shape[1] :] = small_ref[...]


def prepare_heads(query, key, value, output, small, half):
    share = output.shape[0]
    vmem = pl.BlockSpec(memory_space=pltpu.VMEM)
    return pl.pallas_call(
        heads_kernel,
        out_shape=jax.ShapeDtypeStruct((4, share, half), jnp.bfloat16),
        in_specs=[vmem] * 5,
        out_specs=vmem,
        compiler_params=pltpu.CompilerParams(vmem_limit_bytes=60 << 20),
        cost_estimate=pl.CostEstimate(flops=0, bytes_accessed=2 << 20, transcendentals=0),
        name="prepare_heads",
    )(query, key, value, output, small)


def prepare_kernel(core_ref, up_ref, gate_ref, down_ref, own_ref, other_ref, dw_ref):
    width = down_ref.shape[2]
    step = up_ref.shape[1] // 8
    for kind, ref in enumerate((up_ref, gate_ref)):
        for core in range(2):

            @pl.when(core_ref[0] == core)
            def _():
                for at in range(4):
                    here = pl.ds(at * step, step)
                    own_ref[kind, :, here] = ref[:, (2 * at + core) * step : (2 * at + core + 1) * step]
                    other_ref[kind, :, here] = ref[:, (2 * at + 1 - core) * step : (2 * at + 2 - core) * step]
    for part in range(2):
        for side in range(2):
            dw_ref[part, :, side * width : (side + 1) * width] = down_ref[2 * part + side]


def prepare(c, up, gate, down):
    share, wide = up.shape
    vmem = pl.BlockSpec(memory_space=pltpu.VMEM)
    planes = jax.ShapeDtypeStruct((2, share, wide // 2), jnp.bfloat16)
    return pl.pallas_call(
        prepare_kernel,
        out_shape=(planes,) * 3,
        in_specs=[pl.BlockSpec(memory_space=pltpu.SMEM)] + [vmem] * 3,
        out_specs=(vmem,) * 3,
        compiler_params=pltpu.CompilerParams(vmem_limit_bytes=60 << 20),
        cost_estimate=pl.CostEstimate(flops=0, bytes_accessed=4 << 20, transcendentals=0),
        name="prepare",
    )(c.astype(jnp.int32).reshape(1), up, gate, down)


def run_copies(copies):
    copies = [pltpu.make_async_copy(*copy) for copy in copies]
    for copy in copies:
        copy.start()
    for copy in copies:
        copy.wait()


def place(sources, plan, coords, cuts):
    count, rows = len(sources), sources[0].shape[1]

    def kernel(coord_ref, *refs):
        outs, sems = refs[count:-1], refs[-1]
        copies = []
        for at, (key, array, plane, inner) in enumerate(plan):
            where = tuple(jnp.bitwise_xor(coord_ref[d], key[d]) for d in range(3)) + (inner,)
            for out, (out_ref, (size, start, length)) in enumerate(zip(outs, cuts)):
                copies.append((refs[array].at[plane, :, pl.ds(start, length)], out_ref.at[where], sems.at[at, out]))
        run_copies(copies)

    return pl.pallas_call(
        kernel,
        out_shape=[jax.ShapeDtypeStruct((2, 2, 2, 4, rows, size), jnp.bfloat16) for size, _, _ in cuts],
        in_specs=[pl.BlockSpec(memory_space=pltpu.SMEM)] + [pl.BlockSpec(memory_space=pltpu.HBM)] * count,
        out_specs=[pl.BlockSpec(memory_space=pltpu.VMEM)] * len(cuts),
        scratch_shapes=[pltpu.SemaphoreType.DMA((len(plan), len(cuts)))],
        compiler_params=pltpu.CompilerParams(vmem_limit_bytes=60 << 20),
        cost_estimate=pl.CostEstimate(flops=0, bytes_accessed=14 << 20, transcendentals=0),
        name="place",
    )(coords, *sources)


def spread(sources, plan, coords, width):
    count, share, half = len(sources), sources[0].shape[1], sources[0].shape[2]

    def kernel(coord_ref, *refs):
        up_ref, gate_ref, down_ref, sems = refs[count:]
        copies = []
        for at, (key, array, plane, core) in enumerate(plan):
            yy, xx, zz = (jnp.bitwise_xor(coord_ref[d], key[d]) for d in range(3))
            for kind, out_ref in enumerate((up_ref, gate_ref)):
                copies.append((refs[array].at[plane + kind], out_ref.at[yy, xx, core, zz], sems.at[at, kind]))
            for side in range(2):
                lanes = pl.ds(side * width, width)
                copies.append((refs[array].at[plane + 2, :, lanes], down_ref.at[yy, xx, zz, core, side], sems.at[at, 2 + side]))
        run_copies(copies)

    up, gate, down = pl.pallas_call(
        kernel,
        out_shape=[
            jax.ShapeDtypeStruct((2, 2, 2, 4, share, half), jnp.bfloat16),
            jax.ShapeDtypeStruct((2, 2, 2, 4, share, half), jnp.bfloat16),
            jax.ShapeDtypeStruct((2, 2, 4, 2, 2, share, width), jnp.bfloat16),
        ],
        in_specs=[pl.BlockSpec(memory_space=pltpu.SMEM)] + [pl.BlockSpec(memory_space=pltpu.HBM)] * count,
        out_specs=[pl.BlockSpec(memory_space=pltpu.VMEM)] * 3,
        scratch_shapes=[pltpu.SemaphoreType.DMA((len(plan), 4))],
        compiler_params=pltpu.CompilerParams(vmem_limit_bytes=60 << 20),
        cost_estimate=pl.CostEstimate(flops=0, bytes_accessed=40 << 20, transcendentals=0),
        name="spread",
    )(coords, *sources)
    return up, gate, down


def spread_last(weights, parts, key, coords):
    _, share, half = parts[0].shape
    width = weights[2].shape[-1]

    def kernel(coord_ref, *refs):
        held_ref, in_sems, out_sems = refs[8:]
        yy, xx, zz = (jnp.bitwise_xor(coord_ref[d], key[d]) for d in range(3))
        run_copies([(refs[core], held_ref.at[core], in_sems.at[core]) for core in range(2)])
        up_ref, gate_ref, down_ref = refs[5:8]
        copies = []
        for core in range(2):
            for kind, ref in enumerate((up_ref, gate_ref)):
                copies.append((held_ref.at[core, kind], ref.at[yy, xx, core, zz], out_sems.at[core, kind]))
            for side in range(2):
                lanes = pl.ds(side * width, width)
                copies.append((held_ref.at[core, 2, :, lanes], down_ref.at[yy, xx, zz, core, side], out_sems.at[core, 2 + side]))
        run_copies(copies)

    hbm = pl.BlockSpec(memory_space=pltpu.HBM)
    up, gate, down = pl.pallas_call(
        kernel,
        out_shape=[jax.ShapeDtypeStruct(v.shape, v.dtype) for v in weights],
        in_specs=[pl.BlockSpec(memory_space=pltpu.SMEM)] + [hbm] * 5,
        out_specs=[hbm] * 3,
        scratch_shapes=[
            pltpu.VMEM((2, 3, share, half), jnp.bfloat16),
            pltpu.SemaphoreType.DMA((2,)),
            pltpu.SemaphoreType.DMA((2, 4)),
        ],
        input_output_aliases={3: 0, 4: 1, 5: 2},
        compiler_params=pltpu.CompilerParams(vmem_limit_bytes=BIG),
        cost_estimate=small_cost(),
        name="spread_last",
    )(coords, *parts, *weights)
    return up.reshape(32 * share, half), gate.reshape(32 * share, half), down.reshape(64 * share, width)

BIG = 60 << 20
TILE = 512


def small_cost(bytes_accessed=1 << 20):
    return pl.CostEstimate(flops=0, bytes_accessed=bytes_accessed, transcendentals=0)


def dot(a, b, on_a=1, on_b=0):
    return lax.dot_general(a, b, (((on_a,), (on_b,)), ((), ())), preferred_element_type=jnp.float32)


def ff_forward(own, other, up, gate, down, scale_up, scale_gate):
    rows, width = own.shape
    hidden = up.shape[1]
    steps = hidden // TILE

    def kernel(own_ref, other_ref, up_ref, gate_ref, down_ref, su_ref, sg_ref,
               upper_ref, gating_ref, hidden_ref, lower_ref, lower_other_ref, turned_ref, both_ref, acc_ref):
        step = pl.program_id(0)

        @pl.when(step == 0)
        def _():
            both_ref[:rows] = own_ref[...]
            both_ref[rows:] = other_ref[...]

        both = both_ref[...]
        upper = dot(both, up_ref[...])
        gating = dot(both, gate_ref[...])
        upper_ref[...] = upper
        gating_ref[...] = gating
        gate_arg = gating * sg_ref[...]
        hid = ((upper * su_ref[...]) * (gate_arg / (1.0 + jnp.exp(-gate_arg)))).astype(jnp.bfloat16)
        hidden_ref[...] = hid
        part = dot(hid, down_ref[...])

        @pl.when(step == 0)
        def _():
            acc_ref[...] = part

        @pl.when(step > 0)
        def _():
            acc_ref[...] += part

        @pl.when(step == steps - 1)
        def _():
            lower_ref[...] = acc_ref[:rows]
            lower_other_ref[...] = acc_ref[rows:].astype(jnp.bfloat16)

        @pl.when(step == 1)
        def _():
            turned_ref[...] = both_ref[...].T

    f32, low = jnp.float32, jnp.bfloat16
    return pl.pallas_call(
        kernel,
        out_shape=(
            jax.ShapeDtypeStruct((2 * rows, hidden), f32),
            jax.ShapeDtypeStruct((2 * rows, hidden), f32),
            jax.ShapeDtypeStruct((2 * rows, hidden), low),
            jax.ShapeDtypeStruct((rows, width), f32),
            jax.ShapeDtypeStruct((rows, width), low),
            jax.ShapeDtypeStruct((width, 2 * rows), low),
        ),
        grid=(steps,),
        in_specs=[
            pl.BlockSpec((rows, width), lambda i: (0, 0)),
            pl.BlockSpec((rows, width), lambda i: (0, 0)),
            pl.BlockSpec((width, TILE), lambda i: (0, i)),
            pl.BlockSpec((width, TILE), lambda i: (0, i)),
            pl.BlockSpec((TILE, width), lambda i: (i, 0)),
            pl.BlockSpec((1, TILE), lambda i: (0, i)),
            pl.BlockSpec((1, TILE), lambda i: (0, i)),
        ],
        out_specs=(
            pl.BlockSpec((2 * rows, TILE), lambda i: (0, i)),
            pl.BlockSpec((2 * rows, TILE), lambda i: (0, i)),
            pl.BlockSpec((2 * rows, TILE), lambda i: (0, i)),
            pl.BlockSpec((rows, width), lambda i: (0, 0)),
            pl.BlockSpec((rows, width), lambda i: (0, 0)),
            pl.BlockSpec((width, 2 * rows), lambda i: (0, 0)),
        ),
        scratch_shapes=[pltpu.VMEM((2 * rows, width), low), pltpu.VMEM((2 * rows, width), f32)],
        compiler_params=pltpu.CompilerParams(vmem_limit_bytes=BIG),
        cost_estimate=small_cost(),
        name="ff_forward",
    )(own, other, up, gate, down, scale_up, scale_gate)


def down_back(coords, hidden, own, other):
    rows, width = own.shape
    cell = hidden.shape[1] // 4
    unit = width // 2

    def kernel(coord_ref, hidden_ref, own_ref, other_ref, corner0, side0, relay0, keep0, corner1, side1, relay1, keep1):
        step = pl.program_id(0)
        part = dot(hidden_ref[:rows], own_ref[...], 0, 0) + dot(hidden_ref[rows:], other_ref[...], 0, 0)
        part = part.astype(jnp.bfloat16)
        for at, refs in enumerate(((corner0, corner1), (relay0, side1), (side0, relay1), (keep0, keep1))):

            @pl.when(step == at)
            def _():
                refs[0][...] = part[:, :unit]
                refs[1][...] = part[:, unit:]

    one = jax.ShapeDtypeStruct((cell, unit), jnp.bfloat16)
    whole = pl.BlockSpec((rows, width), lambda i, coord_ref: (0, 0))
    one_spec = pl.BlockSpec((cell, unit), lambda i, coord_ref: (0, 0))
    return pl.pallas_call(
        kernel,
        out_shape=(one,) * 8,
        grid_spec=pltpu.PrefetchScalarGridSpec(
            num_scalar_prefetch=1,
            grid=(4,),
            in_specs=[
                pl.BlockSpec((2 * rows, cell), lambda i, coord_ref: (0, jnp.bitwise_xor(2 * coord_ref[0] + coord_ref[1], 3 - i))),
                whole,
                whole,
            ],
            out_specs=(one_spec,) * 8,
        ),
        compiler_params=pltpu.CompilerParams(vmem_limit_bytes=BIG),
        cost_estimate=small_cost(),
        name="down_back",
    )(coords, hidden, own, other)


def hidden_back(own, other, down, upper, gating, scale_up, scale_gate):
    rows, width = own.shape
    hidden = down.shape[0]

    def kernel(own_ref, other_ref, down_ref, upper_ref, gating_ref, su_ref, sg_ref, d_up_ref, d_gate_ref, us_ref, gs_ref):
        for part, ref in enumerate((own_ref, other_ref)):
            at = pl.ds(part * rows, rows)
            d_hidden = dot(ref[...], down_ref[...], 1, 1)
            upper, gating = upper_ref[at, :], gating_ref[at, :]
            su, sg = su_ref[...], sg_ref[...]
            gate_arg = gating * sg
            sig = 1.0 / (1.0 + jnp.exp(-gate_arg))
            d_upper = d_hidden * (gate_arg * sig)
            d_gate_arg = d_hidden * (upper * su) * (sig * (1.0 + gate_arg * (1.0 - sig)))
            us = jnp.sum(d_upper * upper, axis=0, keepdims=True)
            gs = jnp.sum(d_gate_arg * gating, axis=0, keepdims=True)
            us_ref[...] = us if part == 0 else us_ref[...] + us
            gs_ref[...] = gs if part == 0 else gs_ref[...] + gs
            d_up_ref[at, :] = (d_upper * su).astype(jnp.bfloat16)
            d_gate_ref[at, :] = (d_gate_arg * sg).astype(jnp.bfloat16)

    tall = lambda: pl.BlockSpec((2 * rows, TILE), lambda i: (0, i))
    flat = lambda: pl.BlockSpec((1, TILE), lambda i: (0, i))
    return pl.pallas_call(
        kernel,
        out_shape=(
            jax.ShapeDtypeStruct((2 * rows, hidden), jnp.bfloat16),
            jax.ShapeDtypeStruct((2 * rows, hidden), jnp.bfloat16),
            jax.ShapeDtypeStruct((1, hidden), jnp.float32),
            jax.ShapeDtypeStruct((1, hidden), jnp.float32),
        ),
        grid=(hidden // TILE,),
        in_specs=[
            pl.BlockSpec((rows, width), lambda i: (0, 0)),
            pl.BlockSpec((rows, width), lambda i: (0, 0)),
            pl.BlockSpec((TILE, width), lambda i: (i, 0)),
            tall(), tall(), flat(), flat(),
        ],
        out_specs=(tall(), tall(), flat(), flat()),
        compiler_params=pltpu.CompilerParams(vmem_limit_bytes=BIG),
        cost_estimate=small_cost(),
        name="hidden_back",
    )(own, other, down, upper, gating, scale_up, scale_gate)


def wide_back(coords, turned, d_wide):
    width, tokens = turned.shape
    hidden = d_wide.shape[1]
    part = width // 8

    def kernel(coord_ref, turned_ref, d_ref, corner0, side0, relay0, keep0, corner1, side1, relay1, keep1, order_ref):
        @pl.when(pl.program_id(0) == 0)
        def _():
            for at in range(4):
                start = jnp.bitwise_xor(2 * coord_ref[0] + coord_ref[1], at) * (2 * part)
                order_ref[pl.ds(at * 2 * part, 2 * part), :] = turned_ref[pl.ds(pl.multiple_of(start, 2 * part), 2 * part), :]

        out = dot(order_ref[...], d_ref[...]).astype(jnp.bfloat16)
        for at, ref in enumerate((keep0, keep1, side0, relay1, relay0, side1, corner0, corner1)):
            ref[...] = out[at * part : (at + 1) * part]

    tile = 512
    one = jax.ShapeDtypeStruct((part, hidden), jnp.bfloat16)
    one_spec = pl.BlockSpec((part, tile), lambda i: (0, i))
    return pl.pallas_call(
        kernel,
        out_shape=(one,) * 8,
        grid=(hidden // tile,),
        in_specs=[
            pl.BlockSpec(memory_space=pltpu.SMEM),
            pl.BlockSpec((width, tokens), lambda i: (0, 0)),
            pl.BlockSpec((tokens, tile), lambda i: (0, i)),
        ],
        out_specs=(one_spec,) * 8,
        scratch_shapes=[pltpu.VMEM((width, tokens), jnp.bfloat16)],
        compiler_params=pltpu.CompilerParams(vmem_limit_bytes=BIG),
        cost_estimate=small_cost(),
        name="wide_back",
    )(coords, turned, d_wide)


def states_back(line, d_qkv0, d_qkv1, weights, local, masks):
    width = weights.shape[0]
    low = jnp.bfloat16

    def kernel(line_ref, d0_ref, d1_ref, w_ref, *out_refs):
        step = pl.program_id(0)
        split = d0_ref.shape[1]
        part = dot(d0_ref[...], w_ref[:, :split], 1, 1) + dot(d1_ref[...], w_ref[:, split:], 1, 1)
        for at, ref in enumerate(out_refs):

            @pl.when(step == at)
            def _():
                ref[...] = part.astype(low)

    def block(i, line_ref):
        mask = masks[-1]
        for at in range(len(masks) - 1):
            mask = jnp.where(i == at, masks[at], mask)
        return (jnp.bitwise_xor(line_ref[0], mask), 0)

    return pl.pallas_call(
        kernel,
        out_shape=[jax.ShapeDtypeStruct((local, width), low) for _ in masks],
        grid_spec=pltpu.PrefetchScalarGridSpec(
            num_scalar_prefetch=1,
            grid=(len(masks),),
            in_specs=[
                pl.BlockSpec((local, d_qkv0.shape[1]), block),
                pl.BlockSpec((local, d_qkv1.shape[1]), block),
                pl.BlockSpec(weights.shape, lambda i, line_ref: (0, 0)),
            ],
            out_specs=[pl.BlockSpec((local, width), lambda i, line_ref: (0, 0)) for _ in masks],
        ),
        compiler_params=pltpu.CompilerParams(vmem_limit_bytes=BIG),
        cost_estimate=small_cost(),
        name="states_back",
    )(line, d_qkv0, d_qkv1, weights)


def project(line, states, weights):
    local, width = states[0].shape
    split = COLS[1]
    rest = weights.shape[1] - split

    def kernel(line_ref, *refs):
        w_ref, out0_ref, out1_ref = refs[4:]
        step = pl.program_id(0)
        for at in range(4):

            @pl.when(step == at)
            def _():
                out = dot(refs[at][...], w_ref[...])
                out0_ref[...] = out[:, :split]
                out1_ref[...] = out[:, split:]

    spot = lambda i, line_ref: (jnp.bitwise_xor(line_ref[0], i), 0)
    fixed = lambda i, line_ref: (0, 0)
    return pl.pallas_call(
        kernel,
        out_shape=[jax.ShapeDtypeStruct((4 * local, n), jnp.float32) for n in (split, rest)],
        grid_spec=pltpu.PrefetchScalarGridSpec(
            num_scalar_prefetch=1,
            grid=(4,),
            in_specs=[pl.BlockSpec((local, width), fixed)] * 4 + [pl.BlockSpec(weights.shape, fixed)],
            out_specs=[pl.BlockSpec((local, n), spot) for n in (split, rest)],
        ),
        compiler_params=pltpu.CompilerParams(vmem_limit_bytes=BIG),
        cost_estimate=small_cost(),
        name="project",
    )(line, *states, weights)


def rows_back(coords, states, d_qkv0, d_qkv1, gain_grad, spare):
    chunk, width = states[0].shape
    cell = width // 8
    split, three = d_qkv0.shape[1], d_qkv0.shape[1] + d_qkv1.shape[1]
    tokens = 4 * chunk
    steps = 4
    low = jnp.bfloat16

    def kernel(coord_ref, *refs):
        d0_ref, d1_ref, gain_ref, keep_ref, send_ref, acc0_ref, acc1_ref = refs[4:]
        step = pl.program_id(0)

        for at in range(4):

            @pl.when(step == at)
            def _():
                for d_ref, acc_ref in ((d0_ref, acc0_ref), (d1_ref, acc1_ref)):
                    part = dot(refs[at][...], d_ref[...], 0, 0)
                    acc_ref[...] = part if at == 0 else acc_ref[...] + part

        @pl.when(step == steps - 1)
        def _():
            here = lax.broadcasted_iota(jnp.int32, (cell, split), 1) == spare
            for at in range(4):
                for ref, core in ((keep_ref, coord_ref[2]), (send_ref, 1 - coord_ref[2])):
                    start = (2 * jnp.bitwise_xor(2 * coord_ref[0] + coord_ref[1], at) + core) * cell
                    rows = pl.ds(pl.multiple_of(start, cell), cell)
                    ref[at, :, :split] = jnp.where(here, gain_ref[rows, :], acc0_ref[rows, :]).astype(low)
                    ref[at, :, split:] = acc1_ref[rows, :].astype(low)

    shape = jax.ShapeDtypeStruct((4, cell, three), low)
    return pl.pallas_call(
        kernel,
        out_shape=(shape, shape),
        grid_spec=pltpu.PrefetchScalarGridSpec(
            num_scalar_prefetch=1,
            grid=(steps,),
            in_specs=[pl.BlockSpec((chunk, width), lambda i, coord_ref: (0, 0))] * 4
            + [
                pl.BlockSpec((chunk, split), lambda i, coord_ref: (jnp.bitwise_xor(coord_ref[3], i), 0)),
                pl.BlockSpec((chunk, three - split), lambda i, coord_ref: (jnp.bitwise_xor(coord_ref[3], i), 0)),
                pl.BlockSpec((width, 1), lambda i, coord_ref: (0, 0)),
            ],
            out_specs=(pl.BlockSpec((4, cell, three), lambda i, coord_ref: (0, 0, 0)),) * 2,
            scratch_shapes=[pltpu.VMEM((width, split), jnp.float32), pltpu.VMEM((width, three - split), jnp.float32)],
        ),
        compiler_params=pltpu.CompilerParams(vmem_limit_bytes=BIG),
        cost_estimate=pl.CostEstimate(flops=2 * tokens * width * three, bytes_accessed=16 << 20, transcendentals=0),
        name="rows_back",
    )(coords, *states, d_qkv0, d_qkv1, gain_grad)


def interleave(c, own, other):
    _, share, half = own.shape
    step = half // 4

    def kernel(core_ref, own_ref, other_ref, up_ref, gate_ref):
        for core in range(2):

            @pl.when(core_ref[0] == core)
            def _():
                for kind, ref in enumerate((up_ref, gate_ref)):
                    for at in range(4):
                        here = pl.ds(at * step, step)
                        ref[:, (2 * at + core) * step : (2 * at + core + 1) * step] = own_ref[kind, :, here]
                        ref[:, (2 * at + 1 - core) * step : (2 * at + 2 - core) * step] = other_ref[kind, :, here]

    vmem = pl.BlockSpec(memory_space=pltpu.VMEM)
    return pl.pallas_call(
        kernel,
        out_shape=(jax.ShapeDtypeStruct((share, 2 * half), own.dtype),) * 2,
        in_specs=[pl.BlockSpec(memory_space=pltpu.SMEM), vmem, vmem],
        out_specs=(vmem,) * 2,
        compiler_params=pltpu.CompilerParams(vmem_limit_bytes=BIG),
        cost_estimate=small_cost(),
        name="interleave",
    )(c.astype(jnp.int32).reshape(1), own, other)


def middle_back(d_up, d_gate, up, gate):
    tokens, hidden = d_up.shape
    width = up.shape[0]
    rows = tokens // 2
    steps = hidden // TILE

    def kernel(d_up_ref, d_gate_ref, up_ref, gate_ref, own_ref, other_ref, acc_ref):
        step = pl.program_id(0)
        part = dot(d_up_ref[...], up_ref[...], 1, 1) + dot(d_gate_ref[...], gate_ref[...], 1, 1)

        @pl.when(step == 0)
        def _():
            acc_ref[...] = part

        @pl.when(step > 0)
        def _():
            acc_ref[...] += part

        @pl.when(step == steps - 1)
        def _():
            own_ref[...] = acc_ref[:rows]
            other_ref[...] = acc_ref[rows:].astype(jnp.bfloat16)

    tall = lambda n: pl.BlockSpec((n, TILE), lambda i: (0, i))
    return pl.pallas_call(
        kernel,
        out_shape=(jax.ShapeDtypeStruct((rows, width), jnp.float32), jax.ShapeDtypeStruct((rows, width), jnp.bfloat16)),
        grid=(steps,),
        in_specs=[tall(tokens), tall(tokens), tall(width), tall(width)],
        out_specs=(pl.BlockSpec((rows, width), lambda i: (0, 0)),) * 2,
        scratch_shapes=[pltpu.VMEM((tokens, width), jnp.float32)],
        compiler_params=pltpu.CompilerParams(vmem_limit_bytes=BIG),
        cost_estimate=small_cost(),
        name="middle_back",
    )(d_up, d_gate, up, gate)


def on_cores(
    inputs,
    teacher,
    lengths,
    query_weight,
    key_weight,
    value_projection,
    output_weight,
    score_gain,
    attention_step,
    up_weight,
    gate_weight,
    down_weight,
    up_scale,
    gate_scale,
    swiglu_step,
):
    local, width = inputs.shape[1:]
    share = query_weight.shape[0]
    hidden_share = down_weight.shape[0]
    heads_width = width // 4
    three = COLS[-1]
    hidden_half = up_weight.shape[1] // 2
    tokens = local * 4
    low = jnp.bfloat16
    f32 = jnp.float32
    dp, z = lax.axis_index("dp"), lax.axis_index("ctx")
    c, x, y = dp % 2, dp // 2 % 2, dp // 4
    chip = jnp.stack([y, x, z]).astype(jnp.int32)
    line = z.astype(jnp.int32).reshape(1)
    states = inputs.reshape(local, width)

    length_parts = jnp.stack([lengths[0] // 64, lengths[0] % 64]).astype(low)
    small = jnp.concatenate([score_gain, attention_step, up_scale, gate_scale, swiglu_step, length_parts])
    cuts = [0]
    for size in (share, share, hidden_share, hidden_share, share, 2):
        cuts.append(cuts[-1] + size)
    small = jnp.pad(small, (0, 512 - small.shape[0])).reshape(2, 256)
    half = up_weight.shape[1] // 2
    ug_own, ug_other, dw = prepare(c, up_weight, gate_weight, down_weight.reshape(4, share, width))
    q0 = prepare_heads(query_weight, key_weight, value_projection, output_weight, small, half)

    def on_x(*v):
        return swap_dp(jnp.concatenate(v) if len(v) > 1 else v[0], XAX)

    def on_y(*v):
        return swap_dp(jnp.concatenate(v) if len(v) > 1 else v[0], YAX)

    def exchange(blocks):
        return lax.all_to_all(blocks, "ctx", 0, 0, tiled=True)

    ug_sib = swap_dp(ug_other, CORE)
    ug_sib, ug_own = fence(ug_sib, ug_own)
    f0 = jnp.concatenate([by_core(c, ug_own, ug_sib), dw[:, None]], 1).reshape(6, share, half)
    q0 = exchange(q0)
    f0x, f0y, f1 = on_x(f0), on_y(f0), swap_z(f0, 1)
    f0, f0x, f0y, f1, q0, states = fence(f0, f0x, f0y, f1, q0, states)
    xb, yb = on_x(f1, f0y[:3], q0), on_y(f1, f0x[3:], q0)
    s1, s2 = swap_z(states, 1), swap_z(states, 2)
    xb, yb, s1, s2, f0 = fence(xb, yb, s1, s2, f0)
    f2a, s3 = swap_z(f0[:3], 2), swap_z(s2, 1)
    xc, yc = on_x(yb[:3], yb[9:11]), on_y(xb[3:6], xb[11:])
    qc = swap_dp(jnp.concatenate([q0, xb[9:], yb[9:]]), CORE)
    f2a, s3, xc, yc, qc, f0 = fence(f2a, s3, xc, yc, qc, f0)
    f2b, f3a = swap_z(f0[3:], 2), swap_z(f2a, 1)
    f2ax, f2ay = on_x(f2a), on_y(f2a)
    qd = swap_dp(jnp.concatenate([xc[3:], yc[3:]]), CORE)
    sources = [q0, xb, yb, xc, yc, qc, qd]
    plan = []
    for mc, (own, own_at, on_x_, x_at, on_y_, y_at, cross0, at0, cross1, at1) in enumerate(
        ((0, 0, 1, 9, 2, 9, 3, 3, 4, 3), (5, 0, 5, 4, 5, 8, 6, 0, 6, 2))
    ):
        for zz in range(4):
            plan.append(((0, 0, mc), own, own_at + zz, zz))
            plan.append(((0, 1, mc), on_x_, x_at + zz, zz))
            plan.append(((1, 0, mc), on_y_, y_at + zz, zz))
            if zz < 2:
                plan.append(((1, 1, mc), cross0, at0 + zz, zz))
            else:
                plan.append(((1, 1, mc), cross1, at1 + zz - 2, zz))
    full_output, full_qkv, vectors = place(
        sources, plan, jnp.stack([y, x, c]).astype(jnp.int32),
        [(width, 0, width), (half - width - 256, width, half - width - 256), (256, half - 256, 256)],
    )
    vectors = vectors[:, :, :, :, :2].reshape(2, 2, 2, 4, 512)
    full_output = full_output.reshape(width, width)
    full_qkv = full_qkv.reshape(width, -1)
    full_gain, full_astep, full_uscale, full_gscale, full_mstep, full_lengths = (
        vectors[..., a:b].astype(f32) for a, b in zip(cuts[:-1], cuts[1:])
    )
    count = jnp.sum(full_lengths[:, :, :, 0] * jnp.array([64.0, 1.0], f32))
    astep = full_astep.reshape(width)
    mstep = full_mstep.reshape(width)
    scale_up = pick(full_uscale, c, 2).reshape(-1)
    scale_gate = pick(full_gscale, c, 2).reshape(-1)
    gain = pick(full_gain.reshape(4, 1, heads_width), z)
    pieces = (states, s1, s2, s3)
    gains = [gain[:, a * HD : b * HD] for a, b in GROUPS]
    qkv0, qkv1 = project(line, pieces, full_qkv)
    qkv0, qkv1, f2b, f2ax, f2ay, f3a = fence(qkv0, qkv1, f2b, f2ax, f2ay, f3a)
    f3b = swap_z(f2b, 1)
    f2bx, f2by, f3ax, f3ay = on_x(f2b), on_y(f2b), on_x(f3a), on_y(f3a)
    mixed0, heads0, qa0, ka0, va0 = attend(qkv0, gains[0], lengths)
    heads0, f3b, f2bx, f2by, f3ax, f3ay, qkv1 = fence(heads0, f3b, f2bx, f2by, f3ax, f3ay, qkv1)
    parts0 = exchange(heads0.reshape(4, local, -1))
    f3bx, f3by, f2ac, f2bc = on_x(f3b), on_y(f3b), on_x(f2ay), on_y(f2bx)
    mixed1, heads1, qa1, ka1, va1 = attend(qkv1, gains[1], lengths)
    heads1, f3bx, f3by, f2ac, f2bc, parts0 = fence(heads1, f3bx, f3by, f2ac, f2bc, parts0)
    parts1 = exchange(heads1.reshape(4, local, -1))
    f3ac, f3bc = on_x(f3ay), on_y(f3bx)
    sources = [f0, f0x, f0y, f1, xb, yb, xc, yc]
    sources += [f2a, f2ax, f2ay, f2ac, f2b, f2bx, f2by, f2bc, f3a, f3ax, f3ay, f3b, f3bx, f3by]
    chips = ((0, 0), (0, 1), (1, 0), (1, 1))
    spots = {
        (0, 0): ((0, 0), (1, 0), (2, 0), (4, 6)),
        (0, 1): ((0, 3), (1, 3), (2, 3), (5, 6)),
        (1, 0): ((3, 0), (4, 0), (5, 0), (6, 0)),
        (1, 1): ((3, 3), (4, 3), (5, 3), (7, 0)),
        (2, 0): ((8, 0), (9, 0), (10, 0), (11, 0)),
        (2, 1): ((12, 0), (13, 0), (14, 0), (15, 0)),
        (3, 0): ((16, 0), (17, 0), (18, 0)),
        (3, 1): ((19, 0), (20, 0), (21, 0)),
    }
    plan = [
        (key + (mz,), array, plane, core)
        for (mz, core), arrays in spots.items()
        for key, (array, plane) in zip(chips, arrays)
    ]
    weights = spread(sources, plan, chip, width)
    weights, f3ac, f3bc, parts1 = fence(weights, f3ac, f3bc, parts1)
    full_up, full_gate, full_down = spread_last(weights, (f3ac, f3bc), (1, 1, 3), chip)
    mixed_low = jnp.concatenate([parts0, parts1], -1).transpose(1, 0, 2).reshape(local, width)
    branch = matmul(mixed_low, full_output)
    resid = states.astype(f32)
    branch_norm = normalize(branch)
    first = resid + astep * (branch_norm - resid)
    middle = normalize(first)
    middle_low = middle.astype(low)
    middle_other = swap_dp(middle_low, CORE)

    flat_up, flat_gate = scale_up.reshape(1, -1), scale_gate.reshape(1, -1)
    upper, gating, hidden, lower, lower_other, turned = ff_forward(
        middle_low, middle_other, full_up, full_gate, full_down, flat_up, flat_gate
    )
    lower = lower + swap_dp(lower_other, CORE).astype(f32)
    lower_norm = normalize(lower)
    second = middle + mstep * (lower_norm - middle)
    final = normalize(second)

    query_pos = z * local + jnp.arange(local, dtype=jnp.int32)
    valid = (query_pos < lengths[0]).astype(f32).reshape(local, 1)
    diff = final - teacher.reshape(local, width).astype(f32)
    err_local = jnp.sum(valid * diff * diff)
    cot = loss_scale * 2.0 / count * valid * diff

    d_second = norm_back(second, final, cot)
    d_middle = d_second * (1.0 - mstep)
    grad_mstep = jnp.sum(d_second * (lower_norm - middle), axis=0)
    d_lower = norm_back(lower, lower_norm, d_second * mstep).astype(low)
    d_lower_other = swap_dp(d_lower, CORE)
    downs = cells(down_back(chip, hidden, d_lower, d_lower_other))
    downs[0].corner, downs[1].corner, d_lower, d_lower_other = fence(downs[0].corner, downs[1].corner, d_lower, d_lower_other)
    down_corner = [p.first(p.corner) for p in downs]
    down_side = [p.first(p.side) for p in downs]
    d_up, d_gate, grad_uscale, grad_gscale = hidden_back(
        d_lower, d_lower_other, full_down, upper, gating, flat_up, flat_gate
    )
    d_up, d_gate, down_corner, down_side = fence(d_up, d_gate, down_corner, down_side)
    down_relay = [p.second(v) for p, v in zip(downs, down_corner)]
    ups = cells(wide_back(chip, turned, d_up))
    ups[0].corner, ups[1].corner, down_relay, d_up, d_gate = fence(ups[0].corner, ups[1].corner, down_relay, d_up, d_gate)
    up_corner = [p.first(p.corner) for p in ups]
    d_both, d_both_other = middle_back(d_up, d_gate, full_up, full_gate)
    up_corner, d_both, d_both_other, ups[0].side, ups[1].side = fence(
        up_corner, d_both, d_both_other, ups[0].side, ups[1].side
    )
    up_side = [p.first(p.side) for p in ups]
    d_middle = d_middle + d_both + swap_dp(d_both_other, CORE).astype(f32)
    d_first = norm_back(first, middle, d_middle)
    input_grad = d_first * (1.0 - astep)
    grad_astep = jnp.sum(d_first * (branch_norm - resid), axis=0)
    d_branch = norm_back(branch, branch_norm, d_first * astep).astype(low)
    d_mixed = right_tdot(d_branch, full_output).astype(low)
    blocks = d_mixed.reshape(local, 4, heads_width).transpose(1, 0, 2)
    blocks = [blocks[:, :, a * HD : b * HD] for a, b in GROUPS]
    scales = jnp.concatenate([grad_uscale.reshape(2, 2, 4, hidden_share), grad_gscale.reshape(2, 2, 4, hidden_share)], -1)
    scales = jnp.where((jnp.arange(2) == c)[None, None, :, None, None], scales[:, :, None], 0.0).reshape(32, -1)
    packed = jnp.concatenate(
        [grad_astep.reshape(32, share), scales, grad_mstep.reshape(32, share), jnp.full((32, 1), err_local)], 1
    )
    packed = jnp.pad(packed, ((0, 0), (0, 512 - packed.shape[1]))).reshape(2, 2, 2, 4, 4, 128)
    packed = pick(packed, c, 2) + swap_dp(pick(packed, 1 - c, 2), CORE)
    down = jnp.concatenate([p.total(v, r) for p, v, r in zip(downs, down_side, down_relay)], 1)
    down = down.reshape(4, hidden_share, width)
    down_far = swap_z(pick(down, z ^ 3), 1)
    blocks, d_branch, up_side, d_gate, up_corner, packed, down, down_far = fence(
        blocks, d_branch, up_side, d_gate, up_corner, packed, down, down_far
    )
    parts0 = exchange(blocks[0])
    up_relay = [p.second(v) for p, v in zip(ups, up_corner)]
    gates = cells(wide_back(chip, turned, d_gate))
    packed = pick(packed, x, 1) + swap_dp(pick(packed, 1 - x, 1), XAX)
    up_relay, gates[0].corner, gates[1].corner, block1, d_branch, packed = fence(
        up_relay, gates[0].corner, gates[1].corner, blocks[1], d_branch, packed
    )
    gate_corner = [p.first(p.corner) for p in gates]
    up = jnp.stack([p.total(v, r) for p, v, r in zip(ups, up_side, up_relay)]).reshape(2, 4, share, hidden_half)
    down_far, down_near = swap_z(add_low(pick(down, z ^ 2), down_far), 2), swap_z(pick(down, z ^ 1), 1)
    g_out = left_tdot(mixed_low, d_branch).astype(low).reshape(2, 2, 2, 2, 2 * share, width)
    out_c = swap_dp(pick(g_out, 1 - c, 2), CORE)
    g_out = add_low(pick(g_out, c, 2), out_c)
    parts0, gate_corner, up, g_out, gates[0].side, gates[1].side, down_far, down_near = fence(
        parts0, gate_corner, up, g_out, gates[0].side, gates[1].side, down_far, down_near
    )
    parts1 = exchange(block1)
    gate_side = [p.first(p.side) for p in gates]
    gate_relay = [p.second(v) for p, v in zip(gates, gate_corner)]
    up_far = swap_z(pick(up, z ^ 3, 1), 1)
    d_heads0 = parts0.reshape(tokens, -1)
    d_qkv0, gain_grad0 = attend_back(qkv0, gains[0], lengths, mixed0, d_heads0, qa0, ka0, va0)
    d_qkv0, gain_grad0, parts1, gate_side, gate_relay, up_far, up, packed = fence(
        d_qkv0, gain_grad0, parts1, gate_side, gate_relay, up_far, up, packed
    )
    gate = jnp.stack([p.total(v, r) for p, v, r in zip(gates, gate_side, gate_relay)]).reshape(2, 4, share, hidden_half)
    up_far, up_near = swap_z(add_low(pick(up, z ^ 2, 1), up_far), 2), swap_z(pick(up, z ^ 1, 1), 1)
    gate_far, gate_near = swap_z(pick(gate, z ^ 3, 1), 1), swap_z(pick(gate, z ^ 1, 1), 1)
    packed = pick(packed, y) + swap_dp(pick(packed, 1 - y), YAX)
    d_heads1 = parts1.reshape(tokens, -1)
    d_qkv1, gain_grad1 = attend_back(qkv1, gains[1], lengths, mixed1, d_heads1, qa1, ka1, va1)
    d_qkv1, gain_grad1, gate, up_far, up_near, gate_far, gate_near, d_qkv0, packed = fence(
        d_qkv1, gain_grad1, gate, up_far, up_near, gate_far, gate_near, d_qkv0, packed
    )
    (states_send,) = states_back(line, d_qkv0, d_qkv1, full_qkv, local, (3,))
    gate_send = add_low(pick(gate, z ^ 2, 1), gate_far)
    states_send, gate_send, gate, packed, d_qkv0, d_qkv1 = fence(states_send, gate_send, gate, packed, d_qkv0, d_qkv1)
    states_relay = swap_z(states_send, 1)
    gate_far = swap_z(gate_send, 2)
    pair = swap_z(jnp.stack([pick(packed, z ^ 2), pick(packed, z ^ 3)]), 2)
    packed = jnp.stack([pick(packed, z), pick(packed, z ^ 1)]) + pair
    states_far, states_near, states_own = states_back(line, d_qkv0, d_qkv1, full_qkv, local, (2, 1, 0))
    grad_gain = jnp.concatenate([gain_grad0, gain_grad1], 1).reshape(-1)
    gain_all = lax.dynamic_update_slice(jnp.zeros((4 * heads_width,), f32), grad_gain, (z * heads_width,))
    spare = COLS[0] + 3 * (GROUPS[0][1] - GROUPS[0][0]) * HD
    qkv_keep, qkv_send = rows_back(
        jnp.stack([y, x, c, z]).astype(jnp.int32), pieces, d_qkv0, d_qkv1, gain_all.reshape(width, 1), spare
    )
    states_relay, qkv_send, qkv_keep, states_far, states_near, states_own, packed, gate_far = fence(
        states_relay, qkv_send, qkv_keep, states_far, states_near, states_own, packed, gate_far
    )
    states_far = swap_z(add_low(states_far, states_relay), 2)
    states_near = swap_z(states_near, 1)
    qkv_sum = add_low(qkv_keep, swap_dp(qkv_send, CORE))
    out_sum = [lax.dynamic_slice(g_out, (y ^ (at // 2), x ^ (at % 2), 0, 0, 0), (1, 1) + g_out.shape[2:]) for at in range(4)]
    out_sum = [v.reshape(2 * 2 * share, width) for v in out_sum]
    cell = lambda at, unit: jnp.concatenate(
        [v[2 * share * unit : 2 * share * (unit + 1)] for v in (qkv_sum[at], out_sum[at])], 1
    )
    rows = [Cells((cell(3, u), cell(1 + u, u), cell(2 - u, u), cell(0, u)), u == 0) for u in range(2)]
    row_far = [p.first(jnp.stack([p.side, p.corner])) for p in rows]
    packed = packed[0] + swap_z(packed[1], 1)
    own_rows = total3(pick(up, z, 1), up_near, up_far), total3(pick(gate, z, 1), gate_near, gate_far)
    own_rows = jnp.stack(own_rows, 1)
    own_part, other_part = pick(own_rows, c), swap_dp(pick(own_rows, 1 - c), CORE)
    down_grad = total3(pick(down, z), down_near, down_far).reshape(hidden_share, width)
    row_relay = [p.second(v[1]) for p, v in zip(rows, row_far)]
    up_grad, gate_grad = interleave(c, own_part, other_part)
    rows_sum = jnp.stack([p.total(v[0], r) for p, v, r in zip(rows, row_far, row_relay)]).reshape(4, share, three + width)
    columns = exchange(rows_sum)
    packed = packed.reshape(512)
    output_grad = jnp.sum(columns[..., three:].astype(f32), 0)
    columns_cut = [
        columns[..., at : at + 3 * (b - a) * HD].reshape(4, share, 3, -1) for (a, b), at in zip(GROUPS, COLS)
    ]
    score_gain_grad = jnp.sum(columns[..., spare].astype(f32), 0)
    columns = jnp.concatenate(columns_cut, -1).transpose(2, 1, 0, 3).reshape(3, share, width).astype(f32)
    columns, output_grad, score_gain_grad, input_grad, states_far, states_near, up_grad, gate_grad, down_grad = fence(
        columns, output_grad, score_gain_grad, input_grad, states_far, states_near, up_grad, gate_grad, down_grad
    )
    input_grad = input_grad + total3(states_own, states_near, states_far)
    return (
        final.astype(low)[None],
        packed[cuts[5] - cuts[1]] / count,
        input_grad[None],
        columns[0],
        columns[1],
        columns[2],
        output_grad,
        score_gain_grad,
        packed[: cuts[1]],
        up_grad,
        gate_grad,
        down_grad,
        packed[cuts[2] - cuts[1] : cuts[3] - cuts[1]],
        packed[cuts[3] - cuts[1] : cuts[4] - cuts[1]],
        packed[cuts[4] - cuts[1] : cuts[5] - cuts[1]],
    )


def per_device(
    inputs,
    teacher,
    lengths,
    query_weight,
    key_weight,
    value_projection,
    output_weight,
    score_gain,
    attention_step,
    up_weight,
    gate_weight,
    down_weight,
    up_scale,
    gate_scale,
    swiglu_step,
):
    seqs, local, width = inputs.shape
    full_len = local * lax.axis_size("ctx")
    rows = seqs * local
    heads = width // HD
    key_block = min(512, full_len)
    query_pos = lax.axis_index("ctx") * local + jnp.arange(local, dtype=jnp.int32)
    valid = (query_pos[None, :] < lengths[:, None]).astype(jnp.float32).reshape(rows, 1)
    count_local = jnp.sum(valid)
    full_query, full_key, full_value, full_output, full_gain, full_astep = (
        lax.all_gather(query_weight, ("dp", "ctx"), axis=0, tiled=True),
        lax.all_gather(key_weight, ("dp", "ctx"), axis=0, tiled=True),
        lax.all_gather(value_projection, ("dp", "ctx"), axis=0, tiled=True),
        lax.all_gather(output_weight, ("dp", "ctx"), axis=0, tiled=True),
        lax.all_gather(score_gain, ("dp", "ctx"), axis=0, tiled=True),
        lax.all_gather(attention_step, ("dp", "ctx"), axis=0, tiled=True),
    )
    states = inputs.reshape(rows, width)
    resid = states.astype(jnp.float32)
    queries = matmul(states, full_query)
    keys_raw = matmul(states, full_key)
    values_raw = matmul(states, full_value)
    gains = full_gain.astype(jnp.float32).reshape(heads, HD)
    query_norm = normalize(queries.reshape(rows, heads, HD))
    key_norm = normalize(keys_raw.reshape(rows, heads, HD))
    q_heads = (gains * query_norm).astype(jnp.bfloat16).reshape(seqs, local, heads, HD)
    k_flat = (gains * key_norm).astype(jnp.bfloat16).reshape(seqs, local, width)
    v_flat = values_raw.astype(jnp.bfloat16).reshape(seqs, local, width)

    def key_step(carry, key_piece, value_piece, key_pos):
        top, total, accum = carry
        count_keys = key_piece.shape[1]
        scores, allowed = block_scores(
            q_heads, key_piece.reshape(seqs, count_keys, heads, HD), query_pos, key_pos, lengths
        )
        scores = jnp.where(allowed, scores, -1e30)
        top_new = jnp.maximum(top, jnp.max(scores, axis=-1))
        weights = jnp.where(allowed, jnp.exp(scores - top_new[..., None]), 0.0)
        factor = jnp.exp(top - top_new)
        total = total * factor + jnp.sum(weights, axis=-1)
        accum = accum * jnp.transpose(factor, (0, 2, 1))[..., None] + jnp.einsum(
            "shqk,skhd->sqhd",
            weights.astype(jnp.bfloat16),
            value_piece.reshape(seqs, count_keys, heads, HD),
            preferred_element_type=jnp.float32,
        )
        return (top_new, total, accum)

    init = (
        jnp.full((seqs, heads, local), -1e30, jnp.float32),
        jnp.zeros((seqs, heads, local), jnp.float32),
        jnp.zeros((seqs, local, heads, HD), jnp.float32),
    )
    carry = init
    key_piece = lax.all_gather(k_flat, "ctx", axis=1, tiled=True)
    value_piece = lax.all_gather(v_flat, "ctx", axis=1, tiled=True)
    count_keys = key_piece.shape[1]

    def inner(state, index):
        offset = index * key_block
        key_part = lax.dynamic_slice_in_dim(key_piece, offset, key_block, 1)
        value_part = lax.dynamic_slice_in_dim(value_piece, offset, key_block, 1)
        positions = offset + jnp.arange(key_block, dtype=jnp.int32)
        return (key_step(state, key_part, value_part, positions), None)

    carry, unused = lax.scan(inner, carry, jnp.arange(count_keys // key_block, dtype=jnp.int32))
    top, total, accum = carry
    mixed = accum / jnp.transpose(total, (0, 2, 1))[..., None]
    log_total = top + jnp.log(total)
    mixed_low = mixed.reshape(rows, width).astype(jnp.bfloat16)
    branch = matmul(mixed_low, full_output)
    branch_norm = normalize(branch)
    astep = full_astep.astype(jnp.float32)
    first = resid + astep * (branch_norm - resid)
    middle = normalize(first)
    middle_low = middle.astype(jnp.bfloat16)
    full_up, full_gate, full_down, full_uscale, complete_gate_scale, full_mstep = (
        lax.all_gather(up_weight, ("dp", "ctx"), axis=0, tiled=True),
        lax.all_gather(gate_weight, ("dp", "ctx"), axis=0, tiled=True),
        lax.all_gather(down_weight, ("dp", "ctx"), axis=0, tiled=True),
        lax.all_gather(up_scale, ("dp", "ctx"), axis=0, tiled=True),
        lax.all_gather(gate_scale, ("dp", "ctx"), axis=0, tiled=True),
        lax.all_gather(swiglu_step, ("dp", "ctx"), axis=0, tiled=True),
    )
    upper = matmul(middle_low, full_up)
    gating = matmul(middle_low, full_gate)
    scale_up = full_uscale.astype(jnp.float32)
    scale_gate = complete_gate_scale.astype(jnp.float32)
    upper_scaled = upper * scale_up
    gate_arg = gating * scale_gate
    gate_act = jax.nn.silu(gate_arg)
    hidden = (upper_scaled * gate_act).astype(jnp.bfloat16)
    lower = matmul(hidden, full_down)
    lower_norm = normalize(lower)
    mstep = full_mstep.astype(jnp.float32)
    second = middle + mstep * (lower_norm - middle)
    final = normalize(second)
    target = teacher.reshape(rows, width).astype(jnp.float32)
    diff = final - target
    err_local = jnp.sum(valid * diff * diff)
    err_total, count = lax.psum((err_local, count_local), ("dp", "ctx"))
    cot = loss_scale * 2.0 / count * valid * diff
    full_up, full_gate, full_down, full_uscale, complete_gate_scale, full_mstep = (
        lax.all_gather(up_weight, ("dp", "ctx"), axis=0, tiled=True),
        lax.all_gather(gate_weight, ("dp", "ctx"), axis=0, tiled=True),
        lax.all_gather(down_weight, ("dp", "ctx"), axis=0, tiled=True),
        lax.all_gather(up_scale, ("dp", "ctx"), axis=0, tiled=True),
        lax.all_gather(gate_scale, ("dp", "ctx"), axis=0, tiled=True),
        lax.all_gather(swiglu_step, ("dp", "ctx"), axis=0, tiled=True),
    )
    d_second = norm_back(second, final, cot)
    d_middle = d_second * (1.0 - mstep)
    grad_mstep = jnp.sum(d_second * (lower_norm - middle), axis=0)
    d_lower = norm_back(lower, lower_norm, d_second * mstep).astype(jnp.bfloat16)
    grad_down = left_tdot(hidden, d_lower)
    d_hidden = right_tdot(d_lower, full_down)
    d_upper = d_hidden * gate_act
    sigmoid_gate = jax.nn.sigmoid(gate_arg)
    d_gate_arg = d_hidden * upper_scaled * (sigmoid_gate * (1.0 + gate_arg * (1.0 - sigmoid_gate)))
    grad_uscale = jnp.sum(d_upper * upper, axis=0)
    grad_gscale = jnp.sum(d_gate_arg * gating, axis=0)
    d_up_low = (d_upper * scale_up).astype(jnp.bfloat16)
    d_gate_low = (d_gate_arg * scale_gate).astype(jnp.bfloat16)
    d_middle = d_middle + right_tdot(d_up_low, full_up) + right_tdot(d_gate_low, full_gate)
    grad_up = left_tdot(middle_low, d_up_low)
    grad_gate = left_tdot(middle_low, d_gate_low)
    up_grad, gate_grad, down_grad, up_scale_grad, gate_scale_gradient, swiglu_step_grad = (
        lax.psum_scatter(grad_up, ("dp", "ctx"), scatter_dimension=0, tiled=True),
        lax.psum_scatter(grad_gate, ("dp", "ctx"), scatter_dimension=0, tiled=True),
        lax.psum_scatter(grad_down, ("dp", "ctx"), scatter_dimension=0, tiled=True),
        lax.psum_scatter(grad_uscale, ("dp", "ctx"), scatter_dimension=0, tiled=True),
        lax.psum_scatter(grad_gscale, ("dp", "ctx"), scatter_dimension=0, tiled=True),
        lax.psum_scatter(grad_mstep, ("dp", "ctx"), scatter_dimension=0, tiled=True),
    )
    d_first = norm_back(first, middle, d_middle)
    input_grad = d_first * (1.0 - astep)
    grad_astep = jnp.sum(d_first * (branch_norm - resid), axis=0)
    d_branch = norm_back(branch, branch_norm, d_first * astep).astype(jnp.bfloat16)
    full_query, full_key, full_value, full_output, full_gain, full_astep = (
        lax.all_gather(query_weight, ("dp", "ctx"), axis=0, tiled=True),
        lax.all_gather(key_weight, ("dp", "ctx"), axis=0, tiled=True),
        lax.all_gather(value_projection, ("dp", "ctx"), axis=0, tiled=True),
        lax.all_gather(output_weight, ("dp", "ctx"), axis=0, tiled=True),
        lax.all_gather(score_gain, ("dp", "ctx"), axis=0, tiled=True),
        lax.all_gather(attention_step, ("dp", "ctx"), axis=0, tiled=True),
    )
    gains = full_gain.astype(jnp.float32).reshape(heads, HD)
    grad_output = left_tdot(mixed_low, d_branch)
    d_mixed = right_tdot(d_branch, full_output).astype(jnp.bfloat16)
    d_mixed_heads = d_mixed.reshape(seqs, local, heads, HD)
    delta = jnp.transpose(jnp.sum(d_mixed_heads.astype(jnp.float32) * mixed, axis=-1), (0, 2, 1))
    whole_keys, whole_values = (
        lax.all_gather(k_flat, "ctx", axis=1, tiled=True),
        lax.all_gather(v_flat, "ctx", axis=1, tiled=True),
    )

    def query_terms(index):
        offset = index * key_block
        key_part = lax.dynamic_slice_in_dim(whole_keys, offset, key_block, 1).reshape(
            seqs, key_block, heads, HD
        )
        value_part = lax.dynamic_slice_in_dim(whole_values, offset, key_block, 1).reshape(
            seqs, key_block, heads, HD
        )
        key_pos = offset + jnp.arange(key_block, dtype=jnp.int32)
        scores, allowed = block_scores(q_heads, key_part, query_pos, key_pos, lengths)
        probs = jnp.where(allowed, jnp.exp(scores - log_total[..., None]), 0.0)
        d_probs = jnp.einsum(
            "sqhd,skhd->shqk", d_mixed_heads, value_part, preferred_element_type=jnp.float32
        )
        d_scores = (probs * (d_probs - delta[..., None])).astype(jnp.bfloat16)
        d_query_part = jnp.einsum(
            "shqk,skhd->sqhd", d_scores, key_part, preferred_element_type=jnp.float32
        )
        return (offset, probs, d_scores, d_query_part)

    def key_back(carry, index):
        d_query_acc, d_key_all, d_value_all = carry
        offset, probs, d_scores, d_query_part = query_terms(index)
        d_query_acc = d_query_acc + d_query_part
        d_key_part = jnp.einsum(
            "shqk,sqhd->skhd", d_scores, q_heads, preferred_element_type=jnp.float32
        ) * HD ** (-0.5)
        d_value_part = jnp.einsum(
            "shqk,sqhd->skhd",
            probs.astype(jnp.bfloat16),
            d_mixed_heads,
            preferred_element_type=jnp.float32,
        )
        d_key_all = lax.dynamic_update_slice_in_dim(
            d_key_all, d_key_part.reshape(seqs, key_block, width), offset, 1
        )
        d_value_all = lax.dynamic_update_slice_in_dim(
            d_value_all, d_value_part.reshape(seqs, key_block, width), offset, 1
        )
        return ((d_query_acc, d_key_all, d_value_all), None)

    start_carry = (
        jnp.zeros((seqs, local, heads, HD), jnp.float32),
        jnp.zeros((seqs, full_len, width), jnp.float32),
        jnp.zeros((seqs, full_len, width), jnp.float32),
    )
    (d_query_heads, d_key_all, d_value_all), unused = lax.scan(
        key_back, start_carry, jnp.arange(full_len // key_block, dtype=jnp.int32)
    )
    d_key_local, d_value_local = (
        lax.psum_scatter(
            d_key_all.astype(jnp.bfloat16), "ctx", scatter_dimension=1, tiled=True
        ).astype(jnp.float32),
        lax.psum_scatter(
            d_value_all.astype(jnp.bfloat16), "ctx", scatter_dimension=1, tiled=True
        ).astype(jnp.float32),
    )
    d_key_heads = d_key_local.reshape(rows, heads, HD)
    d_value_local = d_value_local.reshape(rows, width)
    d_query_heads = (d_query_heads * HD ** (-0.5)).reshape(rows, heads, HD)
    grad_gain = jnp.sum(d_query_heads * query_norm, axis=0) + jnp.sum(
        d_key_heads * key_norm, axis=0
    )
    d_query_low = (
        norm_back(queries.reshape(rows, heads, HD), query_norm, d_query_heads * gains)
        .reshape(rows, width)
        .astype(jnp.bfloat16)
    )
    d_key_low = (
        norm_back(keys_raw.reshape(rows, heads, HD), key_norm, d_key_heads * gains)
        .reshape(rows, width)
        .astype(jnp.bfloat16)
    )
    d_value_low = d_value_local.astype(jnp.bfloat16)
    input_grad = (
        input_grad
        + right_tdot(d_query_low, full_query)
        + right_tdot(d_key_low, full_key)
        + right_tdot(d_value_low, full_value)
    )
    grad_query = left_tdot(states, d_query_low)
    grad_key = left_tdot(states, d_key_low)
    grad_value = left_tdot(states, d_value_low)
    query_grad, key_grad, value_grad, output_grad, score_gain_grad, attention_step_grad = (
        lax.psum_scatter(grad_query, ("dp", "ctx"), scatter_dimension=0, tiled=True),
        lax.psum_scatter(grad_key, ("dp", "ctx"), scatter_dimension=0, tiled=True),
        lax.psum_scatter(grad_value, ("dp", "ctx"), scatter_dimension=0, tiled=True),
        lax.psum_scatter(grad_output, ("dp", "ctx"), scatter_dimension=0, tiled=True),
        lax.psum_scatter(grad_gain.reshape(width), ("dp", "ctx"), scatter_dimension=0, tiled=True),
        lax.psum_scatter(grad_astep, ("dp", "ctx"), scatter_dimension=0, tiled=True),
    )
    distill_loss_mean = err_total / count
    layer_out = final.astype(jnp.bfloat16).reshape(seqs, local, width)
    return (
        layer_out,
        distill_loss_mean,
        input_grad.reshape(seqs, local, width),
        query_grad,
        key_grad,
        value_grad,
        output_grad,
        score_gain_grad,
        attention_step_grad,
        up_grad,
        gate_grad,
        down_grad,
        up_scale_grad,
        gate_scale_gradient,
        swiglu_step_grad,
    )


def solution(mesh):
    placed = (
        P("dp", "ctx", None),
        P("dp", "ctx", None),
        P("dp"),
        P(("dp", "ctx"), None),
        P(("dp", "ctx"), None),
        P(("dp", "ctx"), None),
        P(("dp", "ctx"), None),
        P(("dp", "ctx")),
        P(("dp", "ctx")),
        P(("dp", "ctx"), None),
        P(("dp", "ctx"), None),
        P(("dp", "ctx"), None),
        P(("dp", "ctx")),
        P(("dp", "ctx")),
        P(("dp", "ctx")),
    )
    on_one = on_cores if dict(mesh.shape) == {"dp": 8, "ctx": 4} else per_device
    return jax.shard_map(
        on_one,
        mesh=mesh,
        in_specs=placed,
        out_specs=(
            P("dp", "ctx", None),
            P(),
            P("dp", "ctx", None),
            P(("dp", "ctx"), None),
            P(("dp", "ctx"), None),
            P(("dp", "ctx"), None),
            P(("dp", "ctx"), None),
            P(("dp", "ctx")),
            P(("dp", "ctx")),
            P(("dp", "ctx"), None),
            P(("dp", "ctx"), None),
            P(("dp", "ctx"), None),
            P(("dp", "ctx")),
            P(("dp", "ctx")),
            P(("dp", "ctx")),
        ),
        check_vma=False,
    )
```

```python
import functools

import jax
import jax.numpy as jnp
from jax import lax
from jax.experimental import pallas as pl
from jax.experimental.pallas import tpu as pltpu
from jax.sharding import PartitionSpec as P

HD = 64


eps = 1e-06
loss_scale = 32768.0


def normalize(value_rows):
    return value_rows * lax.rsqrt(jnp.mean(value_rows * value_rows, axis=-1, keepdims=True) + eps)


def norm_back(value_rows, normed, grad):
    factor = lax.rsqrt(jnp.mean(value_rows * value_rows, axis=-1, keepdims=True) + eps)
    return factor * (grad - normed * jnp.mean(grad * normed, axis=-1, keepdims=True))


def matmul(left, right):
    return jnp.dot(left, right, preferred_element_type=jnp.float32)


def left_tdot(left, right):
    return lax.dot_general(
        left, right, (((0,), (0,)), ((), ())), preferred_element_type=jnp.float32
    )


def right_tdot(left, right):
    return lax.dot_general(
        left, right, (((1,), (1,)), ((), ())), preferred_element_type=jnp.float32
    )


def block_scores(queries, keys, query_pos, key_pos, lens):
    scores = jnp.einsum(
        "sqhd,skhd->shqk", queries, keys, preferred_element_type=jnp.float32
    ) * HD ** (-0.5)
    allowed = (key_pos[None, None, :] <= query_pos[None, :, None]) & (
        key_pos[None, None, :] < lens[:, None, None]
    )
    return (scores, allowed[:, None])


BLK = 512
LANES = 128


def same_head(size, value):
    rows = lax.broadcasted_iota(jnp.int32, (size, size), 0) // HD
    cols = lax.broadcasted_iota(jnp.int32, (size, size), 1) // HD
    return jnp.where(rows == cols, value, 0.0).astype(jnp.bfloat16)


def over_heads(v, matrix):
    hi = v.astype(jnp.bfloat16)
    low = (v - hi.astype(jnp.float32)).astype(jnp.bfloat16)
    return jnp.dot(hi, matrix, preferred_element_type=jnp.float32) + jnp.dot(low, matrix, preferred_element_type=jnp.float32)


def split3(v):
    hi = v.astype(jnp.bfloat16)
    rest = v - hi.astype(jnp.float32)
    mid = rest.astype(jnp.bfloat16)
    low = (rest - mid.astype(jnp.float32)).astype(jnp.bfloat16)
    return hi, mid, low


def attend_kernel(heads, length_ref, qkv_ref, gain_ref, mixed_ref, low_ref, qa_ref, ka_ref, va_ref, out_ref):
    tokens = qkv_ref.shape[0]
    width = heads * HD
    length = length_ref[0]
    lane = lax.broadcasted_iota(jnp.int32, (BLK, HD), 1)

    mean = same_head(2 * width, 1.0 / HD)
    gains = jnp.concatenate([gain_ref[...], gain_ref[...]], axis=1)

    def prepare(block, carry):
        start = pl.multiple_of(block * BLK, BLK)
        rows = pl.ds(start, BLK)
        inside = (lax.broadcasted_iota(jnp.int32, (BLK, 1), 0) + start < length).astype(jnp.float32)
        ones = jnp.where(lane < 3, inside, 0.0).astype(jnp.bfloat16)
        nothing = jnp.zeros((BLK, HD), jnp.bfloat16)
        raw = qkv_ref[rows, : 2 * width]
        scaled = gains * (raw * lax.rsqrt(over_heads(raw * raw, mean) + eps))
        qs = scaled[:, :width].astype(jnp.bfloat16) * jnp.bfloat16(HD**-0.5)
        ks = (scaled[:, width:] * inside).astype(jnp.bfloat16)
        vs = (qkv_ref[rows, 2 * width : 3 * width] * inside).astype(jnp.bfloat16)
        for head in range(heads):
            cols = slice(head * HD, (head + 1) * HD)
            qa_ref[head, rows, :] = jnp.concatenate([qs[:, cols], nothing], axis=1)
            ka_ref[head, rows, :] = jnp.concatenate([ks[:, cols], ones], axis=1)
            va_ref[head, rows, :] = jnp.concatenate([vs[:, cols], ones], axis=1)
        return carry

    lax.fori_loop(0, tokens // BLK, prepare, 0)
    part = BLK // 2
    place = lax.broadcasted_iota(jnp.int32, (BLK, part), 0) - lax.broadcasted_iota(jnp.int32, (BLK, part), 1)

    def per_head(head, carry):
        for qi in range(tokens // BLK):
            rows = pl.ds(qi * BLK, BLK)
            q = qa_ref[head, rows, :]
            acc = jnp.zeros((BLK, LANES), jnp.float32)
            for ki in range(2 * (qi + 1)):
                keys = pl.ds(ki * part, part)
                scores = lax.dot_general(
                    q, ka_ref[head, keys, :], (((1,), (1,)), ((), ())), preferred_element_type=jnp.float32
                )
                weights = jnp.exp(scores)
                if ki >= 2 * qi:
                    weights = jnp.where(place >= (ki - 2 * qi) * part, weights, 0.0)
                acc = acc + jnp.dot(
                    weights.astype(jnp.bfloat16), va_ref[head, keys, :], preferred_element_type=jnp.float32
                )
            total = acc[:, HD : HD + 1]
            out_ref[head, rows, :] = acc / total
            hi, mid, low = split3(-jnp.log(total))
            extra = jnp.where(lane == 0, hi, jnp.where(lane == 1, mid, jnp.where(lane == 2, low, jnp.zeros_like(low))))
            qa_ref[head, rows, :] = jnp.concatenate([q[:, :HD], extra], axis=1)
        return carry

    lax.fori_loop(0, heads, per_head, 0)

    def finish(block, carry):
        rows = pl.ds(pl.multiple_of(block * BLK, BLK), BLK)
        whole = jnp.concatenate([out_ref[head, rows, :][:, :HD] for head in range(heads)], axis=1)
        mixed_ref[rows, :] = whole
        low_ref[rows, :] = whole.astype(jnp.bfloat16)
        return carry

    lax.fori_loop(0, tokens // BLK, finish, 0)


def attend(qkv, gain, length):
    tokens, width = qkv.shape[0], gain.shape[1]
    heads = width // HD
    vmem = pl.BlockSpec(memory_space=pltpu.VMEM)
    aug = jax.ShapeDtypeStruct((heads, tokens, LANES), jnp.bfloat16)
    return pl.pallas_call(
        functools.partial(attend_kernel, heads),
        out_shape=(
            jax.ShapeDtypeStruct((tokens, width), jnp.float32),
            jax.ShapeDtypeStruct((tokens, width), jnp.bfloat16),
            aug,
            aug,
            aug,
        ),
        in_specs=[pl.BlockSpec(memory_space=pltpu.SMEM), vmem, vmem],
        out_specs=(vmem,) * 5,
        scratch_shapes=[pltpu.VMEM((heads, tokens, LANES), jnp.float32)],
        compiler_params=pltpu.CompilerParams(vmem_limit_bytes=56 << 20),
        cost_estimate=pl.CostEstimate(
            flops=heads * tokens * tokens, bytes_accessed=8 << 20, transcendentals=0
        ),
        name="attend",
    )(length, qkv, gain)


def attend_back_kernel(
    heads, length_ref, qkv_ref, gain_ref, mixed_ref, cot_ref, qa_ref, ka_ref, va_ref,
    grads_ref, gain_grad_ref, doa_ref, dq_ref, dk_ref, dv_ref, raw_ref, sem,
):
    tokens = qkv_ref.shape[0]
    width = heads * HD
    length = length_ref[0]
    lane = lax.broadcasted_iota(jnp.int32, (BLK, HD), 1)
    raw_copy = pltpu.make_async_copy(qkv_ref.at[:, pl.ds(0, 2 * width)], raw_ref, sem)
    raw_copy.start()
    minus = same_head(width, -1.0)

    def prepare(block, carry):
        rows = pl.ds(pl.multiple_of(block * BLK, BLK), BLK)
        d_mixed = cot_ref[rows, :]
        hi, mid, low = split3(over_heads(d_mixed.astype(jnp.float32) * mixed_ref[rows, :], minus))
        for head in range(heads):
            cols = slice(head * HD, (head + 1) * HD)
            extra = jnp.where(
                lane == 0, hi[:, cols], jnp.where(lane == 1, mid[:, cols], jnp.where(lane == 2, low[:, cols], jnp.zeros_like(low[:, cols])))
            )
            doa_ref[head, rows, :] = jnp.concatenate([d_mixed[:, cols], extra], axis=1)
        return carry

    lax.fori_loop(0, tokens // BLK, prepare, 0)
    causal = lax.broadcasted_iota(jnp.int32, (BLK, BLK), 0) <= lax.broadcasted_iota(jnp.int32, (BLK, BLK), 1)

    def per_head(head, carry):
        for ki in range(tokens // BLK):
            keys = pl.ds(ki * BLK, BLK)
            k = ka_ref[head, keys, :]
            v = va_ref[head, keys, :]
            dk = jnp.zeros((BLK, LANES), jnp.float32)
            dv = jnp.zeros((BLK, LANES), jnp.float32)
            for qi in range(ki, tokens // BLK):
                rows = pl.ds(qi * BLK, BLK)
                q = qa_ref[head, rows, :]
                d_out = doa_ref[head, rows, :]
                scores = lax.dot_general(k, q, (((1,), (1,)), ((), ())), preferred_element_type=jnp.float32)
                probs = jnp.exp(scores)
                if ki == qi:
                    probs = jnp.where(causal, probs, 0.0)
                d_probs = lax.dot_general(v, d_out, (((1,), (1,)), ((), ())), preferred_element_type=jnp.float32)
                d_scores = (probs * d_probs).astype(jnp.bfloat16)
                dv = dv + jnp.dot(probs.astype(jnp.bfloat16), d_out, preferred_element_type=jnp.float32)
                dk = dk + jnp.dot(d_scores, q, preferred_element_type=jnp.float32)
                dq = lax.dot_general(d_scores, k, (((0,), (0,)), ((), ())), preferred_element_type=jnp.float32)
                if ki == 0:
                    dq_ref[head, rows, :] = dq
                else:
                    dq_ref[head, rows, :] += dq
            dk_ref[head, keys, :] = dk
            dv_ref[head, keys, :] = dv
        return carry

    lax.fori_loop(0, heads, per_head, 0)

    raw_copy.wait()
    mean = same_head(2 * width, 1.0 / HD)
    gains = jnp.concatenate([gain_ref[...], gain_ref[...]], axis=1)
    scale = jnp.where(lax.broadcasted_iota(jnp.int32, (1, 2 * width), 1) < width, HD**-0.5, 1.0)

    def finish(block, sums):
        start = pl.multiple_of(block * BLK, BLK)
        rows = pl.ds(start, BLK)
        inside = lax.broadcasted_iota(jnp.int32, (BLK, 1), 0) + start < length
        grad = jnp.concatenate([ref[head, rows, :][:, :HD] for ref in (dq_ref, dk_ref) for head in range(heads)], axis=1)
        grad = grad * scale
        raw = raw_ref[rows, :]
        factor = lax.rsqrt(over_heads(raw * raw, mean) + eps)
        normed = raw * factor
        scaled = grad * gains
        back = factor * (scaled - normed * over_heads(scaled * normed, mean))
        grads_ref[rows, : 2 * width] = back.astype(jnp.bfloat16)
        dv = jnp.concatenate([dv_ref[head, rows, :][:, :HD] for head in range(heads)], axis=1)
        grads_ref[rows, 2 * width : 3 * width] = jnp.where(inside, dv, 0.0).astype(jnp.bfloat16)
        rest = grads_ref.shape[1] - 3 * width
        if rest:
            grads_ref[rows, 3 * width :] = jnp.zeros((BLK, rest), jnp.bfloat16)
        return sums + jnp.sum(grad * normed, axis=0, keepdims=True)

    sums = lax.fori_loop(0, tokens // BLK, finish, jnp.zeros((1, 2 * width), jnp.float32))
    gain_grad_ref[...] = sums[:, :width] + sums[:, width:]


def attend_back(qkv, gain, length, mixed, d_mixed, qa, ka, va):
    tokens, three = qkv.shape
    width = gain.shape[1]
    heads = width // HD
    vmem = pl.BlockSpec(memory_space=pltpu.VMEM)
    aug = pltpu.VMEM((heads, tokens, LANES), jnp.float32)
    return pl.pallas_call(
        functools.partial(attend_back_kernel, heads),
        out_shape=(
            jax.ShapeDtypeStruct((tokens, three), jnp.bfloat16),
            jax.ShapeDtypeStruct((1, width), jnp.float32),
        ),
        in_specs=[pl.BlockSpec(memory_space=pltpu.SMEM), pl.BlockSpec(memory_space=pltpu.HBM)] + [vmem] * 6,
        out_specs=(vmem,) * 2,
        scratch_shapes=[
            pltpu.VMEM((heads, tokens, LANES), jnp.bfloat16),
            aug,
            aug,
            aug,
            pltpu.VMEM((tokens, 2 * width), jnp.float32),
            pltpu.SemaphoreType.DMA,
        ],
        compiler_params=pltpu.CompilerParams(vmem_limit_bytes=60 << 20),
        cost_estimate=pl.CostEstimate(
            flops=heads * tokens * tokens, bytes_accessed=8 << 20, transcendentals=0
        ),
        name="attend_back",
    )(length, qkv, gain, mixed, d_mixed, qa, ka, va)


CORE, XAX, YAX = 1, 2, 4
GROUPS = ((0, 3), (3, 5))


def swap_dp(v, bit):
    return lax.ppermute(v, "dp", [(i, i ^ bit) for i in range(8)])


def swap_z(v, mask):
    return lax.ppermute(v, "ctx", [(i, i ^ mask) for i in range(4)])


def fence(*arrays):
    return lax.optimization_barrier(arrays)


def pick(v, index, axis=0):
    return lax.dynamic_index_in_dim(v, index, axis, keepdims=False)


def add_low(a, b):
    return (a.astype(jnp.float32) + b.astype(jnp.float32)).astype(jnp.bfloat16)


def by_core(c, own, other, axis=0):
    return jnp.where(c == 0, jnp.stack([own, other], axis), jnp.stack([other, own], axis))


def add3(a, b, d):
    return (a.astype(jnp.float32) + b.astype(jnp.float32) + d.astype(jnp.float32)).astype(jnp.bfloat16)


class Cells:
    def __init__(self, parts, x_first):
        self.corner, self.side, self.relay, self.keep = parts
        self.links = (XAX, YAX) if x_first else (YAX, XAX)

    def first(self, v):
        return swap_dp(v, self.links[0])

    def second(self, corner):
        return swap_dp(add_low(self.relay, corner), self.links[1])

    def total(self, side, relay):
        return add3(self.keep, side, relay)


def cells(parts):
    return [Cells(parts[:4], True), Cells(parts[4:], False)]


def total3(a, b, d):
    return a.astype(jnp.float32) + b.astype(jnp.float32) + d.astype(jnp.float32)


COLS = (0, 640, 1024)


def heads_kernel(q_ref, k_ref, v_ref, o_ref, small_ref, out_ref):
    share, width = o_ref.shape
    heads_width = width // 4
    out_ref[...] = jnp.zeros_like(out_ref)
    for z in range(4):
        out_ref[z, :, :width] = o_ref[...]
        for (a, b), at in zip(GROUPS, COLS):
            size = (b - a) * HD
            cols = [ref[:, z * heads_width + a * HD : z * heads_width + b * HD] for ref in (q_ref, k_ref, v_ref)]
            out_ref[z, :, width + at : width + at + 3 * size] = jnp.concatenate(cols, 1)
        out_ref[z, : small_ref.shape[0], out_ref.shape[2] - small_ref.shape[1] :] = small_ref[...]


def prepare_heads(query, key, value, output, small, half):
    share = output.shape[0]
    vmem = pl.BlockSpec(memory_space=pltpu.VMEM)
    return pl.pallas_call(
        heads_kernel,
        out_shape=jax.ShapeDtypeStruct((4, share, half), jnp.bfloat16),
        in_specs=[vmem] * 5,
        out_specs=vmem,
        compiler_params=pltpu.CompilerParams(vmem_limit_bytes=60 << 20),
        cost_estimate=pl.CostEstimate(flops=0, bytes_accessed=2 << 20, transcendentals=0),
        name="prepare_heads",
    )(query, key, value, output, small)


def prepare_kernel(core_ref, up_ref, gate_ref, down_ref, own_ref, other_ref, dw_ref):
    width = down_ref.shape[2]
    step = up_ref.shape[1] // 8
    for kind, ref in enumerate((up_ref, gate_ref)):
        for core in range(2):

            @pl.when(core_ref[0] == core)
            def _():
                for at in range(4):
                    here = pl.ds(at * step, step)
                    own_ref[kind, :, here] = ref[:, (2 * at + core) * step : (2 * at + core + 1) * step]
                    other_ref[kind, :, here] = ref[:, (2 * at + 1 - core) * step : (2 * at + 2 - core) * step]
    for part in range(2):
        for side in range(2):
            dw_ref[part, :, side * width : (side + 1) * width] = down_ref[2 * part + side]


def prepare(c, up, gate, down):
    share, wide = up.shape
    vmem = pl.BlockSpec(memory_space=pltpu.VMEM)
    planes = jax.ShapeDtypeStruct((2, share, wide // 2), jnp.bfloat16)
    return pl.pallas_call(
        prepare_kernel,
        out_shape=(planes,) * 3,
        in_specs=[pl.BlockSpec(memory_space=pltpu.SMEM)] + [vmem] * 3,
        out_specs=(vmem,) * 3,
        compiler_params=pltpu.CompilerParams(vmem_limit_bytes=60 << 20),
        cost_estimate=pl.CostEstimate(flops=0, bytes_accessed=4 << 20, transcendentals=0),
        name="prepare",
    )(c.astype(jnp.int32).reshape(1), up, gate, down)


def run_copies(copies):
    copies = [pltpu.make_async_copy(*copy) for copy in copies]
    for copy in copies:
        copy.start()
    for copy in copies:
        copy.wait()


def place(sources, plan, coords, cuts):
    count, rows = len(sources), sources[0].shape[1]

    def kernel(coord_ref, *refs):
        outs, sems = refs[count:-1], refs[-1]
        copies = []
        for at, (key, array, plane, inner) in enumerate(plan):
            where = tuple(jnp.bitwise_xor(coord_ref[d], key[d]) for d in range(3)) + (inner,)
            for out, (out_ref, (size, start, length)) in enumerate(zip(outs, cuts)):
                copies.append((refs[array].at[plane, :, pl.ds(start, length)], out_ref.at[where], sems.at[at, out]))
        run_copies(copies)

    return pl.pallas_call(
        kernel,
        out_shape=[jax.ShapeDtypeStruct((2, 2, 2, 4, rows, size), jnp.bfloat16) for size, _, _ in cuts],
        in_specs=[pl.BlockSpec(memory_space=pltpu.SMEM)] + [pl.BlockSpec(memory_space=pltpu.HBM)] * count,
        out_specs=[pl.BlockSpec(memory_space=pltpu.VMEM)] * len(cuts),
        scratch_shapes=[pltpu.SemaphoreType.DMA((len(plan), len(cuts)))],
        compiler_params=pltpu.CompilerParams(vmem_limit_bytes=60 << 20),
        cost_estimate=pl.CostEstimate(flops=0, bytes_accessed=14 << 20, transcendentals=0),
        name="place",
    )(coords, *sources)


def spread(sources, plan, coords, width):
    count, share, half = len(sources), sources[0].shape[1], sources[0].shape[2]

    def kernel(coord_ref, *refs):
        up_ref, gate_ref, down_ref, sems = refs[count:]
        copies = []
        for at, (key, array, plane, core) in enumerate(plan):
            yy, xx, zz = (jnp.bitwise_xor(coord_ref[d], key[d]) for d in range(3))
            for kind, out_ref in enumerate((up_ref, gate_ref)):
                copies.append((refs[array].at[plane + kind], out_ref.at[yy, xx, core, zz], sems.at[at, kind]))
            for side in range(2):
                lanes = pl.ds(side * width, width)
                copies.append((refs[array].at[plane + 2, :, lanes], down_ref.at[yy, xx, zz, core, side], sems.at[at, 2 + side]))
        run_copies(copies)

    up, gate, down = pl.pallas_call(
        kernel,
        out_shape=[
            jax.ShapeDtypeStruct((2, 2, 2, 4, share, half), jnp.bfloat16),
            jax.ShapeDtypeStruct((2, 2, 2, 4, share, half), jnp.bfloat16),
            jax.ShapeDtypeStruct((2, 2, 4, 2, 2, share, width), jnp.bfloat16),
        ],
        in_specs=[pl.BlockSpec(memory_space=pltpu.SMEM)] + [pl.BlockSpec(memory_space=pltpu.HBM)] * count,
        out_specs=[pl.BlockSpec(memory_space=pltpu.VMEM)] * 3,
        scratch_shapes=[pltpu.SemaphoreType.DMA((len(plan), 4))],
        compiler_params=pltpu.CompilerParams(vmem_limit_bytes=60 << 20),
        cost_estimate=pl.CostEstimate(flops=0, bytes_accessed=40 << 20, transcendentals=0),
        name="spread",
    )(coords, *sources)
    return up, gate, down


def spread_last(weights, parts, key, coords):
    _, share, half = parts[0].shape
    width = weights[2].shape[-1]

    def kernel(coord_ref, *refs):
        held_ref, in_sems, out_sems = refs[8:]
        yy, xx, zz = (jnp.bitwise_xor(coord_ref[d], key[d]) for d in range(3))
        run_copies([(refs[core], held_ref.at[core], in_sems.at[core]) for core in range(2)])
        up_ref, gate_ref, down_ref = refs[5:8]
        copies = []
        for core in range(2):
            for kind, ref in enumerate((up_ref, gate_ref)):
                copies.append((held_ref.at[core, kind], ref.at[yy, xx, core, zz], out_sems.at[core, kind]))
            for side in range(2):
                lanes = pl.ds(side * width, width)
                copies.append((held_ref.at[core, 2, :, lanes], down_ref.at[yy, xx, zz, core, side], out_sems.at[core, 2 + side]))
        run_copies(copies)

    hbm = pl.BlockSpec(memory_space=pltpu.HBM)
    up, gate, down = pl.pallas_call(
        kernel,
        out_shape=[jax.ShapeDtypeStruct(v.shape, v.dtype) for v in weights],
        in_specs=[pl.BlockSpec(memory_space=pltpu.SMEM)] + [hbm] * 5,
        out_specs=[hbm] * 3,
        scratch_shapes=[
            pltpu.VMEM((2, 3, share, half), jnp.bfloat16),
            pltpu.SemaphoreType.DMA((2,)),
            pltpu.SemaphoreType.DMA((2, 4)),
        ],
        input_output_aliases={3: 0, 4: 1, 5: 2},
        compiler_params=pltpu.CompilerParams(vmem_limit_bytes=BIG),
        cost_estimate=small_cost(),
        name="spread_last",
    )(coords, *parts, *weights)
    return up.reshape(32 * share, half), gate.reshape(32 * share, half), down.reshape(64 * share, width)

BIG = 60 << 20
TILE = 512


def small_cost(bytes_accessed=1 << 20):
    return pl.CostEstimate(flops=0, bytes_accessed=bytes_accessed, transcendentals=0)


def dot(a, b, on_a=1, on_b=0):
    return lax.dot_general(a, b, (((on_a,), (on_b,)), ((), ())), preferred_element_type=jnp.float32)


def ff_forward(own, other, up, gate, down, scale_up, scale_gate):
    rows, width = own.shape
    hidden = up.shape[1]
    steps = hidden // TILE

    def kernel(own_ref, other_ref, up_ref, gate_ref, down_ref, su_ref, sg_ref,
               upper_ref, gating_ref, hidden_ref, lower_ref, lower_other_ref, turned_ref, both_ref, acc_ref):
        step = pl.program_id(0)

        @pl.when(step == 0)
        def _():
            both_ref[:rows] = own_ref[...]
            both_ref[rows:] = other_ref[...]

        both = both_ref[...]
        upper = dot(both, up_ref[...])
        gating = dot(both, gate_ref[...])
        upper_ref[...] = upper
        gating_ref[...] = gating
        gate_arg = gating * sg_ref[...]
        hid = ((upper * su_ref[...]) * (gate_arg / (1.0 + jnp.exp(-gate_arg)))).astype(jnp.bfloat16)
        hidden_ref[...] = hid
        part = dot(hid, down_ref[...])

        @pl.when(step == 0)
        def _():
            acc_ref[...] = part

        @pl.when(step > 0)
        def _():
            acc_ref[...] += part

        @pl.when(step == steps - 1)
        def _():
            lower_ref[...] = acc_ref[:rows]
            lower_other_ref[...] = acc_ref[rows:].astype(jnp.bfloat16)

        @pl.when(step == 1)
        def _():
            turned_ref[...] = both_ref[...].T

    f32, low = jnp.float32, jnp.bfloat16
    return pl.pallas_call(
        kernel,
        out_shape=(
            jax.ShapeDtypeStruct((2 * rows, hidden), f32),
            jax.ShapeDtypeStruct((2 * rows, hidden), f32),
            jax.ShapeDtypeStruct((2 * rows, hidden), low),
            jax.ShapeDtypeStruct((rows, width), f32),
            jax.ShapeDtypeStruct((rows, width), low),
            jax.ShapeDtypeStruct((width, 2 * rows), low),
        ),
        grid=(steps,),
        in_specs=[
            pl.BlockSpec((rows, width), lambda i: (0, 0)),
            pl.BlockSpec((rows, width), lambda i: (0, 0)),
            pl.BlockSpec((width, TILE), lambda i: (0, i)),
            pl.BlockSpec((width, TILE), lambda i: (0, i)),
            pl.BlockSpec((TILE, width), lambda i: (i, 0)),
            pl.BlockSpec((1, TILE), lambda i: (0, i)),
            pl.BlockSpec((1, TILE), lambda i: (0, i)),
        ],
        out_specs=(
            pl.BlockSpec((2 * rows, TILE), lambda i: (0, i)),
            pl.BlockSpec((2 * rows, TILE), lambda i: (0, i)),
            pl.BlockSpec((2 * rows, TILE), lambda i: (0, i)),
            pl.BlockSpec((rows, width), lambda i: (0, 0)),
            pl.BlockSpec((rows, width), lambda i: (0, 0)),
            pl.BlockSpec((width, 2 * rows), lambda i: (0, 0)),
        ),
        scratch_shapes=[pltpu.VMEM((2 * rows, width), low), pltpu.VMEM((2 * rows, width), f32)],
        compiler_params=pltpu.CompilerParams(vmem_limit_bytes=BIG),
        cost_estimate=small_cost(),
        name="ff_forward",
    )(own, other, up, gate, down, scale_up, scale_gate)


def down_back(coords, hidden, own, other):
    rows, width = own.shape
    cell = hidden.shape[1] // 4
    unit = width // 2

    def kernel(coord_ref, hidden_ref, own_ref, other_ref, corner0, side0, relay0, keep0, corner1, side1, relay1, keep1):
        step = pl.program_id(0)
        part = dot(hidden_ref[:rows], own_ref[...], 0, 0) + dot(hidden_ref[rows:], other_ref[...], 0, 0)
        part = part.astype(jnp.bfloat16)
        for at, refs in enumerate(((corner0, corner1), (relay0, side1), (side0, relay1), (keep0, keep1))):

            @pl.when(step == at)
            def _():
                refs[0][...] = part[:, :unit]
                refs[1][...] = part[:, unit:]

    one = jax.ShapeDtypeStruct((cell, unit), jnp.bfloat16)
    whole = pl.BlockSpec((rows, width), lambda i, coord_ref: (0, 0))
    one_spec = pl.BlockSpec((cell, unit), lambda i, coord_ref: (0, 0))
    return pl.pallas_call(
        kernel,
        out_shape=(one,) * 8,
        grid_spec=pltpu.PrefetchScalarGridSpec(
            num_scalar_prefetch=1,
            grid=(4,),
            in_specs=[
                pl.BlockSpec((2 * rows, cell), lambda i, coord_ref: (0, jnp.bitwise_xor(2 * coord_ref[0] + coord_ref[1], 3 - i))),
                whole,
                whole,
            ],
            out_specs=(one_spec,) * 8,
        ),
        compiler_params=pltpu.CompilerParams(vmem_limit_bytes=BIG),
        cost_estimate=small_cost(),
        name="down_back",
    )(coords, hidden, own, other)


def hidden_back(own, other, down, upper, gating, scale_up, scale_gate):
    rows, width = own.shape
    hidden = down.shape[0]

    def kernel(own_ref, other_ref, down_ref, upper_ref, gating_ref, su_ref, sg_ref, d_up_ref, d_gate_ref, us_ref, gs_ref):
        for part, ref in enumerate((own_ref, other_ref)):
            at = pl.ds(part * rows, rows)
            d_hidden = dot(ref[...], down_ref[...], 1, 1)
            upper, gating = upper_ref[at, :], gating_ref[at, :]
            su, sg = su_ref[...], sg_ref[...]
            gate_arg = gating * sg
            sig = 1.0 / (1.0 + jnp.exp(-gate_arg))
            d_upper = d_hidden * (gate_arg * sig)
            d_gate_arg = d_hidden * (upper * su) * (sig * (1.0 + gate_arg * (1.0 - sig)))
            us = jnp.sum(d_upper * upper, axis=0, keepdims=True)
            gs = jnp.sum(d_gate_arg * gating, axis=0, keepdims=True)
            us_ref[...] = us if part == 0 else us_ref[...] + us
            gs_ref[...] = gs if part == 0 else gs_ref[...] + gs
            d_up_ref[at, :] = (d_upper * su).astype(jnp.bfloat16)
            d_gate_ref[at, :] = (d_gate_arg * sg).astype(jnp.bfloat16)

    tall = lambda: pl.BlockSpec((2 * rows, TILE), lambda i: (0, i))
    flat = lambda: pl.BlockSpec((1, TILE), lambda i: (0, i))
    return pl.pallas_call(
        kernel,
        out_shape=(
            jax.ShapeDtypeStruct((2 * rows, hidden), jnp.bfloat16),
            jax.ShapeDtypeStruct((2 * rows, hidden), jnp.bfloat16),
            jax.ShapeDtypeStruct((1, hidden), jnp.float32),
            jax.ShapeDtypeStruct((1, hidden), jnp.float32),
        ),
        grid=(hidden // TILE,),
        in_specs=[
            pl.BlockSpec((rows, width), lambda i: (0, 0)),
            pl.BlockSpec((rows, width), lambda i: (0, 0)),
            pl.BlockSpec((TILE, width), lambda i: (i, 0)),
            tall(), tall(), flat(), flat(),
        ],
        out_specs=(tall(), tall(), flat(), flat()),
        compiler_params=pltpu.CompilerParams(vmem_limit_bytes=BIG),
        cost_estimate=small_cost(),
        name="hidden_back",
    )(own, other, down, upper, gating, scale_up, scale_gate)


def wide_back(coords, turned, d_wide):
    width, tokens = turned.shape
    hidden = d_wide.shape[1]
    part = width // 8

    def kernel(coord_ref, turned_ref, d_ref, corner0, side0, relay0, keep0, corner1, side1, relay1, keep1, order_ref):
        @pl.when(pl.program_id(0) == 0)
        def _():
            for at in range(4):
                start = jnp.bitwise_xor(2 * coord_ref[0] + coord_ref[1], at) * (2 * part)
                order_ref[pl.ds(at * 2 * part, 2 * part), :] = turned_ref[pl.ds(pl.multiple_of(start, 2 * part), 2 * part), :]

        out = dot(order_ref[...], d_ref[...]).astype(jnp.bfloat16)
        for at, ref in enumerate((keep0, keep1, side0, relay1, relay0, side1, corner0, corner1)):
            ref[...] = out[at * part : (at + 1) * part]

    tile = 512
    one = jax.ShapeDtypeStruct((part, hidden), jnp.bfloat16)
    one_spec = pl.BlockSpec((part, tile), lambda i: (0, i))
    return pl.pallas_call(
        kernel,
        out_shape=(one,) * 8,
        grid=(hidden // tile,),
        in_specs=[
            pl.BlockSpec(memory_space=pltpu.SMEM),
            pl.BlockSpec((width, tokens), lambda i: (0, 0)),
            pl.BlockSpec((tokens, tile), lambda i: (0, i)),
        ],
        out_specs=(one_spec,) * 8,
        scratch_shapes=[pltpu.VMEM((width, tokens), jnp.bfloat16)],
        compiler_params=pltpu.CompilerParams(vmem_limit_bytes=BIG),
        cost_estimate=small_cost(),
        name="wide_back",
    )(coords, turned, d_wide)


def states_back(line, d_qkv0, d_qkv1, weights, local, masks):
    width = weights.shape[0]
    low = jnp.bfloat16

    def kernel(line_ref, d0_ref, d1_ref, w_ref, *out_refs):
        step = pl.program_id(0)
        split = d0_ref.shape[1]
        part = dot(d0_ref[...], w_ref[:, :split], 1, 1) + dot(d1_ref[...], w_ref[:, split:], 1, 1)
        for at, ref in enumerate(out_refs):

            @pl.when(step == at)
            def _():
                ref[...] = part.astype(low)

    def block(i, line_ref):
        mask = masks[-1]
        for at in range(len(masks) - 1):
            mask = jnp.where(i == at, masks[at], mask)
        return (jnp.bitwise_xor(line_ref[0], mask), 0)

    return pl.pallas_call(
        kernel,
        out_shape=[jax.ShapeDtypeStruct((local, width), low) for _ in masks],
        grid_spec=pltpu.PrefetchScalarGridSpec(
            num_scalar_prefetch=1,
            grid=(len(masks),),
            in_specs=[
                pl.BlockSpec((local, d_qkv0.shape[1]), block),
                pl.BlockSpec((local, d_qkv1.shape[1]), block),
                pl.BlockSpec(weights.shape, lambda i, line_ref: (0, 0)),
            ],
            out_specs=[pl.BlockSpec((local, width), lambda i, line_ref: (0, 0)) for _ in masks],
        ),
        compiler_params=pltpu.CompilerParams(vmem_limit_bytes=BIG),
        cost_estimate=small_cost(),
        name="states_back",
    )(line, d_qkv0, d_qkv1, weights)


def project(line, states, weights):
    local, width = states[0].shape
    split = COLS[1]
    rest = weights.shape[1] - split

    def kernel(line_ref, *refs):
        w_ref, out0_ref, out1_ref = refs[4:]
        step = pl.program_id(0)
        for at in range(4):

            @pl.when(step == at)
            def _():
                out = dot(refs[at][...], w_ref[...])
                out0_ref[...] = out[:, :split]
                out1_ref[...] = out[:, split:]

    spot = lambda i, line_ref: (jnp.bitwise_xor(line_ref[0], i), 0)
    fixed = lambda i, line_ref: (0, 0)
    return pl.pallas_call(
        kernel,
        out_shape=[jax.ShapeDtypeStruct((4 * local, n), jnp.float32) for n in (split, rest)],
        grid_spec=pltpu.PrefetchScalarGridSpec(
            num_scalar_prefetch=1,
            grid=(4,),
            in_specs=[pl.BlockSpec((local, width), fixed)] * 4 + [pl.BlockSpec(weights.shape, fixed)],
            out_specs=[pl.BlockSpec((local, n), spot) for n in (split, rest)],
        ),
        compiler_params=pltpu.CompilerParams(vmem_limit_bytes=BIG),
        cost_estimate=small_cost(),
        name="project",
    )(line, *states, weights)


def rows_back(coords, states, d_qkv0, d_qkv1, gain_grad, spare):
    chunk, width = states[0].shape
    cell = width // 8
    split, three = d_qkv0.shape[1], d_qkv0.shape[1] + d_qkv1.shape[1]
    tokens = 4 * chunk
    steps = 4
    low = jnp.bfloat16

    def kernel(coord_ref, *refs):
        d0_ref, d1_ref, gain_ref, keep_ref, send_ref, acc0_ref, acc1_ref = refs[4:]
        step = pl.program_id(0)

        for at in range(4):

            @pl.when(step == at)
            def _():
                for d_ref, acc_ref in ((d0_ref, acc0_ref), (d1_ref, acc1_ref)):
                    part = dot(refs[at][...], d_ref[...], 0, 0)
                    acc_ref[...] = part if at == 0 else acc_ref[...] + part

        @pl.when(step == steps - 1)
        def _():
            here = lax.broadcasted_iota(jnp.int32, (cell, split), 1) == spare
            for at in range(4):
                for ref, core in ((keep_ref, coord_ref[2]), (send_ref, 1 - coord_ref[2])):
                    start = (2 * jnp.bitwise_xor(2 * coord_ref[0] + coord_ref[1], at) + core) * cell
                    rows = pl.ds(pl.multiple_of(start, cell), cell)
                    ref[at, :, :split] = jnp.where(here, gain_ref[rows, :], acc0_ref[rows, :]).astype(low)
                    ref[at, :, split:] = acc1_ref[rows, :].astype(low)

    shape = jax.ShapeDtypeStruct((4, cell, three), low)
    return pl.pallas_call(
        kernel,
        out_shape=(shape, shape),
        grid_spec=pltpu.PrefetchScalarGridSpec(
            num_scalar_prefetch=1,
            grid=(steps,),
            in_specs=[pl.BlockSpec((chunk, width), lambda i, coord_ref: (0, 0))] * 4
            + [
                pl.BlockSpec((chunk, split), lambda i, coord_ref: (jnp.bitwise_xor(coord_ref[3], i), 0)),
                pl.BlockSpec((chunk, three - split), lambda i, coord_ref: (jnp.bitwise_xor(coord_ref[3], i), 0)),
                pl.BlockSpec((width, 1), lambda i, coord_ref: (0, 0)),
            ],
            out_specs=(pl.BlockSpec((4, cell, three), lambda i, coord_ref: (0, 0, 0)),) * 2,
            scratch_shapes=[pltpu.VMEM((width, split), jnp.float32), pltpu.VMEM((width, three - split), jnp.float32)],
        ),
        compiler_params=pltpu.CompilerParams(vmem_limit_bytes=BIG),
        cost_estimate=pl.CostEstimate(flops=2 * tokens * width * three, bytes_accessed=16 << 20, transcendentals=0),
        name="rows_back",
    )(coords, *states, d_qkv0, d_qkv1, gain_grad)


def interleave(c, own, other):
    _, share, half = own.shape
    step = half // 4

    def kernel(core_ref, own_ref, other_ref, up_ref, gate_ref):
        for core in range(2):

            @pl.when(core_ref[0] == core)
            def _():
                for kind, ref in enumerate((up_ref, gate_ref)):
                    for at in range(4):
                        here = pl.ds(at * step, step)
                        ref[:, (2 * at + core) * step : (2 * at + core + 1) * step] = own_ref[kind, :, here]
                        ref[:, (2 * at + 1 - core) * step : (2 * at + 2 - core) * step] = other_ref[kind, :, here]

    vmem = pl.BlockSpec(memory_space=pltpu.VMEM)
    return pl.pallas_call(
        kernel,
        out_shape=(jax.ShapeDtypeStruct((share, 2 * half), own.dtype),) * 2,
        in_specs=[pl.BlockSpec(memory_space=pltpu.SMEM), vmem, vmem],
        out_specs=(vmem,) * 2,
        compiler_params=pltpu.CompilerParams(vmem_limit_bytes=BIG),
        cost_estimate=small_cost(),
        name="interleave",
    )(c.astype(jnp.int32).reshape(1), own, other)


def row_mean(v):
    return jnp.mean(v, axis=-1, keepdims=True)


def loss_back(inside, scale, lower, lower_got, middle, teacher, mstep):
    rows, width = lower.shape
    tile = rows // 4
    f32, low = jnp.float32, jnp.bfloat16

    def kernel(inside_ref, scale_ref, lower_ref, got_ref, middle_ref, teacher_ref, step_ref,
               final_ref, d_lower_ref, d_middle_ref, sum_ref, err_ref):
        at = pl.program_id(0)
        lower = lower_ref[...] + got_ref[...].astype(f32)
        middle, mstep = middle_ref[...], step_ref[...]
        factor = lax.rsqrt(row_mean(lower * lower) + eps)
        normed = lower * factor
        second = middle + mstep * (normed - middle)
        factor_end = lax.rsqrt(row_mean(second * second) + eps)
        final = second * factor_end
        final_ref[...] = final.astype(low)
        diff = final - teacher_ref[...].astype(f32)
        valid = (lax.broadcasted_iota(jnp.int32, (tile, 1), 0) + at * tile < inside_ref[0]).astype(f32)
        diff = valid * diff
        cot = scale_ref[0] * diff
        d_second = factor_end * (cot - final * row_mean(cot * final))
        d_middle_ref[...] = d_second * (1.0 - mstep)
        grad = d_second * mstep
        d_lower_ref[...] = (factor * (grad - normed * row_mean(grad * normed))).astype(low)
        sums = jnp.sum(d_second * (normed - middle), axis=0, keepdims=True)
        errs = jnp.sum(diff * diff, axis=0, keepdims=True)

        @pl.when(at == 0)
        def _():
            sum_ref[...] = sums
            err_ref[...] = errs

        @pl.when(at > 0)
        def _():
            sum_ref[...] += sums
            err_ref[...] += errs

    by_row = pl.BlockSpec((tile, width), lambda i: (i, 0))
    flat = pl.BlockSpec((1, width), lambda i: (0, 0))
    smem = pl.BlockSpec(memory_space=pltpu.SMEM)
    return pl.pallas_call(
        kernel,
        out_shape=(
            jax.ShapeDtypeStruct((rows, width), low),
            jax.ShapeDtypeStruct((rows, width), low),
            jax.ShapeDtypeStruct((rows, width), f32),
            jax.ShapeDtypeStruct((1, width), f32),
            jax.ShapeDtypeStruct((1, width), f32),
        ),
        grid=(rows // tile,),
        in_specs=[smem, smem, by_row, by_row, by_row, by_row, flat],
        out_specs=(by_row, by_row, by_row, flat, flat),
        compiler_params=pltpu.CompilerParams(vmem_limit_bytes=BIG),
        cost_estimate=small_cost(),
        name="loss_back",
    )(inside, scale, lower, lower_got, middle, teacher, mstep)


def branch_back(d_middle, d_own, d_got, branch, states, astep):
    rows, width = branch.shape
    tile = rows // 4
    f32, low = jnp.float32, jnp.bfloat16

    def kernel(d_middle_ref, own_ref, got_ref, branch_ref, states_ref, step_ref, grad_ref, d_branch_ref, sum_ref):
        at = pl.program_id(0)
        d_middle = d_middle_ref[...] + own_ref[...] + got_ref[...].astype(f32)
        branch, resid, astep = branch_ref[...], states_ref[...].astype(f32), step_ref[...]
        factor_branch = lax.rsqrt(row_mean(branch * branch) + eps)
        normed = branch * factor_branch
        first = resid + astep * (normed - resid)
        factor = lax.rsqrt(row_mean(first * first) + eps)
        middle = first * factor
        d_first = factor * (d_middle - middle * row_mean(d_middle * middle))
        grad_ref[...] = d_first * (1.0 - astep)
        grad = d_first * astep
        d_branch_ref[...] = (factor_branch * (grad - normed * row_mean(grad * normed))).astype(low)
        sums = jnp.sum(d_first * (normed - resid), axis=0, keepdims=True)

        @pl.when(at == 0)
        def _():
            sum_ref[...] = sums

        @pl.when(at > 0)
        def _():
            sum_ref[...] += sums

    by_row = pl.BlockSpec((tile, width), lambda i: (i, 0))
    flat = pl.BlockSpec((1, width), lambda i: (0, 0))
    return pl.pallas_call(
        kernel,
        out_shape=(
            jax.ShapeDtypeStruct((rows, width), f32),
            jax.ShapeDtypeStruct((rows, width), low),
            jax.ShapeDtypeStruct((1, width), f32),
        ),
        grid=(rows // tile,),
        in_specs=[by_row, by_row, by_row, by_row, by_row, flat],
        out_specs=(by_row, by_row, flat),
        compiler_params=pltpu.CompilerParams(vmem_limit_bytes=BIG),
        cost_estimate=small_cost(),
        name="branch_back",
    )(d_middle, d_own, d_got, branch, states, astep)


def middle_back(d_up, d_gate, up, gate):
    tokens, hidden = d_up.shape
    width = up.shape[0]
    rows = tokens // 2
    steps = hidden // TILE

    def kernel(d_up_ref, d_gate_ref, up_ref, gate_ref, own_ref, other_ref, acc_ref):
        step = pl.program_id(0)
        part = dot(d_up_ref[...], up_ref[...], 1, 1) + dot(d_gate_ref[...], gate_ref[...], 1, 1)

        @pl.when(step == 0)
        def _():
            acc_ref[...] = part

        @pl.when(step > 0)
        def _():
            acc_ref[...] += part

        @pl.when(step == steps - 1)
        def _():
            own_ref[...] = acc_ref[:rows]
            other_ref[...] = acc_ref[rows:].astype(jnp.bfloat16)

    tall = lambda n: pl.BlockSpec((n, TILE), lambda i: (0, i))
    return pl.pallas_call(
        kernel,
        out_shape=(jax.ShapeDtypeStruct((rows, width), jnp.float32), jax.ShapeDtypeStruct((rows, width), jnp.bfloat16)),
        grid=(steps,),
        in_specs=[tall(tokens), tall(tokens), tall(width), tall(width)],
        out_specs=(pl.BlockSpec((rows, width), lambda i: (0, 0)),) * 2,
        scratch_shapes=[pltpu.VMEM((tokens, width), jnp.float32)],
        compiler_params=pltpu.CompilerParams(vmem_limit_bytes=BIG),
        cost_estimate=small_cost(),
        name="middle_back",
    )(d_up, d_gate, up, gate)


def on_cores(
    inputs,
    teacher,
    lengths,
    query_weight,
    key_weight,
    value_projection,
    output_weight,
    score_gain,
    attention_step,
    up_weight,
    gate_weight,
    down_weight,
    up_scale,
    gate_scale,
    swiglu_step,
):
    local, width = inputs.shape[1:]
    share = query_weight.shape[0]
    hidden_share = down_weight.shape[0]
    heads_width = width // 4
    three = COLS[-1]
    hidden_half = up_weight.shape[1] // 2
    tokens = local * 4
    low = jnp.bfloat16
    f32 = jnp.float32
    dp, z = lax.axis_index("dp"), lax.axis_index("ctx")
    c, x, y = dp % 2, dp // 2 % 2, dp // 4
    chip = jnp.stack([y, x, z]).astype(jnp.int32)
    line = z.astype(jnp.int32).reshape(1)
    states = inputs.reshape(local, width)

    half = up_weight.shape[1] // 2
    ug_own, ug_other, dw = prepare(c, up_weight, gate_weight, down_weight.reshape(4, share, width))
    def on_x(*v):
        return swap_dp(jnp.concatenate(v) if len(v) > 1 else v[0], XAX)

    def on_y(*v):
        return swap_dp(jnp.concatenate(v) if len(v) > 1 else v[0], YAX)

    def exchange(blocks):
        return lax.all_to_all(blocks, "ctx", 0, 0, tiled=True)

    ug_sib = swap_dp(ug_other, CORE)
    ug_sib, ug_own, score_gain, query_weight = fence(ug_sib, ug_own, score_gain, query_weight)
    f0 = jnp.concatenate([by_core(c, ug_own, ug_sib), dw[:, None]], 1).reshape(6, share, half)
    length_parts = jnp.stack([lengths[0] // 64, lengths[0] % 64]).astype(low)
    small = jnp.concatenate([score_gain, attention_step, up_scale, gate_scale, swiglu_step, length_parts])
    cuts = [0]
    for size in (share, share, hidden_share, hidden_share, share, 2):
        cuts.append(cuts[-1] + size)
    small = jnp.pad(small, (0, 512 - small.shape[0])).reshape(2, 256)
    q0 = exchange(prepare_heads(query_weight, key_weight, value_projection, output_weight, small, half))
    f0x, f0y, f1 = on_x(f0), on_y(f0), swap_z(f0, 1)
    f0, f0x, f0y, f1, q0, states = fence(f0, f0x, f0y, f1, q0, states)
    xb, yb = on_x(f1, f0y[:3], q0), on_y(f1, f0x[3:], q0)
    s1, s2 = swap_z(states, 1), swap_z(states, 2)
    xb, yb, s1, s2, f0 = fence(xb, yb, s1, s2, f0)
    f2a, s3 = swap_z(f0[:3], 2), swap_z(s2, 1)
    xc, yc = on_x(yb[:3], yb[9:11]), on_y(xb[3:6], xb[11:])
    qc = swap_dp(jnp.concatenate([q0, xb[9:], yb[9:]]), CORE)
    f2a, s3, xc, yc, qc, f0 = fence(f2a, s3, xc, yc, qc, f0)
    f2b, f3a = swap_z(f0[3:], 2), swap_z(f2a, 1)
    f2ax, f2ay = on_x(f2a), on_y(f2a)
    qd = swap_dp(jnp.concatenate([xc[3:], yc[3:]]), CORE)
    sources = [q0, xb, yb, xc, yc, qc, qd]
    plan = []
    for mc, (own, own_at, on_x_, x_at, on_y_, y_at, cross0, at0, cross1, at1) in enumerate(
        ((0, 0, 1, 9, 2, 9, 3, 3, 4, 3), (5, 0, 5, 4, 5, 8, 6, 0, 6, 2))
    ):
        for zz in range(4):
            plan.append(((0, 0, mc), own, own_at + zz, zz))
            plan.append(((0, 1, mc), on_x_, x_at + zz, zz))
            plan.append(((1, 0, mc), on_y_, y_at + zz, zz))
            if zz < 2:
                plan.append(((1, 1, mc), cross0, at0 + zz, zz))
            else:
                plan.append(((1, 1, mc), cross1, at1 + zz - 2, zz))
    full_output, full_qkv, vectors = place(
        sources, plan, jnp.stack([y, x, c]).astype(jnp.int32),
        [(width, 0, width), (half - width - 256, width, half - width - 256), (256, half - 256, 256)],
    )
    vectors = vectors[:, :, :, :, :2].reshape(2, 2, 2, 4, 512)
    full_output = full_output.reshape(width, width)
    full_qkv = full_qkv.reshape(width, -1)
    full_gain, full_astep, full_uscale, full_gscale, full_mstep, full_lengths = (
        vectors[..., a:b].astype(f32) for a, b in zip(cuts[:-1], cuts[1:])
    )
    count = jnp.sum(full_lengths[:, :, :, 0] * jnp.array([64.0, 1.0], f32))
    astep = full_astep.reshape(width)
    mstep = full_mstep.reshape(width)
    scale_up = pick(full_uscale, c, 2).reshape(-1)
    scale_gate = pick(full_gscale, c, 2).reshape(-1)
    gain = pick(full_gain.reshape(4, 1, heads_width), z)
    pieces = (states, s1, s2, s3)
    gains = [gain[:, a * HD : b * HD] for a, b in GROUPS]
    qkv0, qkv1 = project(line, pieces, full_qkv)
    qkv0, qkv1, f2b, f2ax, f2ay, f3a = fence(qkv0, qkv1, f2b, f2ax, f2ay, f3a)
    f3b = swap_z(f2b, 1)
    f2bx, f2by, f3ax, f3ay = on_x(f2b), on_y(f2b), on_x(f3a), on_y(f3a)
    mixed0, heads0, qa0, ka0, va0 = attend(qkv0, gains[0], lengths)
    heads0, f3b, f2bx, f2by, f3ax, f3ay, qkv1 = fence(heads0, f3b, f2bx, f2by, f3ax, f3ay, qkv1)
    parts0 = exchange(heads0.reshape(4, local, -1))
    f3bx, f3by, f2ac, f2bc = on_x(f3b), on_y(f3b), on_x(f2ay), on_y(f2bx)
    mixed1, heads1, qa1, ka1, va1 = attend(qkv1, gains[1], lengths)
    heads1, f3bx, f3by, f2ac, f2bc, parts0 = fence(heads1, f3bx, f3by, f2ac, f2bc, parts0)
    parts1 = exchange(heads1.reshape(4, local, -1))
    f3ac, f3bc = on_x(f3ay), on_y(f3bx)
    sources = [f0, f0x, f0y, f1, xb, yb, xc, yc]
    sources += [f2a, f2ax, f2ay, f2ac, f2b, f2bx, f2by, f2bc, f3a, f3ax, f3ay, f3b, f3bx, f3by]
    chips = ((0, 0), (0, 1), (1, 0), (1, 1))
    spots = {
        (0, 0): ((0, 0), (1, 0), (2, 0), (4, 6)),
        (0, 1): ((0, 3), (1, 3), (2, 3), (5, 6)),
        (1, 0): ((3, 0), (4, 0), (5, 0), (6, 0)),
        (1, 1): ((3, 3), (4, 3), (5, 3), (7, 0)),
        (2, 0): ((8, 0), (9, 0), (10, 0), (11, 0)),
        (2, 1): ((12, 0), (13, 0), (14, 0), (15, 0)),
        (3, 0): ((16, 0), (17, 0), (18, 0)),
        (3, 1): ((19, 0), (20, 0), (21, 0)),
    }
    plan = [
        (key + (mz,), array, plane, core)
        for (mz, core), arrays in spots.items()
        for key, (array, plane) in zip(chips, arrays)
    ]
    weights = spread(sources, plan, chip, width)
    weights, f3ac, f3bc, parts1 = fence(weights, f3ac, f3bc, parts1)
    full_up, full_gate, full_down = spread_last(weights, (f3ac, f3bc), (1, 1, 3), chip)
    mixed_low = jnp.concatenate([parts0, parts1], -1).transpose(1, 0, 2).reshape(local, width)
    branch = matmul(mixed_low, full_output)
    resid = states.astype(f32)
    branch_norm = normalize(branch)
    first = resid + astep * (branch_norm - resid)
    middle = normalize(first)
    middle_low = middle.astype(low)
    middle_other = swap_dp(middle_low, CORE)

    flat_up, flat_gate = scale_up.reshape(1, -1), scale_gate.reshape(1, -1)
    upper, gating, hidden, lower, lower_other, turned = ff_forward(
        middle_low, middle_other, full_up, full_gate, full_down, flat_up, flat_gate
    )
    final, d_lower, d_middle, grad_mstep, err_sums = loss_back(
        (lengths - z * local).astype(jnp.int32),
        (loss_scale * 2.0 / count).reshape(1),
        lower,
        swap_dp(lower_other, CORE),
        middle,
        teacher.reshape(local, width),
        mstep.reshape(1, width),
    )
    err_local = jnp.sum(err_sums)
    d_lower_other = swap_dp(d_lower, CORE)
    downs = cells(down_back(chip, hidden, d_lower, d_lower_other))
    downs[0].corner, downs[1].corner, d_lower, d_lower_other = fence(downs[0].corner, downs[1].corner, d_lower, d_lower_other)
    down_corner = [p.first(p.corner) for p in downs]
    down_side = [p.first(p.side) for p in downs]
    d_up, d_gate, grad_uscale, grad_gscale = hidden_back(
        d_lower, d_lower_other, full_down, upper, gating, flat_up, flat_gate
    )
    d_up, d_gate, down_corner = fence(d_up, d_gate, down_corner)
    down_relay = [p.second(v) for p, v in zip(downs, down_corner)]
    ups = cells(wide_back(chip, turned, d_up))
    ups[0].corner, ups[1].corner, down_side, d_up, d_gate = fence(ups[0].corner, ups[1].corner, down_side, d_up, d_gate)
    up_corner = [p.first(p.corner) for p in ups]
    d_both, d_both_other = middle_back(d_up, d_gate, full_up, full_gate)
    down_relay, d_both, d_both_other, ups[0].side, ups[1].side = fence(
        down_relay, d_both, d_both_other, ups[0].side, ups[1].side
    )
    up_side = [p.first(p.side) for p in ups]
    input_grad, d_branch, grad_astep = branch_back(
        d_middle, d_both, swap_dp(d_both_other, CORE), branch, states, astep.reshape(1, width)
    )
    d_mixed = right_tdot(d_branch, full_output).astype(low)
    blocks = d_mixed.reshape(local, 4, heads_width).transpose(1, 0, 2)
    blocks = [blocks[:, :, a * HD : b * HD] for a, b in GROUPS]
    scales = jnp.concatenate([grad_uscale.reshape(2, 2, 4, hidden_share), grad_gscale.reshape(2, 2, 4, hidden_share)], -1)
    scales = jnp.where((jnp.arange(2) == c)[None, None, :, None, None], scales[:, :, None], 0.0).reshape(32, -1)
    packed = jnp.concatenate(
        [grad_astep.reshape(32, share), scales, grad_mstep.reshape(32, share), jnp.full((32, 1), err_local)], 1
    )
    packed = jnp.pad(packed, ((0, 0), (0, 512 - packed.shape[1]))).reshape(2, 2, 2, 4, 4, 128)
    packed = pick(packed, c, 2) + swap_dp(pick(packed, 1 - c, 2), CORE)
    down = jnp.concatenate([p.total(v, r) for p, v, r in zip(downs, down_side, down_relay)], 1)
    down = down.reshape(4, hidden_share, width)
    blocks, d_branch, d_gate, up_corner, packed, down = fence(blocks, d_branch, d_gate, up_corner, packed, down)
    parts0 = exchange(blocks[0])
    up_relay = [p.second(v) for p, v in zip(ups, up_corner)]
    gates = cells(wide_back(chip, turned, d_gate))
    down_far = swap_z(pick(down, z ^ 3), 1)
    parts0, up_relay, up_side, gates[0].corner, gates[1].corner, block1, d_branch, packed = fence(
        parts0, up_relay, up_side, gates[0].corner, gates[1].corner, blocks[1], d_branch, packed
    )
    packed = pick(packed, x, 1) + swap_dp(pick(packed, 1 - x, 1), XAX)
    gate_corner = [p.first(p.corner) for p in gates]
    up = jnp.stack([p.total(v, r) for p, v, r in zip(ups, up_side, up_relay)]).reshape(2, 4, share, hidden_half)
    down_far, down_near = swap_z(add_low(pick(down, z ^ 2), down_far), 2), swap_z(pick(down, z ^ 1), 1)
    g_out = left_tdot(mixed_low, d_branch).astype(low).reshape(2, 2, 2, 2, 2 * share, width)
    out_c = swap_dp(pick(g_out, 1 - c, 2), CORE)
    g_out = add_low(pick(g_out, c, 2), out_c)
    parts0, gate_corner, up, g_out, gates[0].side, gates[1].side, down_near, packed = fence(
        parts0, gate_corner, up, g_out, gates[0].side, gates[1].side, down_near, packed
    )
    parts1 = exchange(block1)
    gate_side = [p.first(p.side) for p in gates]
    gate_relay = [p.second(v) for p, v in zip(gates, gate_corner)]
    up_far = swap_z(pick(up, z ^ 3, 1), 1)
    d_heads0 = parts0.reshape(tokens, -1)
    d_qkv0, gain_grad0 = attend_back(qkv0, gains[0], lengths, mixed0, d_heads0, qa0, ka0, va0)
    d_qkv0, gain_grad0, parts1, gate_side, gate_relay, up_far, up, packed, down_far = fence(
        d_qkv0, gain_grad0, parts1, gate_side, gate_relay, up_far, up, packed, down_far
    )
    gate = jnp.stack([p.total(v, r) for p, v, r in zip(gates, gate_side, gate_relay)]).reshape(2, 4, share, hidden_half)
    up_far, up_near = swap_z(add_low(pick(up, z ^ 2, 1), up_far), 2), swap_z(pick(up, z ^ 1, 1), 1)
    gate_far, gate_near = swap_z(pick(gate, z ^ 3, 1), 1), swap_z(pick(gate, z ^ 1, 1), 1)
    packed = pick(packed, y) + swap_dp(pick(packed, 1 - y), YAX)
    d_heads1 = parts1.reshape(tokens, -1)
    d_qkv1, gain_grad1 = attend_back(qkv1, gains[1], lengths, mixed1, d_heads1, qa1, ka1, va1)
    d_qkv1, gain_grad1, gate, up_far, up_near, gate_far, gate_near, d_qkv0, packed = fence(
        d_qkv1, gain_grad1, gate, up_far, up_near, gate_far, gate_near, d_qkv0, packed
    )
    (states_send,) = states_back(line, d_qkv0, d_qkv1, full_qkv, local, (3,))
    gate_send = add_low(pick(gate, z ^ 2, 1), gate_far)
    states_send, gate_send, gate, packed, d_qkv0, d_qkv1 = fence(states_send, gate_send, gate, packed, d_qkv0, d_qkv1)
    states_relay = swap_z(states_send, 1)
    gate_far = swap_z(gate_send, 2)
    pair = swap_z(jnp.stack([pick(packed, z ^ 2), pick(packed, z ^ 3)]), 2)
    packed = jnp.stack([pick(packed, z), pick(packed, z ^ 1)]) + pair
    states_far, states_near, states_own = states_back(line, d_qkv0, d_qkv1, full_qkv, local, (2, 1, 0))
    grad_gain = jnp.concatenate([gain_grad0, gain_grad1], 1).reshape(-1)
    gain_all = lax.dynamic_update_slice(jnp.zeros((4 * heads_width,), f32), grad_gain, (z * heads_width,))
    spare = COLS[0] + 3 * (GROUPS[0][1] - GROUPS[0][0]) * HD
    qkv_keep, qkv_send = rows_back(
        jnp.stack([y, x, c, z]).astype(jnp.int32), pieces, d_qkv0, d_qkv1, gain_all.reshape(width, 1), spare
    )
    states_relay, qkv_send, qkv_keep, states_far, states_near, states_own, packed, gate_far = fence(
        states_relay, qkv_send, qkv_keep, states_far, states_near, states_own, packed, gate_far
    )
    states_far = swap_z(add_low(states_far, states_relay), 2)
    states_near = swap_z(states_near, 1)
    qkv_sum = add_low(qkv_keep, swap_dp(qkv_send, CORE))
    out_sum = [lax.dynamic_slice(g_out, (y ^ (at // 2), x ^ (at % 2), 0, 0, 0), (1, 1) + g_out.shape[2:]) for at in range(4)]
    out_sum = [v.reshape(2 * 2 * share, width) for v in out_sum]
    cell = lambda at, unit: jnp.concatenate(
        [v[2 * share * unit : 2 * share * (unit + 1)] for v in (qkv_sum[at], out_sum[at])], 1
    )
    rows = [Cells((cell(3, u), cell(1 + u, u), cell(2 - u, u), cell(0, u)), u == 0) for u in range(2)]
    row_far = [p.first(jnp.stack([p.side, p.corner])) for p in rows]
    packed = packed[0] + swap_z(packed[1], 1)
    own_rows = total3(pick(up, z, 1), up_near, up_far), total3(pick(gate, z, 1), gate_near, gate_far)
    own_rows = jnp.stack(own_rows, 1)
    own_part, other_part = pick(own_rows, c), swap_dp(pick(own_rows, 1 - c), CORE)
    down_grad = total3(pick(down, z), down_near, down_far).reshape(hidden_share, width)
    row_relay = [p.second(v[1]) for p, v in zip(rows, row_far)]
    up_grad, gate_grad = interleave(c, own_part, other_part)
    rows_sum = jnp.stack([p.total(v[0], r) for p, v, r in zip(rows, row_far, row_relay)]).reshape(4, share, three + width)
    columns = exchange(rows_sum)
    packed = packed.reshape(512)
    output_grad = jnp.sum(columns[..., three:].astype(f32), 0)
    columns_cut = [
        columns[..., at : at + 3 * (b - a) * HD].reshape(4, share, 3, -1) for (a, b), at in zip(GROUPS, COLS)
    ]
    score_gain_grad = jnp.sum(columns[..., spare].astype(f32), 0)
    columns = jnp.concatenate(columns_cut, -1).transpose(2, 1, 0, 3).reshape(3, share, width).astype(f32)
    columns, output_grad, score_gain_grad, input_grad, states_far, states_near, up_grad, gate_grad, down_grad = fence(
        columns, output_grad, score_gain_grad, input_grad, states_far, states_near, up_grad, gate_grad, down_grad
    )
    input_grad = input_grad + total3(states_own, states_near, states_far)
    return (
        final[None],
        packed[cuts[5] - cuts[1]] / count,
        input_grad[None],
        columns[0],
        columns[1],
        columns[2],
        output_grad,
        score_gain_grad,
        packed[: cuts[1]],
        up_grad,
        gate_grad,
        down_grad,
        packed[cuts[2] - cuts[1] : cuts[3] - cuts[1]],
        packed[cuts[3] - cuts[1] : cuts[4] - cuts[1]],
        packed[cuts[4] - cuts[1] : cuts[5] - cuts[1]],
    )


def per_device(
    inputs,
    teacher,
    lengths,
    query_weight,
    key_weight,
    value_projection,
    output_weight,
    score_gain,
    attention_step,
    up_weight,
    gate_weight,
    down_weight,
    up_scale,
    gate_scale,
    swiglu_step,
):
    seqs, local, width = inputs.shape
    full_len = local * lax.axis_size("ctx")
    rows = seqs * local
    heads = width // HD
    key_block = min(512, full_len)
    query_pos = lax.axis_index("ctx") * local + jnp.arange(local, dtype=jnp.int32)
    valid = (query_pos[None, :] < lengths[:, None]).astype(jnp.float32).reshape(rows, 1)
    count_local = jnp.sum(valid)
    full_query, full_key, full_value, full_output, full_gain, full_astep = (
        lax.all_gather(query_weight, ("dp", "ctx"), axis=0, tiled=True),
        lax.all_gather(key_weight, ("dp", "ctx"), axis=0, tiled=True),
        lax.all_gather(value_projection, ("dp", "ctx"), axis=0, tiled=True),
        lax.all_gather(output_weight, ("dp", "ctx"), axis=0, tiled=True),
        lax.all_gather(score_gain, ("dp", "ctx"), axis=0, tiled=True),
        lax.all_gather(attention_step, ("dp", "ctx"), axis=0, tiled=True),
    )
    states = inputs.reshape(rows, width)
    resid = states.astype(jnp.float32)
    queries = matmul(states, full_query)
    keys_raw = matmul(states, full_key)
    values_raw = matmul(states, full_value)
    gains = full_gain.astype(jnp.float32).reshape(heads, HD)
    query_norm = normalize(queries.reshape(rows, heads, HD))
    key_norm = normalize(keys_raw.reshape(rows, heads, HD))
    q_heads = (gains * query_norm).astype(jnp.bfloat16).reshape(seqs, local, heads, HD)
    k_flat = (gains * key_norm).astype(jnp.bfloat16).reshape(seqs, local, width)
    v_flat = values_raw.astype(jnp.bfloat16).reshape(seqs, local, width)

    def key_step(carry, key_piece, value_piece, key_pos):
        top, total, accum = carry
        count_keys = key_piece.shape[1]
        scores, allowed = block_scores(
            q_heads, key_piece.reshape(seqs, count_keys, heads, HD), query_pos, key_pos, lengths
        )
        scores = jnp.where(allowed, scores, -1e30)
        top_new = jnp.maximum(top, jnp.max(scores, axis=-1))
        weights = jnp.where(allowed, jnp.exp(scores - top_new[..., None]), 0.0)
        factor = jnp.exp(top - top_new)
        total = total * factor + jnp.sum(weights, axis=-1)
        accum = accum * jnp.transpose(factor, (0, 2, 1))[..., None] + jnp.einsum(
            "shqk,skhd->sqhd",
            weights.astype(jnp.bfloat16),
            value_piece.reshape(seqs, count_keys, heads, HD),
            preferred_element_type=jnp.float32,
        )
        return (top_new, total, accum)

    init = (
        jnp.full((seqs, heads, local), -1e30, jnp.float32),
        jnp.zeros((seqs, heads, local), jnp.float32),
        jnp.zeros((seqs, local, heads, HD), jnp.float32),
    )
    carry = init
    key_piece = lax.all_gather(k_flat, "ctx", axis=1, tiled=True)
    value_piece = lax.all_gather(v_flat, "ctx", axis=1, tiled=True)
    count_keys = key_piece.shape[1]

    def inner(state, index):
        offset = index * key_block
        key_part = lax.dynamic_slice_in_dim(key_piece, offset, key_block, 1)
        value_part = lax.dynamic_slice_in_dim(value_piece, offset, key_block, 1)
        positions = offset + jnp.arange(key_block, dtype=jnp.int32)
        return (key_step(state, key_part, value_part, positions), None)

    carry, unused = lax.scan(inner, carry, jnp.arange(count_keys // key_block, dtype=jnp.int32))
    top, total, accum = carry
    mixed = accum / jnp.transpose(total, (0, 2, 1))[..., None]
    log_total = top + jnp.log(total)
    mixed_low = mixed.reshape(rows, width).astype(jnp.bfloat16)
    branch = matmul(mixed_low, full_output)
    branch_norm = normalize(branch)
    astep = full_astep.astype(jnp.float32)
    first = resid + astep * (branch_norm - resid)
    middle = normalize(first)
    middle_low = middle.astype(jnp.bfloat16)
    full_up, full_gate, full_down, full_uscale, complete_gate_scale, full_mstep = (
        lax.all_gather(up_weight, ("dp", "ctx"), axis=0, tiled=True),
        lax.all_gather(gate_weight, ("dp", "ctx"), axis=0, tiled=True),
        lax.all_gather(down_weight, ("dp", "ctx"), axis=0, tiled=True),
        lax.all_gather(up_scale, ("dp", "ctx"), axis=0, tiled=True),
        lax.all_gather(gate_scale, ("dp", "ctx"), axis=0, tiled=True),
        lax.all_gather(swiglu_step, ("dp", "ctx"), axis=0, tiled=True),
    )
    upper = matmul(middle_low, full_up)
    gating = matmul(middle_low, full_gate)
    scale_up = full_uscale.astype(jnp.float32)
    scale_gate = complete_gate_scale.astype(jnp.float32)
    upper_scaled = upper * scale_up
    gate_arg = gating * scale_gate
    gate_act = jax.nn.silu(gate_arg)
    hidden = (upper_scaled * gate_act).astype(jnp.bfloat16)
    lower = matmul(hidden, full_down)
    lower_norm = normalize(lower)
    mstep = full_mstep.astype(jnp.float32)
    second = middle + mstep * (lower_norm - middle)
    final = normalize(second)
    target = teacher.reshape(rows, width).astype(jnp.float32)
    diff = final - target
    err_local = jnp.sum(valid * diff * diff)
    err_total, count = lax.psum((err_local, count_local), ("dp", "ctx"))
    cot = loss_scale * 2.0 / count * valid * diff
    full_up, full_gate, full_down, full_uscale, complete_gate_scale, full_mstep = (
        lax.all_gather(up_weight, ("dp", "ctx"), axis=0, tiled=True),
        lax.all_gather(gate_weight, ("dp", "ctx"), axis=0, tiled=True),
        lax.all_gather(down_weight, ("dp", "ctx"), axis=0, tiled=True),
        lax.all_gather(up_scale, ("dp", "ctx"), axis=0, tiled=True),
        lax.all_gather(gate_scale, ("dp", "ctx"), axis=0, tiled=True),
        lax.all_gather(swiglu_step, ("dp", "ctx"), axis=0, tiled=True),
    )
    d_second = norm_back(second, final, cot)
    d_middle = d_second * (1.0 - mstep)
    grad_mstep = jnp.sum(d_second * (lower_norm - middle), axis=0)
    d_lower = norm_back(lower, lower_norm, d_second * mstep).astype(jnp.bfloat16)
    grad_down = left_tdot(hidden, d_lower)
    d_hidden = right_tdot(d_lower, full_down)
    d_upper = d_hidden * gate_act
    sigmoid_gate = jax.nn.sigmoid(gate_arg)
    d_gate_arg = d_hidden * upper_scaled * (sigmoid_gate * (1.0 + gate_arg * (1.0 - sigmoid_gate)))
    grad_uscale = jnp.sum(d_upper * upper, axis=0)
    grad_gscale = jnp.sum(d_gate_arg * gating, axis=0)
    d_up_low = (d_upper * scale_up).astype(jnp.bfloat16)
    d_gate_low = (d_gate_arg * scale_gate).astype(jnp.bfloat16)
    d_middle = d_middle + right_tdot(d_up_low, full_up) + right_tdot(d_gate_low, full_gate)
    grad_up = left_tdot(middle_low, d_up_low)
    grad_gate = left_tdot(middle_low, d_gate_low)
    up_grad, gate_grad, down_grad, up_scale_grad, gate_scale_gradient, swiglu_step_grad = (
        lax.psum_scatter(grad_up, ("dp", "ctx"), scatter_dimension=0, tiled=True),
        lax.psum_scatter(grad_gate, ("dp", "ctx"), scatter_dimension=0, tiled=True),
        lax.psum_scatter(grad_down, ("dp", "ctx"), scatter_dimension=0, tiled=True),
        lax.psum_scatter(grad_uscale, ("dp", "ctx"), scatter_dimension=0, tiled=True),
        lax.psum_scatter(grad_gscale, ("dp", "ctx"), scatter_dimension=0, tiled=True),
        lax.psum_scatter(grad_mstep, ("dp", "ctx"), scatter_dimension=0, tiled=True),
    )
    d_first = norm_back(first, middle, d_middle)
    input_grad = d_first * (1.0 - astep)
    grad_astep = jnp.sum(d_first * (branch_norm - resid), axis=0)
    d_branch = norm_back(branch, branch_norm, d_first * astep).astype(jnp.bfloat16)
    full_query, full_key, full_value, full_output, full_gain, full_astep = (
        lax.all_gather(query_weight, ("dp", "ctx"), axis=0, tiled=True),
        lax.all_gather(key_weight, ("dp", "ctx"), axis=0, tiled=True),
        lax.all_gather(value_projection, ("dp", "ctx"), axis=0, tiled=True),
        lax.all_gather(output_weight, ("dp", "ctx"), axis=0, tiled=True),
        lax.all_gather(score_gain, ("dp", "ctx"), axis=0, tiled=True),
        lax.all_gather(attention_step, ("dp", "ctx"), axis=0, tiled=True),
    )
    gains = full_gain.astype(jnp.float32).reshape(heads, HD)
    grad_output = left_tdot(mixed_low, d_branch)
    d_mixed = right_tdot(d_branch, full_output).astype(jnp.bfloat16)
    d_mixed_heads = d_mixed.reshape(seqs, local, heads, HD)
    delta = jnp.transpose(jnp.sum(d_mixed_heads.astype(jnp.float32) * mixed, axis=-1), (0, 2, 1))
    whole_keys, whole_values = (
        lax.all_gather(k_flat, "ctx", axis=1, tiled=True),
        lax.all_gather(v_flat, "ctx", axis=1, tiled=True),
    )

    def query_terms(index):
        offset = index * key_block
        key_part = lax.dynamic_slice_in_dim(whole_keys, offset, key_block, 1).reshape(
            seqs, key_block, heads, HD
        )
        value_part = lax.dynamic_slice_in_dim(whole_values, offset, key_block, 1).reshape(
            seqs, key_block, heads, HD
        )
        key_pos = offset + jnp.arange(key_block, dtype=jnp.int32)
        scores, allowed = block_scores(q_heads, key_part, query_pos, key_pos, lengths)
        probs = jnp.where(allowed, jnp.exp(scores - log_total[..., None]), 0.0)
        d_probs = jnp.einsum(
            "sqhd,skhd->shqk", d_mixed_heads, value_part, preferred_element_type=jnp.float32
        )
        d_scores = (probs * (d_probs - delta[..., None])).astype(jnp.bfloat16)
        d_query_part = jnp.einsum(
            "shqk,skhd->sqhd", d_scores, key_part, preferred_element_type=jnp.float32
        )
        return (offset, probs, d_scores, d_query_part)

    def key_back(carry, index):
        d_query_acc, d_key_all, d_value_all = carry
        offset, probs, d_scores, d_query_part = query_terms(index)
        d_query_acc = d_query_acc + d_query_part
        d_key_part = jnp.einsum(
            "shqk,sqhd->skhd", d_scores, q_heads, preferred_element_type=jnp.float32
        ) * HD ** (-0.5)
        d_value_part = jnp.einsum(
            "shqk,sqhd->skhd",
            probs.astype(jnp.bfloat16),
            d_mixed_heads,
            preferred_element_type=jnp.float32,
        )
        d_key_all = lax.dynamic_update_slice_in_dim(
            d_key_all, d_key_part.reshape(seqs, key_block, width), offset, 1
        )
        d_value_all = lax.dynamic_update_slice_in_dim(
            d_value_all, d_value_part.reshape(seqs, key_block, width), offset, 1
        )
        return ((d_query_acc, d_key_all, d_value_all), None)

    start_carry = (
        jnp.zeros((seqs, local, heads, HD), jnp.float32),
        jnp.zeros((seqs, full_len, width), jnp.float32),
        jnp.zeros((seqs, full_len, width), jnp.float32),
    )
    (d_query_heads, d_key_all, d_value_all), unused = lax.scan(
        key_back, start_carry, jnp.arange(full_len // key_block, dtype=jnp.int32)
    )
    d_key_local, d_value_local = (
        lax.psum_scatter(
            d_key_all.astype(jnp.bfloat16), "ctx", scatter_dimension=1, tiled=True
        ).astype(jnp.float32),
        lax.psum_scatter(
            d_value_all.astype(jnp.bfloat16), "ctx", scatter_dimension=1, tiled=True
        ).astype(jnp.float32),
    )
    d_key_heads = d_key_local.reshape(rows, heads, HD)
    d_value_local = d_value_local.reshape(rows, width)
    d_query_heads = (d_query_heads * HD ** (-0.5)).reshape(rows, heads, HD)
    grad_gain = jnp.sum(d_query_heads * query_norm, axis=0) + jnp.sum(
        d_key_heads * key_norm, axis=0
    )
    d_query_low = (
        norm_back(queries.reshape(rows, heads, HD), query_norm, d_query_heads * gains)
        .reshape(rows, width)
        .astype(jnp.bfloat16)
    )
    d_key_low = (
        norm_back(keys_raw.reshape(rows, heads, HD), key_norm, d_key_heads * gains)
        .reshape(rows, width)
        .astype(jnp.bfloat16)
    )
    d_value_low = d_value_local.astype(jnp.bfloat16)
    input_grad = (
        input_grad
        + right_tdot(d_query_low, full_query)
        + right_tdot(d_key_low, full_key)
        + right_tdot(d_value_low, full_value)
    )
    grad_query = left_tdot(states, d_query_low)
    grad_key = left_tdot(states, d_key_low)
    grad_value = left_tdot(states, d_value_low)
    query_grad, key_grad, value_grad, output_grad, score_gain_grad, attention_step_grad = (
        lax.psum_scatter(grad_query, ("dp", "ctx"), scatter_dimension=0, tiled=True),
        lax.psum_scatter(grad_key, ("dp", "ctx"), scatter_dimension=0, tiled=True),
        lax.psum_scatter(grad_value, ("dp", "ctx"), scatter_dimension=0, tiled=True),
        lax.psum_scatter(grad_output, ("dp", "ctx"), scatter_dimension=0, tiled=True),
        lax.psum_scatter(grad_gain.reshape(width), ("dp", "ctx"), scatter_dimension=0, tiled=True),
        lax.psum_scatter(grad_astep, ("dp", "ctx"), scatter_dimension=0, tiled=True),
    )
    distill_loss_mean = err_total / count
    layer_out = final.astype(jnp.bfloat16).reshape(seqs, local, width)
    return (
        layer_out,
        distill_loss_mean,
        input_grad.reshape(seqs, local, width),
        query_grad,
        key_grad,
        value_grad,
        output_grad,
        score_gain_grad,
        attention_step_grad,
        up_grad,
        gate_grad,
        down_grad,
        up_scale_grad,
        gate_scale_gradient,
        swiglu_step_grad,
    )


def solution(mesh):
    placed = (
        P("dp", "ctx", None),
        P("dp", "ctx", None),
        P("dp"),
        P(("dp", "ctx"), None),
        P(("dp", "ctx"), None),
        P(("dp", "ctx"), None),
        P(("dp", "ctx"), None),
        P(("dp", "ctx")),
        P(("dp", "ctx")),
        P(("dp", "ctx"), None),
        P(("dp", "ctx"), None),
        P(("dp", "ctx"), None),
        P(("dp", "ctx")),
        P(("dp", "ctx")),
        P(("dp", "ctx")),
    )
    on_one = on_cores if dict(mesh.shape) == {"dp": 8, "ctx": 4} else per_device
    return jax.shard_map(
        on_one,
        mesh=mesh,
        in_specs=placed,
        out_specs=(
            P("dp", "ctx", None),
            P(),
            P("dp", "ctx", None),
            P(("dp", "ctx"), None),
            P(("dp", "ctx"), None),
            P(("dp", "ctx"), None),
            P(("dp", "ctx"), None),
            P(("dp", "ctx")),
            P(("dp", "ctx")),
            P(("dp", "ctx"), None),
            P(("dp", "ctx"), None),
            P(("dp", "ctx"), None),
            P(("dp", "ctx")),
            P(("dp", "ctx")),
            P(("dp", "ctx")),
        ),
        check_vma=False,
    )
```

```python
import functools

import jax
import jax.numpy as jnp
from jax import lax
from jax.experimental import pallas as pl
from jax.experimental.pallas import tpu as pltpu
from jax.sharding import PartitionSpec as P

HD = 64


eps = 1e-06
loss_scale = 32768.0


def normalize(value_rows):
    return value_rows * lax.rsqrt(jnp.mean(value_rows * value_rows, axis=-1, keepdims=True) + eps)


def norm_back(value_rows, normed, grad):
    factor = lax.rsqrt(jnp.mean(value_rows * value_rows, axis=-1, keepdims=True) + eps)
    return factor * (grad - normed * jnp.mean(grad * normed, axis=-1, keepdims=True))


def matmul(left, right):
    return jnp.dot(left, right, preferred_element_type=jnp.float32)


def left_tdot(left, right):
    return lax.dot_general(
        left, right, (((0,), (0,)), ((), ())), preferred_element_type=jnp.float32
    )


def right_tdot(left, right):
    return lax.dot_general(
        left, right, (((1,), (1,)), ((), ())), preferred_element_type=jnp.float32
    )


def block_scores(queries, keys, query_pos, key_pos, lens):
    scores = jnp.einsum(
        "sqhd,skhd->shqk", queries, keys, preferred_element_type=jnp.float32
    ) * HD ** (-0.5)
    allowed = (key_pos[None, None, :] <= query_pos[None, :, None]) & (
        key_pos[None, None, :] < lens[:, None, None]
    )
    return (scores, allowed[:, None])


BLK = 512
LANES = 128


def same_head(size, value):
    rows = lax.broadcasted_iota(jnp.int32, (size, size), 0) // HD
    cols = lax.broadcasted_iota(jnp.int32, (size, size), 1) // HD
    return jnp.where(rows == cols, value, 0.0).astype(jnp.bfloat16)


def over_heads(v, matrix):
    hi = v.astype(jnp.bfloat16)
    low = (v - hi.astype(jnp.float32)).astype(jnp.bfloat16)
    return jnp.dot(hi, matrix, preferred_element_type=jnp.float32) + jnp.dot(low, matrix, preferred_element_type=jnp.float32)


def split3(v):
    hi = v.astype(jnp.bfloat16)
    rest = v - hi.astype(jnp.float32)
    mid = rest.astype(jnp.bfloat16)
    low = (rest - mid.astype(jnp.float32)).astype(jnp.bfloat16)
    return hi, mid, low


def attend_kernel(heads, length_ref, qkv_ref, gain_ref, mixed_ref, low_ref, qa_ref, ka_ref, va_ref, out_ref):
    tokens = qkv_ref.shape[0]
    width = heads * HD
    length = length_ref[0]
    lane = lax.broadcasted_iota(jnp.int32, (BLK, HD), 1)

    mean = same_head(2 * width, 1.0 / HD)
    gains = jnp.concatenate([gain_ref[...], gain_ref[...]], axis=1)

    def prepare(block, carry):
        start = pl.multiple_of(block * BLK, BLK)
        rows = pl.ds(start, BLK)
        inside = (lax.broadcasted_iota(jnp.int32, (BLK, 1), 0) + start < length).astype(jnp.float32)
        ones = jnp.where(lane < 3, inside, 0.0).astype(jnp.bfloat16)
        nothing = jnp.zeros((BLK, HD), jnp.bfloat16)
        raw = qkv_ref[rows, : 2 * width]
        scaled = gains * (raw * lax.rsqrt(over_heads(raw * raw, mean) + eps))
        qs = scaled[:, :width].astype(jnp.bfloat16) * jnp.bfloat16(HD**-0.5)
        ks = (scaled[:, width:] * inside).astype(jnp.bfloat16)
        vs = (qkv_ref[rows, 2 * width : 3 * width] * inside).astype(jnp.bfloat16)
        for head in range(heads):
            cols = slice(head * HD, (head + 1) * HD)
            qa_ref[head, rows, :] = jnp.concatenate([qs[:, cols], nothing], axis=1)
            ka_ref[head, rows, :] = jnp.concatenate([ks[:, cols], ones], axis=1)
            va_ref[head, rows, :] = jnp.concatenate([vs[:, cols], ones], axis=1)
        return carry

    lax.fori_loop(0, tokens // BLK, prepare, 0)
    part = BLK // 2
    place = lax.broadcasted_iota(jnp.int32, (BLK, part), 0) - lax.broadcasted_iota(jnp.int32, (BLK, part), 1)

    def per_head(head, carry):
        for qi in range(tokens // BLK):
            rows = pl.ds(qi * BLK, BLK)
            q = qa_ref[head, rows, :]
            acc = jnp.zeros((BLK, LANES), jnp.float32)
            for ki in range(2 * (qi + 1)):
                keys = pl.ds(ki * part, part)
                scores = lax.dot_general(
                    q, ka_ref[head, keys, :], (((1,), (1,)), ((), ())), preferred_element_type=jnp.float32
                )
                weights = jnp.exp(scores)
                if ki >= 2 * qi:
                    weights = jnp.where(place >= (ki - 2 * qi) * part, weights, 0.0)
                acc = acc + jnp.dot(
                    weights.astype(jnp.bfloat16), va_ref[head, keys, :], preferred_element_type=jnp.float32
                )
            total = acc[:, HD : HD + 1]
            out_ref[head, rows, :] = acc / total
            hi, mid, low = split3(-jnp.log(total))
            extra = jnp.where(lane == 0, hi, jnp.where(lane == 1, mid, jnp.where(lane == 2, low, jnp.zeros_like(low))))
            qa_ref[head, rows, :] = jnp.concatenate([q[:, :HD], extra], axis=1)
        return carry

    lax.fori_loop(0, heads, per_head, 0)

    def finish(block, carry):
        rows = pl.ds(pl.multiple_of(block * BLK, BLK), BLK)
        whole = jnp.concatenate([out_ref[head, rows, :][:, :HD] for head in range(heads)], axis=1)
        mixed_ref[rows, :] = whole
        low_ref[rows, :] = whole.astype(jnp.bfloat16)
        return carry

    lax.fori_loop(0, tokens // BLK, finish, 0)


def attend(qkv, gain, length):
    tokens, width = qkv.shape[0], gain.shape[1]
    heads = width // HD
    vmem = pl.BlockSpec(memory_space=pltpu.VMEM)
    aug = jax.ShapeDtypeStruct((heads, tokens, LANES), jnp.bfloat16)
    return pl.pallas_call(
        functools.partial(attend_kernel, heads),
        out_shape=(
            jax.ShapeDtypeStruct((tokens, width), jnp.float32),
            jax.ShapeDtypeStruct((tokens, width), jnp.bfloat16),
            aug,
            aug,
            aug,
        ),
        in_specs=[pl.BlockSpec(memory_space=pltpu.SMEM), vmem, vmem],
        out_specs=(vmem,) * 5,
        scratch_shapes=[pltpu.VMEM((heads, tokens, LANES), jnp.float32)],
        compiler_params=pltpu.CompilerParams(vmem_limit_bytes=56 << 20),
        cost_estimate=pl.CostEstimate(
            flops=heads * tokens * tokens, bytes_accessed=8 << 20, transcendentals=0
        ),
        name="attend",
    )(length, qkv, gain)


def attend_back_kernel(
    heads, length_ref, qkv_ref, gain_ref, mixed_ref, cot_ref, qa_ref, ka_ref, va_ref,
    grads_ref, gain_grad_ref, doa_ref, dq_ref, dk_ref, dv_ref, raw_ref, sem,
):
    tokens = qkv_ref.shape[0]
    width = heads * HD
    length = length_ref[0]
    lane = lax.broadcasted_iota(jnp.int32, (BLK, HD), 1)
    raw_copy = pltpu.make_async_copy(qkv_ref.at[:, pl.ds(0, 2 * width)], raw_ref, sem)
    raw_copy.start()
    minus = same_head(width, -1.0)

    def prepare(block, carry):
        rows = pl.ds(pl.multiple_of(block * BLK, BLK), BLK)
        d_mixed = cot_ref[rows, :]
        hi, mid, low = split3(over_heads(d_mixed.astype(jnp.float32) * mixed_ref[rows, :], minus))
        for head in range(heads):
            cols = slice(head * HD, (head + 1) * HD)
            extra = jnp.where(
                lane == 0, hi[:, cols], jnp.where(lane == 1, mid[:, cols], jnp.where(lane == 2, low[:, cols], jnp.zeros_like(low[:, cols])))
            )
            doa_ref[head, rows, :] = jnp.concatenate([d_mixed[:, cols], extra], axis=1)
        return carry

    lax.fori_loop(0, tokens // BLK, prepare, 0)
    causal = lax.broadcasted_iota(jnp.int32, (BLK, BLK), 0) <= lax.broadcasted_iota(jnp.int32, (BLK, BLK), 1)

    def per_head(head, carry):
        for ki in range(tokens // BLK):
            keys = pl.ds(ki * BLK, BLK)
            k = ka_ref[head, keys, :]
            v = va_ref[head, keys, :]
            dk = jnp.zeros((BLK, LANES), jnp.float32)
            dv = jnp.zeros((BLK, LANES), jnp.float32)
            for qi in range(ki, tokens // BLK):
                rows = pl.ds(qi * BLK, BLK)
                q = qa_ref[head, rows, :]
                d_out = doa_ref[head, rows, :]
                scores = lax.dot_general(k, q, (((1,), (1,)), ((), ())), preferred_element_type=jnp.float32)
                probs = jnp.exp(scores)
                if ki == qi:
                    probs = jnp.where(causal, probs, 0.0)
                d_probs = lax.dot_general(v, d_out, (((1,), (1,)), ((), ())), preferred_element_type=jnp.float32)
                d_scores = (probs * d_probs).astype(jnp.bfloat16)
                dv = dv + jnp.dot(probs.astype(jnp.bfloat16), d_out, preferred_element_type=jnp.float32)
                dk = dk + jnp.dot(d_scores, q, preferred_element_type=jnp.float32)
                dq = lax.dot_general(d_scores, k, (((0,), (0,)), ((), ())), preferred_element_type=jnp.float32)
                if ki == 0:
                    dq_ref[head, rows, :] = dq
                else:
                    dq_ref[head, rows, :] += dq
            dk_ref[head, keys, :] = dk
            dv_ref[head, keys, :] = dv
        return carry

    lax.fori_loop(0, heads, per_head, 0)

    raw_copy.wait()
    mean = same_head(2 * width, 1.0 / HD)
    gains = jnp.concatenate([gain_ref[...], gain_ref[...]], axis=1)
    scale = jnp.where(lax.broadcasted_iota(jnp.int32, (1, 2 * width), 1) < width, HD**-0.5, 1.0)

    def finish(block, sums):
        start = pl.multiple_of(block * BLK, BLK)
        rows = pl.ds(start, BLK)
        inside = lax.broadcasted_iota(jnp.int32, (BLK, 1), 0) + start < length
        grad = jnp.concatenate([ref[head, rows, :][:, :HD] for ref in (dq_ref, dk_ref) for head in range(heads)], axis=1)
        grad = grad * scale
        raw = raw_ref[rows, :]
        factor = lax.rsqrt(over_heads(raw * raw, mean) + eps)
        normed = raw * factor
        scaled = grad * gains
        back = factor * (scaled - normed * over_heads(scaled * normed, mean))
        grads_ref[rows, : 2 * width] = back.astype(jnp.bfloat16)
        dv = jnp.concatenate([dv_ref[head, rows, :][:, :HD] for head in range(heads)], axis=1)
        grads_ref[rows, 2 * width : 3 * width] = jnp.where(inside, dv, 0.0).astype(jnp.bfloat16)
        rest = grads_ref.shape[1] - 3 * width
        if rest:
            grads_ref[rows, 3 * width :] = jnp.zeros((BLK, rest), jnp.bfloat16)
        return sums + jnp.sum(grad * normed, axis=0, keepdims=True)

    sums = lax.fori_loop(0, tokens // BLK, finish, jnp.zeros((1, 2 * width), jnp.float32))
    gain_grad_ref[...] = sums[:, :width] + sums[:, width:]


def attend_back(qkv, gain, length, mixed, d_mixed, qa, ka, va):
    tokens, three = qkv.shape
    width = gain.shape[1]
    heads = width // HD
    vmem = pl.BlockSpec(memory_space=pltpu.VMEM)
    aug = pltpu.VMEM((heads, tokens, LANES), jnp.float32)
    return pl.pallas_call(
        functools.partial(attend_back_kernel, heads),
        out_shape=(
            jax.ShapeDtypeStruct((tokens, three), jnp.bfloat16),
            jax.ShapeDtypeStruct((1, width), jnp.float32),
        ),
        in_specs=[pl.BlockSpec(memory_space=pltpu.SMEM), pl.BlockSpec(memory_space=pltpu.HBM)] + [vmem] * 6,
        out_specs=(vmem,) * 2,
        scratch_shapes=[
            pltpu.VMEM((heads, tokens, LANES), jnp.bfloat16),
            aug,
            aug,
            aug,
            pltpu.VMEM((tokens, 2 * width), jnp.float32),
            pltpu.SemaphoreType.DMA,
        ],
        compiler_params=pltpu.CompilerParams(vmem_limit_bytes=60 << 20),
        cost_estimate=pl.CostEstimate(
            flops=heads * tokens * tokens, bytes_accessed=8 << 20, transcendentals=0
        ),
        name="attend_back",
    )(length, qkv, gain, mixed, d_mixed, qa, ka, va)


CORE, XAX, YAX = 1, 2, 4
GROUPS = ((0, 3), (3, 5))


def swap_dp(v, bit):
    return lax.ppermute(v, "dp", [(i, i ^ bit) for i in range(8)])


def swap_z(v, mask):
    return lax.ppermute(v, "ctx", [(i, i ^ mask) for i in range(4)])


def fence(*arrays):
    return lax.optimization_barrier(arrays)


def pick(v, index, axis=0):
    return lax.dynamic_index_in_dim(v, index, axis, keepdims=False)


def add_low(a, b):
    return (a.astype(jnp.float32) + b.astype(jnp.float32)).astype(jnp.bfloat16)


def by_core(c, own, other, axis=0):
    return jnp.where(c == 0, jnp.stack([own, other], axis), jnp.stack([other, own], axis))


def add3(a, b, d):
    return (a.astype(jnp.float32) + b.astype(jnp.float32) + d.astype(jnp.float32)).astype(jnp.bfloat16)


class Cells:
    def __init__(self, parts, x_first):
        self.corner, self.side, self.relay, self.keep = parts
        self.links = (XAX, YAX) if x_first else (YAX, XAX)

    def first(self, v):
        return swap_dp(v, self.links[0])

    def second(self, corner):
        return swap_dp(add_low(self.relay, corner), self.links[1])

    def total(self, side, relay):
        return add3(self.keep, side, relay)


def cells(parts):
    return [Cells(parts[:4], True), Cells(parts[4:], False)]


def total3(a, b, d):
    return a.astype(jnp.float32) + b.astype(jnp.float32) + d.astype(jnp.float32)


COLS = (0, 640, 1024)


def heads_kernel(q_ref, k_ref, v_ref, o_ref, small_ref, out_ref):
    share, width = o_ref.shape
    heads_width = width // 4
    out_ref[...] = jnp.zeros_like(out_ref)
    for z in range(4):
        out_ref[z, :, :width] = o_ref[...]
        for (a, b), at in zip(GROUPS, COLS):
            size = (b - a) * HD
            cols = [ref[:, z * heads_width + a * HD : z * heads_width + b * HD] for ref in (q_ref, k_ref, v_ref)]
            out_ref[z, :, width + at : width + at + 3 * size] = jnp.concatenate(cols, 1)
        out_ref[z, : small_ref.shape[0], out_ref.shape[2] - small_ref.shape[1] :] = small_ref[...]


def prepare_heads(query, key, value, output, small, half):
    share = output.shape[0]
    vmem = pl.BlockSpec(memory_space=pltpu.VMEM)
    return pl.pallas_call(
        heads_kernel,
        out_shape=jax.ShapeDtypeStruct((4, share, half), jnp.bfloat16),
        in_specs=[vmem] * 5,
        out_specs=vmem,
        compiler_params=pltpu.CompilerParams(vmem_limit_bytes=60 << 20),
        cost_estimate=pl.CostEstimate(flops=0, bytes_accessed=2 << 20, transcendentals=0),
        name="prepare_heads",
    )(query, key, value, output, small)


def prepare_kernel(core_ref, up_ref, gate_ref, down_ref, own_ref, other_ref, dw_ref):
    width = down_ref.shape[2]
    step = up_ref.shape[1] // 8
    for kind, ref in enumerate((up_ref, gate_ref)):
        for core in range(2):

            @pl.when(core_ref[0] == core)
            def _():
                for at in range(4):
                    here = pl.ds(at * step, step)
                    own_ref[kind, :, here] = ref[:, (2 * at + core) * step : (2 * at + core + 1) * step]
                    other_ref[kind, :, here] = ref[:, (2 * at + 1 - core) * step : (2 * at + 2 - core) * step]
    for part in range(2):
        for side in range(2):
            dw_ref[part, :, side * width : (side + 1) * width] = down_ref[2 * part + side]


def prepare(c, up, gate, down):
    share, wide = up.shape
    vmem = pl.BlockSpec(memory_space=pltpu.VMEM)
    planes = jax.ShapeDtypeStruct((2, share, wide // 2), jnp.bfloat16)
    return pl.pallas_call(
        prepare_kernel,
        out_shape=(planes,) * 3,
        in_specs=[pl.BlockSpec(memory_space=pltpu.SMEM)] + [vmem] * 3,
        out_specs=(vmem,) * 3,
        compiler_params=pltpu.CompilerParams(vmem_limit_bytes=60 << 20),
        cost_estimate=pl.CostEstimate(flops=0, bytes_accessed=4 << 20, transcendentals=0),
        name="prepare",
    )(c.astype(jnp.int32).reshape(1), up, gate, down)


def run_copies(copies):
    copies = [pltpu.make_async_copy(*copy) for copy in copies]
    for copy in copies:
        copy.start()
    for copy in copies:
        copy.wait()


def place(sources, plan, coords, cuts):
    count, rows = len(sources), sources[0].shape[1]

    def kernel(coord_ref, *refs):
        outs, sems = refs[count:-1], refs[-1]
        copies = []
        for at, (key, array, plane, inner) in enumerate(plan):
            where = tuple(jnp.bitwise_xor(coord_ref[d], key[d]) for d in range(3)) + (inner,)
            for out, (out_ref, (size, start, length)) in enumerate(zip(outs, cuts)):
                copies.append((refs[array].at[plane, :, pl.ds(start, length)], out_ref.at[where], sems.at[at, out]))
        run_copies(copies)

    return pl.pallas_call(
        kernel,
        out_shape=[jax.ShapeDtypeStruct((2, 2, 2, 4, rows, size), jnp.bfloat16) for size, _, _ in cuts],
        in_specs=[pl.BlockSpec(memory_space=pltpu.SMEM)] + [pl.BlockSpec(memory_space=pltpu.HBM)] * count,
        out_specs=[pl.BlockSpec(memory_space=pltpu.VMEM)] * len(cuts),
        scratch_shapes=[pltpu.SemaphoreType.DMA((len(plan), len(cuts)))],
        compiler_params=pltpu.CompilerParams(vmem_limit_bytes=60 << 20),
        cost_estimate=pl.CostEstimate(flops=0, bytes_accessed=14 << 20, transcendentals=0),
        name="place",
    )(coords, *sources)


def spread(sources, plan, coords, width):
    count, share, half = len(sources), sources[0].shape[1], sources[0].shape[2]

    def kernel(coord_ref, *refs):
        up_ref, gate_ref, down_ref, sems = refs[count:]
        copies = []
        for at, (key, array, plane, core) in enumerate(plan):
            yy, xx, zz = (jnp.bitwise_xor(coord_ref[d], key[d]) for d in range(3))
            for kind, out_ref in enumerate((up_ref, gate_ref)):
                copies.append((refs[array].at[plane + kind], out_ref.at[yy, xx, core, zz], sems.at[at, kind]))
            for side in range(2):
                lanes = pl.ds(side * width, width)
                copies.append((refs[array].at[plane + 2, :, lanes], down_ref.at[yy, xx, zz, core, side], sems.at[at, 2 + side]))
        run_copies(copies)

    up, gate, down = pl.pallas_call(
        kernel,
        out_shape=[
            jax.ShapeDtypeStruct((2, 2, 2, 4, share, half), jnp.bfloat16),
            jax.ShapeDtypeStruct((2, 2, 2, 4, share, half), jnp.bfloat16),
            jax.ShapeDtypeStruct((2, 2, 4, 2, 2, share, width), jnp.bfloat16),
        ],
        in_specs=[pl.BlockSpec(memory_space=pltpu.SMEM)] + [pl.BlockSpec(memory_space=pltpu.HBM)] * count,
        out_specs=[pl.BlockSpec(memory_space=pltpu.VMEM)] * 3,
        scratch_shapes=[pltpu.SemaphoreType.DMA((len(plan), 4))],
        compiler_params=pltpu.CompilerParams(vmem_limit_bytes=60 << 20),
        cost_estimate=pl.CostEstimate(flops=0, bytes_accessed=40 << 20, transcendentals=0),
        name="spread",
    )(coords, *sources)
    return up, gate, down


def spread_last(weights, parts, key, coords):
    _, share, half = parts[0].shape
    width = weights[2].shape[-1]

    def kernel(coord_ref, *refs):
        held_ref, in_sems, out_sems = refs[8:]
        yy, xx, zz = (jnp.bitwise_xor(coord_ref[d], key[d]) for d in range(3))
        run_copies([(refs[core], held_ref.at[core], in_sems.at[core]) for core in range(2)])
        up_ref, gate_ref, down_ref = refs[5:8]
        copies = []
        for core in range(2):
            for kind, ref in enumerate((up_ref, gate_ref)):
                copies.append((held_ref.at[core, kind], ref.at[yy, xx, core, zz], out_sems.at[core, kind]))
            for side in range(2):
                lanes = pl.ds(side * width, width)
                copies.append((held_ref.at[core, 2, :, lanes], down_ref.at[yy, xx, zz, core, side], out_sems.at[core, 2 + side]))
        run_copies(copies)

    hbm = pl.BlockSpec(memory_space=pltpu.HBM)
    up, gate, down = pl.pallas_call(
        kernel,
        out_shape=[jax.ShapeDtypeStruct(v.shape, v.dtype) for v in weights],
        in_specs=[pl.BlockSpec(memory_space=pltpu.SMEM)] + [hbm] * 5,
        out_specs=[hbm] * 3,
        scratch_shapes=[
            pltpu.VMEM((2, 3, share, half), jnp.bfloat16),
            pltpu.SemaphoreType.DMA((2,)),
            pltpu.SemaphoreType.DMA((2, 4)),
        ],
        input_output_aliases={3: 0, 4: 1, 5: 2},
        compiler_params=pltpu.CompilerParams(vmem_limit_bytes=BIG),
        cost_estimate=small_cost(),
        name="spread_last",
    )(coords, *parts, *weights)
    return up.reshape(32 * share, half), gate.reshape(32 * share, half), down.reshape(64 * share, width)

BIG = 60 << 20
TILE = 512


def small_cost(bytes_accessed=1 << 20):
    return pl.CostEstimate(flops=0, bytes_accessed=bytes_accessed, transcendentals=0)


def dot(a, b, on_a=1, on_b=0):
    return lax.dot_general(a, b, (((on_a,), (on_b,)), ((), ())), preferred_element_type=jnp.float32)


def ff_forward(own, other, up, gate, down, scale_up, scale_gate):
    rows, width = own.shape
    hidden = up.shape[1]
    steps = hidden // TILE

    def kernel(own_ref, other_ref, up_ref, gate_ref, down_ref, su_ref, sg_ref,
               upper_ref, gating_ref, hidden_ref, lower_ref, lower_other_ref, turned_ref, both_ref, acc_ref):
        step = pl.program_id(0)

        @pl.when(step == 0)
        def _():
            both_ref[:rows] = own_ref[...]
            both_ref[rows:] = other_ref[...]

        both = both_ref[...]
        upper = dot(both, up_ref[...])
        gating = dot(both, gate_ref[...])
        upper_ref[...] = upper
        gating_ref[...] = gating
        gate_arg = gating * sg_ref[...]
        hid = ((upper * su_ref[...]) * (gate_arg / (1.0 + jnp.exp(-gate_arg)))).astype(jnp.bfloat16)
        hidden_ref[...] = hid
        part = dot(hid, down_ref[...])

        @pl.when(step == 0)
        def _():
            acc_ref[...] = part

        @pl.when(step > 0)
        def _():
            acc_ref[...] += part

        @pl.when(step == steps - 1)
        def _():
            lower_ref[...] = acc_ref[:rows]
            lower_other_ref[...] = acc_ref[rows:].astype(jnp.bfloat16)

        @pl.when(step == 1)
        def _():
            turned_ref[...] = both_ref[...].T

    f32, low = jnp.float32, jnp.bfloat16
    return pl.pallas_call(
        kernel,
        out_shape=(
            jax.ShapeDtypeStruct((2 * rows, hidden), f32),
            jax.ShapeDtypeStruct((2 * rows, hidden), f32),
            jax.ShapeDtypeStruct((2 * rows, hidden), low),
            jax.ShapeDtypeStruct((rows, width), f32),
            jax.ShapeDtypeStruct((rows, width), low),
            jax.ShapeDtypeStruct((width, 2 * rows), low),
        ),
        grid=(steps,),
        in_specs=[
            pl.BlockSpec((rows, width), lambda i: (0, 0)),
            pl.BlockSpec((rows, width), lambda i: (0, 0)),
            pl.BlockSpec((width, TILE), lambda i: (0, i)),
            pl.BlockSpec((width, TILE), lambda i: (0, i)),
            pl.BlockSpec((TILE, width), lambda i: (i, 0)),
            pl.BlockSpec((1, TILE), lambda i: (0, i)),
            pl.BlockSpec((1, TILE), lambda i: (0, i)),
        ],
        out_specs=(
            pl.BlockSpec((2 * rows, TILE), lambda i: (0, i)),
            pl.BlockSpec((2 * rows, TILE), lambda i: (0, i)),
            pl.BlockSpec((2 * rows, TILE), lambda i: (0, i)),
            pl.BlockSpec((rows, width), lambda i: (0, 0)),
            pl.BlockSpec((rows, width), lambda i: (0, 0)),
            pl.BlockSpec((width, 2 * rows), lambda i: (0, 0)),
        ),
        scratch_shapes=[pltpu.VMEM((2 * rows, width), low), pltpu.VMEM((2 * rows, width), f32)],
        compiler_params=pltpu.CompilerParams(vmem_limit_bytes=BIG),
        cost_estimate=small_cost(),
        name="ff_forward",
    )(own, other, up, gate, down, scale_up, scale_gate)


def down_back(coords, hidden, own, other):
    rows, width = own.shape
    cell = hidden.shape[1] // 4
    unit = width // 2

    def kernel(coord_ref, hidden_ref, own_ref, other_ref, corner0, side0, relay0, keep0, corner1, side1, relay1, keep1):
        step = pl.program_id(0)
        part = dot(hidden_ref[:rows], own_ref[...], 0, 0) + dot(hidden_ref[rows:], other_ref[...], 0, 0)
        part = part.astype(jnp.bfloat16)
        for at, refs in enumerate(((corner0, corner1), (relay0, side1), (side0, relay1), (keep0, keep1))):

            @pl.when(step == at)
            def _():
                refs[0][...] = part[:, :unit]
                refs[1][...] = part[:, unit:]

    one = jax.ShapeDtypeStruct((cell, unit), jnp.bfloat16)
    whole = pl.BlockSpec((rows, width), lambda i, coord_ref: (0, 0))
    one_spec = pl.BlockSpec((cell, unit), lambda i, coord_ref: (0, 0))
    return pl.pallas_call(
        kernel,
        out_shape=(one,) * 8,
        grid_spec=pltpu.PrefetchScalarGridSpec(
            num_scalar_prefetch=1,
            grid=(4,),
            in_specs=[
                pl.BlockSpec((2 * rows, cell), lambda i, coord_ref: (0, jnp.bitwise_xor(2 * coord_ref[0] + coord_ref[1], 3 - i))),
                whole,
                whole,
            ],
            out_specs=(one_spec,) * 8,
        ),
        compiler_params=pltpu.CompilerParams(vmem_limit_bytes=BIG),
        cost_estimate=small_cost(),
        name="down_back",
    )(coords, hidden, own, other)


def hidden_back(own, other, down, upper, gating, scale_up, scale_gate):
    rows, width = own.shape
    hidden = down.shape[0]

    def kernel(own_ref, other_ref, down_ref, upper_ref, gating_ref, su_ref, sg_ref, d_up_ref, d_gate_ref, us_ref, gs_ref):
        for part, ref in enumerate((own_ref, other_ref)):
            at = pl.ds(part * rows, rows)
            d_hidden = dot(ref[...], down_ref[...], 1, 1)
            upper, gating = upper_ref[at, :], gating_ref[at, :]
            su, sg = su_ref[...], sg_ref[...]
            gate_arg = gating * sg
            sig = 1.0 / (1.0 + jnp.exp(-gate_arg))
            d_upper = d_hidden * (gate_arg * sig)
            d_gate_arg = d_hidden * (upper * su) * (sig * (1.0 + gate_arg * (1.0 - sig)))
            us = jnp.sum(d_upper * upper, axis=0, keepdims=True)
            gs = jnp.sum(d_gate_arg * gating, axis=0, keepdims=True)
            us_ref[...] = us if part == 0 else us_ref[...] + us
            gs_ref[...] = gs if part == 0 else gs_ref[...] + gs
            d_up_ref[at, :] = (d_upper * su).astype(jnp.bfloat16)
            d_gate_ref[at, :] = (d_gate_arg * sg).astype(jnp.bfloat16)

    tall = lambda: pl.BlockSpec((2 * rows, TILE), lambda i: (0, i))
    flat = lambda: pl.BlockSpec((1, TILE), lambda i: (0, i))
    return pl.pallas_call(
        kernel,
        out_shape=(
            jax.ShapeDtypeStruct((2 * rows, hidden), jnp.bfloat16),
            jax.ShapeDtypeStruct((2 * rows, hidden), jnp.bfloat16),
            jax.ShapeDtypeStruct((1, hidden), jnp.float32),
            jax.ShapeDtypeStruct((1, hidden), jnp.float32),
        ),
        grid=(hidden // TILE,),
        in_specs=[
            pl.BlockSpec((rows, width), lambda i: (0, 0)),
            pl.BlockSpec((rows, width), lambda i: (0, 0)),
            pl.BlockSpec((TILE, width), lambda i: (i, 0)),
            tall(), tall(), flat(), flat(),
        ],
        out_specs=(tall(), tall(), flat(), flat()),
        compiler_params=pltpu.CompilerParams(vmem_limit_bytes=BIG),
        cost_estimate=small_cost(),
        name="hidden_back",
    )(own, other, down, upper, gating, scale_up, scale_gate)


def wide_back(coords, turned, d_wide):
    width, tokens = turned.shape
    hidden = d_wide.shape[1]
    part = width // 8

    def kernel(coord_ref, turned_ref, d_ref, corner0, side0, relay0, keep0, corner1, side1, relay1, keep1, order_ref):
        @pl.when(pl.program_id(0) == 0)
        def _():
            for at in range(4):
                start = jnp.bitwise_xor(2 * coord_ref[0] + coord_ref[1], at) * (2 * part)
                order_ref[pl.ds(at * 2 * part, 2 * part), :] = turned_ref[pl.ds(pl.multiple_of(start, 2 * part), 2 * part), :]

        out = dot(order_ref[...], d_ref[...]).astype(jnp.bfloat16)
        for at, ref in enumerate((keep0, keep1, side0, relay1, relay0, side1, corner0, corner1)):
            ref[...] = out[at * part : (at + 1) * part]

    tile = 512
    one = jax.ShapeDtypeStruct((part, hidden), jnp.bfloat16)
    one_spec = pl.BlockSpec((part, tile), lambda i: (0, i))
    return pl.pallas_call(
        kernel,
        out_shape=(one,) * 8,
        grid=(hidden // tile,),
        in_specs=[
            pl.BlockSpec(memory_space=pltpu.SMEM),
            pl.BlockSpec((width, tokens), lambda i: (0, 0)),
            pl.BlockSpec((tokens, tile), lambda i: (0, i)),
        ],
        out_specs=(one_spec,) * 8,
        scratch_shapes=[pltpu.VMEM((width, tokens), jnp.bfloat16)],
        compiler_params=pltpu.CompilerParams(vmem_limit_bytes=BIG),
        cost_estimate=small_cost(),
        name="wide_back",
    )(coords, turned, d_wide)


def states_back(line, d_qkv0, d_qkv1, weights, local, masks):
    width = weights.shape[0]
    low = jnp.bfloat16

    def kernel(line_ref, d0_ref, d1_ref, w_ref, *out_refs):
        step = pl.program_id(0)
        split = d0_ref.shape[1]
        part = dot(d0_ref[...], w_ref[:, :split], 1, 1) + dot(d1_ref[...], w_ref[:, split:], 1, 1)
        for at, ref in enumerate(out_refs):

            @pl.when(step == at)
            def _():
                ref[...] = part.astype(low)

    def block(i, line_ref):
        mask = masks[-1]
        for at in range(len(masks) - 1):
            mask = jnp.where(i == at, masks[at], mask)
        return (jnp.bitwise_xor(line_ref[0], mask), 0)

    return pl.pallas_call(
        kernel,
        out_shape=[jax.ShapeDtypeStruct((local, width), low) for _ in masks],
        grid_spec=pltpu.PrefetchScalarGridSpec(
            num_scalar_prefetch=1,
            grid=(len(masks),),
            in_specs=[
                pl.BlockSpec((local, d_qkv0.shape[1]), block),
                pl.BlockSpec((local, d_qkv1.shape[1]), block),
                pl.BlockSpec(weights.shape, lambda i, line_ref: (0, 0)),
            ],
            out_specs=[pl.BlockSpec((local, width), lambda i, line_ref: (0, 0)) for _ in masks],
        ),
        compiler_params=pltpu.CompilerParams(vmem_limit_bytes=BIG),
        cost_estimate=small_cost(),
        name="states_back",
    )(line, d_qkv0, d_qkv1, weights)


def project(line, states, weights):
    local, width = states[0].shape
    split = COLS[1]
    rest = weights.shape[1] - split

    def kernel(line_ref, *refs):
        w_ref, out0_ref, out1_ref = refs[4:]
        step = pl.program_id(0)
        for at in range(4):

            @pl.when(step == at)
            def _():
                out = dot(refs[at][...], w_ref[...])
                out0_ref[...] = out[:, :split]
                out1_ref[...] = out[:, split:]

    spot = lambda i, line_ref: (jnp.bitwise_xor(line_ref[0], i), 0)
    fixed = lambda i, line_ref: (0, 0)
    return pl.pallas_call(
        kernel,
        out_shape=[jax.ShapeDtypeStruct((4 * local, n), jnp.float32) for n in (split, rest)],
        grid_spec=pltpu.PrefetchScalarGridSpec(
            num_scalar_prefetch=1,
            grid=(4,),
            in_specs=[pl.BlockSpec((local, width), fixed)] * 4 + [pl.BlockSpec(weights.shape, fixed)],
            out_specs=[pl.BlockSpec((local, n), spot) for n in (split, rest)],
        ),
        compiler_params=pltpu.CompilerParams(vmem_limit_bytes=BIG),
        cost_estimate=small_cost(),
        name="project",
    )(line, *states, weights)


def rows_back(coords, states, d_qkv0, d_qkv1, gain_grad, spare):
    chunk, width = states[0].shape
    cell = width // 8
    split, three = d_qkv0.shape[1], d_qkv0.shape[1] + d_qkv1.shape[1]
    tokens = 4 * chunk
    steps = 4
    low = jnp.bfloat16

    def kernel(coord_ref, *refs):
        d0_ref, d1_ref, gain_ref, keep_ref, send_ref, acc0_ref, acc1_ref = refs[4:]
        step = pl.program_id(0)

        for at in range(4):

            @pl.when(step == at)
            def _():
                for d_ref, acc_ref in ((d0_ref, acc0_ref), (d1_ref, acc1_ref)):
                    part = dot(refs[at][...], d_ref[...], 0, 0)
                    acc_ref[...] = part if at == 0 else acc_ref[...] + part

        @pl.when(step == steps - 1)
        def _():
            here = lax.broadcasted_iota(jnp.int32, (cell, split), 1) == spare
            for at in range(4):
                for ref, core in ((keep_ref, coord_ref[2]), (send_ref, 1 - coord_ref[2])):
                    start = (2 * jnp.bitwise_xor(2 * coord_ref[0] + coord_ref[1], at) + core) * cell
                    rows = pl.ds(pl.multiple_of(start, cell), cell)
                    ref[at, :, :split] = jnp.where(here, gain_ref[rows, :], acc0_ref[rows, :]).astype(low)
                    ref[at, :, split:] = acc1_ref[rows, :].astype(low)

    shape = jax.ShapeDtypeStruct((4, cell, three), low)
    return pl.pallas_call(
        kernel,
        out_shape=(shape, shape),
        grid_spec=pltpu.PrefetchScalarGridSpec(
            num_scalar_prefetch=1,
            grid=(steps,),
            in_specs=[pl.BlockSpec((chunk, width), lambda i, coord_ref: (0, 0))] * 4
            + [
                pl.BlockSpec((chunk, split), lambda i, coord_ref: (jnp.bitwise_xor(coord_ref[3], i), 0)),
                pl.BlockSpec((chunk, three - split), lambda i, coord_ref: (jnp.bitwise_xor(coord_ref[3], i), 0)),
                pl.BlockSpec((width, 1), lambda i, coord_ref: (0, 0)),
            ],
            out_specs=(pl.BlockSpec((4, cell, three), lambda i, coord_ref: (0, 0, 0)),) * 2,
            scratch_shapes=[pltpu.VMEM((width, split), jnp.float32), pltpu.VMEM((width, three - split), jnp.float32)],
        ),
        compiler_params=pltpu.CompilerParams(vmem_limit_bytes=BIG),
        cost_estimate=pl.CostEstimate(flops=2 * tokens * width * three, bytes_accessed=16 << 20, transcendentals=0),
        name="rows_back",
    )(coords, *states, d_qkv0, d_qkv1, gain_grad)


def interleave(c, own, other):
    _, share, half = own.shape
    step = half // 4

    def kernel(core_ref, own_ref, other_ref, up_ref, gate_ref):
        for core in range(2):

            @pl.when(core_ref[0] == core)
            def _():
                for kind, ref in enumerate((up_ref, gate_ref)):
                    for at in range(4):
                        here = pl.ds(at * step, step)
                        ref[:, (2 * at + core) * step : (2 * at + core + 1) * step] = own_ref[kind, :, here]
                        ref[:, (2 * at + 1 - core) * step : (2 * at + 2 - core) * step] = other_ref[kind, :, here]

    vmem = pl.BlockSpec(memory_space=pltpu.VMEM)
    return pl.pallas_call(
        kernel,
        out_shape=(jax.ShapeDtypeStruct((share, 2 * half), own.dtype),) * 2,
        in_specs=[pl.BlockSpec(memory_space=pltpu.SMEM), vmem, vmem],
        out_specs=(vmem,) * 2,
        compiler_params=pltpu.CompilerParams(vmem_limit_bytes=BIG),
        cost_estimate=small_cost(),
        name="interleave",
    )(c.astype(jnp.int32).reshape(1), own, other)


def row_mean(v):
    return jnp.mean(v, axis=-1, keepdims=True)


def loss_back(inside, scale, lower, lower_got, middle, teacher, mstep):
    rows, width = lower.shape
    tile = rows // 4
    f32, low = jnp.float32, jnp.bfloat16

    def kernel(inside_ref, scale_ref, lower_ref, got_ref, middle_ref, teacher_ref, step_ref,
               final_ref, d_lower_ref, d_middle_ref, sum_ref, err_ref):
        at = pl.program_id(0)
        lower = lower_ref[...] + got_ref[...].astype(f32)
        middle, mstep = middle_ref[...], step_ref[...]
        factor = lax.rsqrt(row_mean(lower * lower) + eps)
        normed = lower * factor
        second = middle + mstep * (normed - middle)
        factor_end = lax.rsqrt(row_mean(second * second) + eps)
        final = second * factor_end
        final_ref[...] = final.astype(low)
        diff = final - teacher_ref[...].astype(f32)
        valid = (lax.broadcasted_iota(jnp.int32, (tile, 1), 0) + at * tile < inside_ref[0]).astype(f32)
        diff = valid * diff
        cot = scale_ref[0] * diff
        d_second = factor_end * (cot - final * row_mean(cot * final))
        d_middle_ref[...] = d_second * (1.0 - mstep)
        grad = d_second * mstep
        d_lower_ref[...] = (factor * (grad - normed * row_mean(grad * normed))).astype(low)
        sums = jnp.sum(d_second * (normed - middle), axis=0, keepdims=True)
        errs = jnp.sum(diff * diff, axis=0, keepdims=True)

        @pl.when(at == 0)
        def _():
            sum_ref[...] = sums
            err_ref[...] = errs

        @pl.when(at > 0)
        def _():
            sum_ref[...] += sums
            err_ref[...] += errs

    by_row = pl.BlockSpec((tile, width), lambda i: (i, 0))
    flat = pl.BlockSpec((1, width), lambda i: (0, 0))
    smem = pl.BlockSpec(memory_space=pltpu.SMEM)
    return pl.pallas_call(
        kernel,
        out_shape=(
            jax.ShapeDtypeStruct((rows, width), low),
            jax.ShapeDtypeStruct((rows, width), low),
            jax.ShapeDtypeStruct((rows, width), f32),
            jax.ShapeDtypeStruct((1, width), f32),
            jax.ShapeDtypeStruct((1, width), f32),
        ),
        grid=(rows // tile,),
        in_specs=[smem, smem, by_row, by_row, by_row, by_row, flat],
        out_specs=(by_row, by_row, by_row, flat, flat),
        compiler_params=pltpu.CompilerParams(vmem_limit_bytes=BIG),
        cost_estimate=small_cost(),
        name="loss_back",
    )(inside, scale, lower, lower_got, middle, teacher, mstep)


def branch_back(d_middle, d_own, d_got, branch, states, astep):
    rows, width = branch.shape
    tile = rows // 4
    f32, low = jnp.float32, jnp.bfloat16

    def kernel(d_middle_ref, own_ref, got_ref, branch_ref, states_ref, step_ref, grad_ref, d_branch_ref, sum_ref):
        at = pl.program_id(0)
        d_middle = d_middle_ref[...] + own_ref[...] + got_ref[...].astype(f32)
        branch, resid, astep = branch_ref[...], states_ref[...].astype(f32), step_ref[...]
        factor_branch = lax.rsqrt(row_mean(branch * branch) + eps)
        normed = branch * factor_branch
        first = resid + astep * (normed - resid)
        factor = lax.rsqrt(row_mean(first * first) + eps)
        middle = first * factor
        d_first = factor * (d_middle - middle * row_mean(d_middle * middle))
        grad_ref[...] = d_first * (1.0 - astep)
        grad = d_first * astep
        d_branch_ref[...] = (factor_branch * (grad - normed * row_mean(grad * normed))).astype(low)
        sums = jnp.sum(d_first * (normed - resid), axis=0, keepdims=True)

        @pl.when(at == 0)
        def _():
            sum_ref[...] = sums

        @pl.when(at > 0)
        def _():
            sum_ref[...] += sums

    by_row = pl.BlockSpec((tile, width), lambda i: (i, 0))
    flat = pl.BlockSpec((1, width), lambda i: (0, 0))
    return pl.pallas_call(
        kernel,
        out_shape=(
            jax.ShapeDtypeStruct((rows, width), f32),
            jax.ShapeDtypeStruct((rows, width), low),
            jax.ShapeDtypeStruct((1, width), f32),
        ),
        grid=(rows // tile,),
        in_specs=[by_row, by_row, by_row, by_row, by_row, flat],
        out_specs=(by_row, by_row, flat),
        compiler_params=pltpu.CompilerParams(vmem_limit_bytes=BIG),
        cost_estimate=small_cost(),
        name="branch_back",
    )(d_middle, d_own, d_got, branch, states, astep)


def middle_back(d_up, d_gate, up, gate):
    tokens, hidden = d_up.shape
    width = up.shape[0]
    rows = tokens // 2
    steps = hidden // TILE

    def kernel(d_up_ref, d_gate_ref, up_ref, gate_ref, own_ref, other_ref, acc_ref):
        step = pl.program_id(0)
        part = dot(d_up_ref[...], up_ref[...], 1, 1) + dot(d_gate_ref[...], gate_ref[...], 1, 1)

        @pl.when(step == 0)
        def _():
            acc_ref[...] = part

        @pl.when(step > 0)
        def _():
            acc_ref[...] += part

        @pl.when(step == steps - 1)
        def _():
            own_ref[...] = acc_ref[:rows]
            other_ref[...] = acc_ref[rows:].astype(jnp.bfloat16)

    tall = lambda n: pl.BlockSpec((n, TILE), lambda i: (0, i))
    return pl.pallas_call(
        kernel,
        out_shape=(jax.ShapeDtypeStruct((rows, width), jnp.float32), jax.ShapeDtypeStruct((rows, width), jnp.bfloat16)),
        grid=(steps,),
        in_specs=[tall(tokens), tall(tokens), tall(width), tall(width)],
        out_specs=(pl.BlockSpec((rows, width), lambda i: (0, 0)),) * 2,
        scratch_shapes=[pltpu.VMEM((tokens, width), jnp.float32)],
        compiler_params=pltpu.CompilerParams(vmem_limit_bytes=BIG),
        cost_estimate=small_cost(),
        name="middle_back",
    )(d_up, d_gate, up, gate)


def on_cores(
    inputs,
    teacher,
    lengths,
    query_weight,
    key_weight,
    value_projection,
    output_weight,
    score_gain,
    attention_step,
    up_weight,
    gate_weight,
    down_weight,
    up_scale,
    gate_scale,
    swiglu_step,
):
    local, width = inputs.shape[1:]
    share = query_weight.shape[0]
    hidden_share = down_weight.shape[0]
    heads_width = width // 4
    three = COLS[-1]
    hidden_half = up_weight.shape[1] // 2
    tokens = local * 4
    low = jnp.bfloat16
    f32 = jnp.float32
    dp, z = lax.axis_index("dp"), lax.axis_index("ctx")
    c, x, y = dp % 2, dp // 2 % 2, dp // 4
    chip = jnp.stack([y, x, z]).astype(jnp.int32)
    line = z.astype(jnp.int32).reshape(1)
    states = inputs.reshape(local, width)

    half = up_weight.shape[1] // 2
    ug_own, ug_other, dw = prepare(c, up_weight, gate_weight, down_weight.reshape(4, share, width))
    def on_x(*v):
        return swap_dp(jnp.concatenate(v) if len(v) > 1 else v[0], XAX)

    def on_y(*v):
        return swap_dp(jnp.concatenate(v) if len(v) > 1 else v[0], YAX)

    def exchange(blocks):
        return lax.all_to_all(blocks, "ctx", 0, 0, tiled=True)

    ug_sib = swap_dp(ug_other, CORE)
    ug_sib, ug_own, score_gain, query_weight = fence(ug_sib, ug_own, score_gain, query_weight)
    f0 = jnp.concatenate([by_core(c, ug_own, ug_sib), dw[:, None]], 1).reshape(6, share, half)
    length_parts = jnp.stack([lengths[0] // 64, lengths[0] % 64]).astype(low)
    small = jnp.concatenate([score_gain, attention_step, up_scale, gate_scale, swiglu_step, length_parts])
    cuts = [0]
    for size in (share, share, hidden_share, hidden_share, share, 2):
        cuts.append(cuts[-1] + size)
    small = jnp.pad(small, (0, 512 - small.shape[0])).reshape(2, 256)
    q0 = exchange(prepare_heads(query_weight, key_weight, value_projection, output_weight, small, half))
    f0x, f0y, f1 = on_x(f0), on_y(f0), swap_z(f0, 1)
    f0, f0x, f0y, f1, q0, states = fence(f0, f0x, f0y, f1, q0, states)
    xb, yb = on_x(f1, f0y[:3], q0), on_y(f1, f0x[3:], q0)
    s1, s2 = swap_z(states, 1), swap_z(states, 2)
    xb, yb, s1, s2, f0 = fence(xb, yb, s1, s2, f0)
    f2a, s3 = swap_z(f0[:3], 2), swap_z(s2, 1)
    xc, yc = on_x(yb[:3], yb[9:11]), on_y(xb[3:6], xb[11:])
    qc = swap_dp(jnp.concatenate([q0, xb[9:], yb[9:]]), CORE)
    f2a, s3, xc, yc, qc, f0 = fence(f2a, s3, xc, yc, qc, f0)
    f2b, f3a = swap_z(f0[3:], 2), swap_z(f2a, 1)
    f2ax, f2ay = on_x(f2a), on_y(f2a)
    qd = swap_dp(jnp.concatenate([xc[3:], yc[3:]]), CORE)
    sources = [q0, xb, yb, xc, yc, qc, qd]
    plan = []
    for mc, (own, own_at, on_x_, x_at, on_y_, y_at, cross0, at0, cross1, at1) in enumerate(
        ((0, 0, 1, 9, 2, 9, 3, 3, 4, 3), (5, 0, 5, 4, 5, 8, 6, 0, 6, 2))
    ):
        for zz in range(4):
            plan.append(((0, 0, mc), own, own_at + zz, zz))
            plan.append(((0, 1, mc), on_x_, x_at + zz, zz))
            plan.append(((1, 0, mc), on_y_, y_at + zz, zz))
            if zz < 2:
                plan.append(((1, 1, mc), cross0, at0 + zz, zz))
            else:
                plan.append(((1, 1, mc), cross1, at1 + zz - 2, zz))
    full_output, full_qkv, vectors = place(
        sources, plan, jnp.stack([y, x, c]).astype(jnp.int32),
        [(width, 0, width), (half - width - 256, width, half - width - 256), (256, half - 256, 256)],
    )
    vectors = vectors[:, :, :, :, :2].reshape(2, 2, 2, 4, 512)
    full_output = full_output.reshape(width, width)
    full_qkv = full_qkv.reshape(width, -1)
    full_gain, full_astep, full_uscale, full_gscale, full_mstep, full_lengths = (
        vectors[..., a:b].astype(f32) for a, b in zip(cuts[:-1], cuts[1:])
    )
    count = jnp.sum(full_lengths[:, :, :, 0] * jnp.array([64.0, 1.0], f32))
    astep = full_astep.reshape(width)
    mstep = full_mstep.reshape(width)
    scale_up = pick(full_uscale, c, 2).reshape(-1)
    scale_gate = pick(full_gscale, c, 2).reshape(-1)
    gain = pick(full_gain.reshape(4, 1, heads_width), z)
    pieces = (states, s1, s2, s3)
    gains = [gain[:, a * HD : b * HD] for a, b in GROUPS]
    qkv0, qkv1 = project(line, pieces, full_qkv)
    qkv0, qkv1, f2b, f2ax, f2ay, f3a = fence(qkv0, qkv1, f2b, f2ax, f2ay, f3a)
    f3b = swap_z(f2b, 1)
    f2bx, f2by, f3ax, f3ay = on_x(f2b), on_y(f2b), on_x(f3a), on_y(f3a)
    mixed0, heads0, qa0, ka0, va0 = attend(qkv0, gains[0], lengths)
    heads0, f3b, f2bx, f2by, f3ax, f3ay, qkv1 = fence(heads0, f3b, f2bx, f2by, f3ax, f3ay, qkv1)
    parts0 = exchange(heads0.reshape(4, local, -1))
    f3bx, f3by, f2ac, f2bc = on_x(f3b), on_y(f3b), on_x(f2ay), on_y(f2bx)
    mixed1, heads1, qa1, ka1, va1 = attend(qkv1, gains[1], lengths)
    heads1, f3bx, f3by, f2ac, f2bc, parts0 = fence(heads1, f3bx, f3by, f2ac, f2bc, parts0)
    parts1 = exchange(heads1.reshape(4, local, -1))
    f3ac, f3bc = on_x(f3ay), on_y(f3bx)
    sources = [f0, f0x, f0y, f1, xb, yb, xc, yc]
    sources += [f2a, f2ax, f2ay, f2ac, f2b, f2bx, f2by, f2bc, f3a, f3ax, f3ay, f3b, f3bx, f3by]
    chips = ((0, 0), (0, 1), (1, 0), (1, 1))
    spots = {
        (0, 0): ((0, 0), (1, 0), (2, 0), (4, 6)),
        (0, 1): ((0, 3), (1, 3), (2, 3), (5, 6)),
        (1, 0): ((3, 0), (4, 0), (5, 0), (6, 0)),
        (1, 1): ((3, 3), (4, 3), (5, 3), (7, 0)),
        (2, 0): ((8, 0), (9, 0), (10, 0), (11, 0)),
        (2, 1): ((12, 0), (13, 0), (14, 0), (15, 0)),
        (3, 0): ((16, 0), (17, 0), (18, 0)),
        (3, 1): ((19, 0), (20, 0), (21, 0)),
    }
    plan = [
        (key + (mz,), array, plane, core)
        for (mz, core), arrays in spots.items()
        for key, (array, plane) in zip(chips, arrays)
    ]
    weights = spread(sources, plan, chip, width)
    weights, f3ac, f3bc, parts1 = fence(weights, f3ac, f3bc, parts1)
    full_up, full_gate, full_down = spread_last(weights, (f3ac, f3bc), (1, 1, 3), chip)
    mixed_low = jnp.concatenate([parts0, parts1], -1).transpose(1, 0, 2).reshape(local, width)
    branch = matmul(mixed_low, full_output)
    resid = states.astype(f32)
    branch_norm = normalize(branch)
    first = resid + astep * (branch_norm - resid)
    middle = normalize(first)
    middle_low = middle.astype(low)
    middle_other = swap_dp(middle_low, CORE)

    flat_up, flat_gate = scale_up.reshape(1, -1), scale_gate.reshape(1, -1)
    upper, gating, hidden, lower, lower_other, turned = ff_forward(
        middle_low, middle_other, full_up, full_gate, full_down, flat_up, flat_gate
    )
    final, d_lower, d_middle, grad_mstep, err_sums = loss_back(
        (lengths - z * local).astype(jnp.int32),
        (loss_scale * 2.0 / count).reshape(1),
        lower,
        swap_dp(lower_other, CORE),
        middle,
        teacher.reshape(local, width),
        mstep.reshape(1, width),
    )
    err_local = jnp.sum(err_sums)
    d_lower_other = swap_dp(d_lower, CORE)
    downs = cells(down_back(chip, hidden, d_lower, d_lower_other))
    downs[0].corner, downs[1].corner, d_lower, d_lower_other = fence(downs[0].corner, downs[1].corner, d_lower, d_lower_other)
    down_corner = [p.first(p.corner) for p in downs]
    down_side = [p.first(p.side) for p in downs]
    d_up, d_gate, grad_uscale, grad_gscale = hidden_back(
        d_lower, d_lower_other, full_down, upper, gating, flat_up, flat_gate
    )
    d_up, d_gate, down_corner = fence(d_up, d_gate, down_corner)
    down_relay = [p.second(v) for p, v in zip(downs, down_corner)]
    ups = cells(wide_back(chip, turned, d_up))
    ups[0].corner, ups[1].corner, down_side, d_up, d_gate = fence(ups[0].corner, ups[1].corner, down_side, d_up, d_gate)
    up_corner = [p.first(p.corner) for p in ups]
    d_both, d_both_other = middle_back(d_up, d_gate, full_up, full_gate)
    down_relay, d_both, d_both_other, ups[0].side, ups[1].side = fence(
        down_relay, d_both, d_both_other, ups[0].side, ups[1].side
    )
    up_side = [p.first(p.side) for p in ups]
    input_grad, d_branch, grad_astep = branch_back(
        d_middle, d_both, swap_dp(d_both_other, CORE), branch, states, astep.reshape(1, width)
    )
    d_mixed = right_tdot(d_branch, full_output).astype(low)
    blocks = d_mixed.reshape(local, 4, heads_width).transpose(1, 0, 2)
    blocks = [blocks[:, :, a * HD : b * HD] for a, b in GROUPS]
    scales = jnp.concatenate([grad_uscale.reshape(2, 2, 4, hidden_share), grad_gscale.reshape(2, 2, 4, hidden_share)], -1)
    scales = jnp.where((jnp.arange(2) == c)[None, None, :, None, None], scales[:, :, None], 0.0).reshape(32, -1)
    packed = jnp.concatenate(
        [grad_astep.reshape(32, share), scales, grad_mstep.reshape(32, share), jnp.full((32, 1), err_local)], 1
    )
    packed = jnp.pad(packed, ((0, 0), (0, 512 - packed.shape[1]))).reshape(2, 2, 2, 4, 4, 128)
    packed = pick(packed, c, 2) + swap_dp(pick(packed, 1 - c, 2), CORE)
    down = jnp.concatenate([p.total(v, r) for p, v, r in zip(downs, down_side, down_relay)], 1)
    down = down.reshape(4, hidden_share, width)
    blocks, d_branch, d_gate, up_corner, packed, down = fence(blocks, d_branch, d_gate, up_corner, packed, down)
    parts0 = exchange(blocks[0])
    up_relay = [p.second(v) for p, v in zip(ups, up_corner)]
    gates = cells(wide_back(chip, turned, d_gate))
    down_far = swap_z(pick(down, z ^ 3), 1)
    parts0, up_relay, up_side, gates[0].corner, gates[1].corner, block1, d_branch, packed = fence(
        parts0, up_relay, up_side, gates[0].corner, gates[1].corner, blocks[1], d_branch, packed
    )
    packed = pick(packed, x, 1) + swap_dp(pick(packed, 1 - x, 1), XAX)
    gate_corner = [p.first(p.corner) for p in gates]
    up = jnp.stack([p.total(v, r) for p, v, r in zip(ups, up_side, up_relay)]).reshape(2, 4, share, hidden_half)
    down_far, down_near = swap_z(add_low(pick(down, z ^ 2), down_far), 2), swap_z(pick(down, z ^ 1), 1)
    parts0, gate_corner, up, gates[0].side, gates[1].side, down_near, packed, d_branch = fence(
        parts0, gate_corner, up, gates[0].side, gates[1].side, down_near, packed, d_branch
    )
    parts1 = exchange(block1)
    gate_side = [p.first(p.side) for p in gates]
    gate_relay = [p.second(v) for p, v in zip(gates, gate_corner)]
    up_far = swap_z(pick(up, z ^ 3, 1), 1)
    d_heads0 = parts0.reshape(tokens, -1)
    d_qkv0, gain_grad0 = attend_back(qkv0, gains[0], lengths, mixed0, d_heads0, qa0, ka0, va0)
    d_qkv0, gain_grad0, parts1, gate_side, gate_relay, up_far, up, packed, down_far, d_branch = fence(
        d_qkv0, gain_grad0, parts1, gate_side, gate_relay, up_far, up, packed, down_far, d_branch
    )
    gate = jnp.stack([p.total(v, r) for p, v, r in zip(gates, gate_side, gate_relay)]).reshape(2, 4, share, hidden_half)
    up_far, up_near = swap_z(add_low(pick(up, z ^ 2, 1), up_far), 2), swap_z(pick(up, z ^ 1, 1), 1)
    gate_far, gate_near = swap_z(pick(gate, z ^ 3, 1), 1), swap_z(pick(gate, z ^ 1, 1), 1)
    packed = pick(packed, y) + swap_dp(pick(packed, 1 - y), YAX)
    d_heads1 = parts1.reshape(tokens, -1)
    d_qkv1, gain_grad1 = attend_back(qkv1, gains[1], lengths, mixed1, d_heads1, qa1, ka1, va1)
    d_qkv1, gain_grad1, gate, up_far, up_near, gate_far, gate_near, d_qkv0, packed = fence(
        d_qkv1, gain_grad1, gate, up_far, up_near, gate_far, gate_near, d_qkv0, packed
    )
    (states_send,) = states_back(line, d_qkv0, d_qkv1, full_qkv, local, (3,))
    gate_send = add_low(pick(gate, z ^ 2, 1), gate_far)
    states_send, gate_send, gate, packed, d_qkv0, d_qkv1 = fence(states_send, gate_send, gate, packed, d_qkv0, d_qkv1)
    states_relay = swap_z(states_send, 1)
    gate_far = swap_z(gate_send, 2)
    pair = swap_z(jnp.stack([pick(packed, z ^ 2), pick(packed, z ^ 3)]), 2)
    packed = jnp.stack([pick(packed, z), pick(packed, z ^ 1)]) + pair
    states_far, states_near, states_own = states_back(line, d_qkv0, d_qkv1, full_qkv, local, (2, 1, 0))
    grad_gain = jnp.concatenate([gain_grad0, gain_grad1], 1).reshape(-1)
    gain_all = lax.dynamic_update_slice(jnp.zeros((4 * heads_width,), f32), grad_gain, (z * heads_width,))
    spare = COLS[0] + 3 * (GROUPS[0][1] - GROUPS[0][0]) * HD
    qkv_keep, qkv_send = rows_back(
        jnp.stack([y, x, c, z]).astype(jnp.int32), pieces, d_qkv0, d_qkv1, gain_all.reshape(width, 1), spare
    )
    states_relay, qkv_send, qkv_keep, states_far, states_near, states_own, packed, gate_far, d_branch = fence(
        states_relay, qkv_send, qkv_keep, states_far, states_near, states_own, packed, gate_far, d_branch
    )
    states_far = swap_z(add_low(states_far, states_relay), 2)
    states_near = swap_z(states_near, 1)
    qkv_sum = add_low(qkv_keep, swap_dp(qkv_send, CORE))
    g_out = left_tdot(mixed_low, d_branch).astype(low).reshape(2, 2, 2, 2, 2 * share, width)
    out_c = swap_dp(pick(g_out, 1 - c, 2), CORE)
    g_out = add_low(pick(g_out, c, 2), out_c)
    out_sum = [lax.dynamic_slice(g_out, (y ^ (at // 2), x ^ (at % 2), 0, 0, 0), (1, 1) + g_out.shape[2:]) for at in range(4)]
    out_sum = [v.reshape(2 * 2 * share, width) for v in out_sum]
    cell = lambda at, unit: jnp.concatenate(
        [v[2 * share * unit : 2 * share * (unit + 1)] for v in (qkv_sum[at], out_sum[at])], 1
    )
    rows = [Cells((cell(3, u), cell(1 + u, u), cell(2 - u, u), cell(0, u)), u == 0) for u in range(2)]
    row_far = [p.first(jnp.stack([p.side, p.corner])) for p in rows]
    packed = packed[0] + swap_z(packed[1], 1)
    own_rows = total3(pick(up, z, 1), up_near, up_far), total3(pick(gate, z, 1), gate_near, gate_far)
    own_rows = jnp.stack(own_rows, 1)
    own_part, other_part = pick(own_rows, c), swap_dp(pick(own_rows, 1 - c), CORE)
    down_grad = total3(pick(down, z), down_near, down_far).reshape(hidden_share, width)
    row_relay = [p.second(v[1]) for p, v in zip(rows, row_far)]
    up_grad, gate_grad = interleave(c, own_part, other_part)
    rows_sum = jnp.stack([p.total(v[0], r) for p, v, r in zip(rows, row_far, row_relay)]).reshape(4, share, three + width)
    columns = exchange(rows_sum)
    packed = packed.reshape(512)
    output_grad = jnp.sum(columns[..., three:].astype(f32), 0)
    columns_cut = [
        columns[..., at : at + 3 * (b - a) * HD].reshape(4, share, 3, -1) for (a, b), at in zip(GROUPS, COLS)
    ]
    score_gain_grad = jnp.sum(columns[..., spare].astype(f32), 0)
    columns = jnp.concatenate(columns_cut, -1).transpose(2, 1, 0, 3).reshape(3, share, width).astype(f32)
    columns, output_grad, score_gain_grad, input_grad, states_far, states_near, up_grad, gate_grad, down_grad = fence(
        columns, output_grad, score_gain_grad, input_grad, states_far, states_near, up_grad, gate_grad, down_grad
    )
    input_grad = input_grad + total3(states_own, states_near, states_far)
    return (
        final[None],
        packed[cuts[5] - cuts[1]] / count,
        input_grad[None],
        columns[0],
        columns[1],
        columns[2],
        output_grad,
        score_gain_grad,
        packed[: cuts[1]],
        up_grad,
        gate_grad,
        down_grad,
        packed[cuts[2] - cuts[1] : cuts[3] - cuts[1]],
        packed[cuts[3] - cuts[1] : cuts[4] - cuts[1]],
        packed[cuts[4] - cuts[1] : cuts[5] - cuts[1]],
    )


def per_device(
    inputs,
    teacher,
    lengths,
    query_weight,
    key_weight,
    value_projection,
    output_weight,
    score_gain,
    attention_step,
    up_weight,
    gate_weight,
    down_weight,
    up_scale,
    gate_scale,
    swiglu_step,
):
    seqs, local, width = inputs.shape
    full_len = local * lax.axis_size("ctx")
    rows = seqs * local
    heads = width // HD
    key_block = min(512, full_len)
    query_pos = lax.axis_index("ctx") * local + jnp.arange(local, dtype=jnp.int32)
    valid = (query_pos[None, :] < lengths[:, None]).astype(jnp.float32).reshape(rows, 1)
    count_local = jnp.sum(valid)
    full_query, full_key, full_value, full_output, full_gain, full_astep = (
        lax.all_gather(query_weight, ("dp", "ctx"), axis=0, tiled=True),
        lax.all_gather(key_weight, ("dp", "ctx"), axis=0, tiled=True),
        lax.all_gather(value_projection, ("dp", "ctx"), axis=0, tiled=True),
        lax.all_gather(output_weight, ("dp", "ctx"), axis=0, tiled=True),
        lax.all_gather(score_gain, ("dp", "ctx"), axis=0, tiled=True),
        lax.all_gather(attention_step, ("dp", "ctx"), axis=0, tiled=True),
    )
    states = inputs.reshape(rows, width)
    resid = states.astype(jnp.float32)
    queries = matmul(states, full_query)
    keys_raw = matmul(states, full_key)
    values_raw = matmul(states, full_value)
    gains = full_gain.astype(jnp.float32).reshape(heads, HD)
    query_norm = normalize(queries.reshape(rows, heads, HD))
    key_norm = normalize(keys_raw.reshape(rows, heads, HD))
    q_heads = (gains * query_norm).astype(jnp.bfloat16).reshape(seqs, local, heads, HD)
    k_flat = (gains * key_norm).astype(jnp.bfloat16).reshape(seqs, local, width)
    v_flat = values_raw.astype(jnp.bfloat16).reshape(seqs, local, width)

    def key_step(carry, key_piece, value_piece, key_pos):
        top, total, accum = carry
        count_keys = key_piece.shape[1]
        scores, allowed = block_scores(
            q_heads, key_piece.reshape(seqs, count_keys, heads, HD), query_pos, key_pos, lengths
        )
        scores = jnp.where(allowed, scores, -1e30)
        top_new = jnp.maximum(top, jnp.max(scores, axis=-1))
        weights = jnp.where(allowed, jnp.exp(scores - top_new[..., None]), 0.0)
        factor = jnp.exp(top - top_new)
        total = total * factor + jnp.sum(weights, axis=-1)
        accum = accum * jnp.transpose(factor, (0, 2, 1))[..., None] + jnp.einsum(
            "shqk,skhd->sqhd",
            weights.astype(jnp.bfloat16),
            value_piece.reshape(seqs, count_keys, heads, HD),
            preferred_element_type=jnp.float32,
        )
        return (top_new, total, accum)

    init = (
        jnp.full((seqs, heads, local), -1e30, jnp.float32),
        jnp.zeros((seqs, heads, local), jnp.float32),
        jnp.zeros((seqs, local, heads, HD), jnp.float32),
    )
    carry = init
    key_piece = lax.all_gather(k_flat, "ctx", axis=1, tiled=True)
    value_piece = lax.all_gather(v_flat, "ctx", axis=1, tiled=True)
    count_keys = key_piece.shape[1]

    def inner(state, index):
        offset = index * key_block
        key_part = lax.dynamic_slice_in_dim(key_piece, offset, key_block, 1)
        value_part = lax.dynamic_slice_in_dim(value_piece, offset, key_block, 1)
        positions = offset + jnp.arange(key_block, dtype=jnp.int32)
        return (key_step(state, key_part, value_part, positions), None)

    carry, unused = lax.scan(inner, carry, jnp.arange(count_keys // key_block, dtype=jnp.int32))
    top, total, accum = carry
    mixed = accum / jnp.transpose(total, (0, 2, 1))[..., None]
    log_total = top + jnp.log(total)
    mixed_low = mixed.reshape(rows, width).astype(jnp.bfloat16)
    branch = matmul(mixed_low, full_output)
    branch_norm = normalize(branch)
    astep = full_astep.astype(jnp.float32)
    first = resid + astep * (branch_norm - resid)
    middle = normalize(first)
    middle_low = middle.astype(jnp.bfloat16)
    full_up, full_gate, full_down, full_uscale, complete_gate_scale, full_mstep = (
        lax.all_gather(up_weight, ("dp", "ctx"), axis=0, tiled=True),
        lax.all_gather(gate_weight, ("dp", "ctx"), axis=0, tiled=True),
        lax.all_gather(down_weight, ("dp", "ctx"), axis=0, tiled=True),
        lax.all_gather(up_scale, ("dp", "ctx"), axis=0, tiled=True),
        lax.all_gather(gate_scale, ("dp", "ctx"), axis=0, tiled=True),
        lax.all_gather(swiglu_step, ("dp", "ctx"), axis=0, tiled=True),
    )
    upper = matmul(middle_low, full_up)
    gating = matmul(middle_low, full_gate)
    scale_up = full_uscale.astype(jnp.float32)
    scale_gate = complete_gate_scale.astype(jnp.float32)
    upper_scaled = upper * scale_up
    gate_arg = gating * scale_gate
    gate_act = jax.nn.silu(gate_arg)
    hidden = (upper_scaled * gate_act).astype(jnp.bfloat16)
    lower = matmul(hidden, full_down)
    lower_norm = normalize(lower)
    mstep = full_mstep.astype(jnp.float32)
    second = middle + mstep * (lower_norm - middle)
    final = normalize(second)
    target = teacher.reshape(rows, width).astype(jnp.float32)
    diff = final - target
    err_local = jnp.sum(valid * diff * diff)
    err_total, count = lax.psum((err_local, count_local), ("dp", "ctx"))
    cot = loss_scale * 2.0 / count * valid * diff
    full_up, full_gate, full_down, full_uscale, complete_gate_scale, full_mstep = (
        lax.all_gather(up_weight, ("dp", "ctx"), axis=0, tiled=True),
        lax.all_gather(gate_weight, ("dp", "ctx"), axis=0, tiled=True),
        lax.all_gather(down_weight, ("dp", "ctx"), axis=0, tiled=True),
        lax.all_gather(up_scale, ("dp", "ctx"), axis=0, tiled=True),
        lax.all_gather(gate_scale, ("dp", "ctx"), axis=0, tiled=True),
        lax.all_gather(swiglu_step, ("dp", "ctx"), axis=0, tiled=True),
    )
    d_second = norm_back(second, final, cot)
    d_middle = d_second * (1.0 - mstep)
    grad_mstep = jnp.sum(d_second * (lower_norm - middle), axis=0)
    d_lower = norm_back(lower, lower_norm, d_second * mstep).astype(jnp.bfloat16)
    grad_down = left_tdot(hidden, d_lower)
    d_hidden = right_tdot(d_lower, full_down)
    d_upper = d_hidden * gate_act
    sigmoid_gate = jax.nn.sigmoid(gate_arg)
    d_gate_arg = d_hidden * upper_scaled * (sigmoid_gate * (1.0 + gate_arg * (1.0 - sigmoid_gate)))
    grad_uscale = jnp.sum(d_upper * upper, axis=0)
    grad_gscale = jnp.sum(d_gate_arg * gating, axis=0)
    d_up_low = (d_upper * scale_up).astype(jnp.bfloat16)
    d_gate_low = (d_gate_arg * scale_gate).astype(jnp.bfloat16)
    d_middle = d_middle + right_tdot(d_up_low, full_up) + right_tdot(d_gate_low, full_gate)
    grad_up = left_tdot(middle_low, d_up_low)
    grad_gate = left_tdot(middle_low, d_gate_low)
    up_grad, gate_grad, down_grad, up_scale_grad, gate_scale_gradient, swiglu_step_grad = (
        lax.psum_scatter(grad_up, ("dp", "ctx"), scatter_dimension=0, tiled=True),
        lax.psum_scatter(grad_gate, ("dp", "ctx"), scatter_dimension=0, tiled=True),
        lax.psum_scatter(grad_down, ("dp", "ctx"), scatter_dimension=0, tiled=True),
        lax.psum_scatter(grad_uscale, ("dp", "ctx"), scatter_dimension=0, tiled=True),
        lax.psum_scatter(grad_gscale, ("dp", "ctx"), scatter_dimension=0, tiled=True),
        lax.psum_scatter(grad_mstep, ("dp", "ctx"), scatter_dimension=0, tiled=True),
    )
    d_first = norm_back(first, middle, d_middle)
    input_grad = d_first * (1.0 - astep)
    grad_astep = jnp.sum(d_first * (branch_norm - resid), axis=0)
    d_branch = norm_back(branch, branch_norm, d_first * astep).astype(jnp.bfloat16)
    full_query, full_key, full_value, full_output, full_gain, full_astep = (
        lax.all_gather(query_weight, ("dp", "ctx"), axis=0, tiled=True),
        lax.all_gather(key_weight, ("dp", "ctx"), axis=0, tiled=True),
        lax.all_gather(value_projection, ("dp", "ctx"), axis=0, tiled=True),
        lax.all_gather(output_weight, ("dp", "ctx"), axis=0, tiled=True),
        lax.all_gather(score_gain, ("dp", "ctx"), axis=0, tiled=True),
        lax.all_gather(attention_step, ("dp", "ctx"), axis=0, tiled=True),
    )
    gains = full_gain.astype(jnp.float32).reshape(heads, HD)
    grad_output = left_tdot(mixed_low, d_branch)
    d_mixed = right_tdot(d_branch, full_output).astype(jnp.bfloat16)
    d_mixed_heads = d_mixed.reshape(seqs, local, heads, HD)
    delta = jnp.transpose(jnp.sum(d_mixed_heads.astype(jnp.float32) * mixed, axis=-1), (0, 2, 1))
    whole_keys, whole_values = (
        lax.all_gather(k_flat, "ctx", axis=1, tiled=True),
        lax.all_gather(v_flat, "ctx", axis=1, tiled=True),
    )

    def query_terms(index):
        offset = index * key_block
        key_part = lax.dynamic_slice_in_dim(whole_keys, offset, key_block, 1).reshape(
            seqs, key_block, heads, HD
        )
        value_part = lax.dynamic_slice_in_dim(whole_values, offset, key_block, 1).reshape(
            seqs, key_block, heads, HD
        )
        key_pos = offset + jnp.arange(key_block, dtype=jnp.int32)
        scores, allowed = block_scores(q_heads, key_part, query_pos, key_pos, lengths)
        probs = jnp.where(allowed, jnp.exp(scores - log_total[..., None]), 0.0)
        d_probs = jnp.einsum(
            "sqhd,skhd->shqk", d_mixed_heads, value_part, preferred_element_type=jnp.float32
        )
        d_scores = (probs * (d_probs - delta[..., None])).astype(jnp.bfloat16)
        d_query_part = jnp.einsum(
            "shqk,skhd->sqhd", d_scores, key_part, preferred_element_type=jnp.float32
        )
        return (offset, probs, d_scores, d_query_part)

    def key_back(carry, index):
        d_query_acc, d_key_all, d_value_all = carry
        offset, probs, d_scores, d_query_part = query_terms(index)
        d_query_acc = d_query_acc + d_query_part
        d_key_part = jnp.einsum(
            "shqk,sqhd->skhd", d_scores, q_heads, preferred_element_type=jnp.float32
        ) * HD ** (-0.5)
        d_value_part = jnp.einsum(
            "shqk,sqhd->skhd",
            probs.astype(jnp.bfloat16),
            d_mixed_heads,
            preferred_element_type=jnp.float32,
        )
        d_key_all = lax.dynamic_update_slice_in_dim(
            d_key_all, d_key_part.reshape(seqs, key_block, width), offset, 1
        )
        d_value_all = lax.dynamic_update_slice_in_dim(
            d_value_all, d_value_part.reshape(seqs, key_block, width), offset, 1
        )
        return ((d_query_acc, d_key_all, d_value_all), None)

    start_carry = (
        jnp.zeros((seqs, local, heads, HD), jnp.float32),
        jnp.zeros((seqs, full_len, width), jnp.float32),
        jnp.zeros((seqs, full_len, width), jnp.float32),
    )
    (d_query_heads, d_key_all, d_value_all), unused = lax.scan(
        key_back, start_carry, jnp.arange(full_len // key_block, dtype=jnp.int32)
    )
    d_key_local, d_value_local = (
        lax.psum_scatter(
            d_key_all.astype(jnp.bfloat16), "ctx", scatter_dimension=1, tiled=True
        ).astype(jnp.float32),
        lax.psum_scatter(
            d_value_all.astype(jnp.bfloat16), "ctx", scatter_dimension=1, tiled=True
        ).astype(jnp.float32),
    )
    d_key_heads = d_key_local.reshape(rows, heads, HD)
    d_value_local = d_value_local.reshape(rows, width)
    d_query_heads = (d_query_heads * HD ** (-0.5)).reshape(rows, heads, HD)
    grad_gain = jnp.sum(d_query_heads * query_norm, axis=0) + jnp.sum(
        d_key_heads * key_norm, axis=0
    )
    d_query_low = (
        norm_back(queries.reshape(rows, heads, HD), query_norm, d_query_heads * gains)
        .reshape(rows, width)
        .astype(jnp.bfloat16)
    )
    d_key_low = (
        norm_back(keys_raw.reshape(rows, heads, HD), key_norm, d_key_heads * gains)
        .reshape(rows, width)
        .astype(jnp.bfloat16)
    )
    d_value_low = d_value_local.astype(jnp.bfloat16)
    input_grad = (
        input_grad
        + right_tdot(d_query_low, full_query)
        + right_tdot(d_key_low, full_key)
        + right_tdot(d_value_low, full_value)
    )
    grad_query = left_tdot(states, d_query_low)
    grad_key = left_tdot(states, d_key_low)
    grad_value = left_tdot(states, d_value_low)
    query_grad, key_grad, value_grad, output_grad, score_gain_grad, attention_step_grad = (
        lax.psum_scatter(grad_query, ("dp", "ctx"), scatter_dimension=0, tiled=True),
        lax.psum_scatter(grad_key, ("dp", "ctx"), scatter_dimension=0, tiled=True),
        lax.psum_scatter(grad_value, ("dp", "ctx"), scatter_dimension=0, tiled=True),
        lax.psum_scatter(grad_output, ("dp", "ctx"), scatter_dimension=0, tiled=True),
        lax.psum_scatter(grad_gain.reshape(width), ("dp", "ctx"), scatter_dimension=0, tiled=True),
        lax.psum_scatter(grad_astep, ("dp", "ctx"), scatter_dimension=0, tiled=True),
    )
    distill_loss_mean = err_total / count
    layer_out = final.astype(jnp.bfloat16).reshape(seqs, local, width)
    return (
        layer_out,
        distill_loss_mean,
        input_grad.reshape(seqs, local, width),
        query_grad,
        key_grad,
        value_grad,
        output_grad,
        score_gain_grad,
        attention_step_grad,
        up_grad,
        gate_grad,
        down_grad,
        up_scale_grad,
        gate_scale_gradient,
        swiglu_step_grad,
    )


def solution(mesh):
    placed = (
        P("dp", "ctx", None),
        P("dp", "ctx", None),
        P("dp"),
        P(("dp", "ctx"), None),
        P(("dp", "ctx"), None),
        P(("dp", "ctx"), None),
        P(("dp", "ctx"), None),
        P(("dp", "ctx")),
        P(("dp", "ctx")),
        P(("dp", "ctx"), None),
        P(("dp", "ctx"), None),
        P(("dp", "ctx"), None),
        P(("dp", "ctx")),
        P(("dp", "ctx")),
        P(("dp", "ctx")),
    )
    on_one = on_cores if dict(mesh.shape) == {"dp": 8, "ctx": 4} else per_device
    return jax.shard_map(
        on_one,
        mesh=mesh,
        in_specs=placed,
        out_specs=(
            P("dp", "ctx", None),
            P(),
            P("dp", "ctx", None),
            P(("dp", "ctx"), None),
            P(("dp", "ctx"), None),
            P(("dp", "ctx"), None),
            P(("dp", "ctx"), None),
            P(("dp", "ctx")),
            P(("dp", "ctx")),
            P(("dp", "ctx"), None),
            P(("dp", "ctx"), None),
            P(("dp", "ctx"), None),
            P(("dp", "ctx")),
            P(("dp", "ctx")),
            P(("dp", "ctx")),
        ),
        check_vma=False,
    )
```
